32 devices in a mesh: dp: 8 (over z, x), row: 2 (over y), col: 2 (over core).
Axes of the slice: x: 2, y: 2, z: 4, core: 2. Of those that a mesh axis runs over, the one named last changes fastest.
Arguments:
- images: bfloat16 [10960, 1024], P(('dp', 'row'), 'col'), may hold values from -19 to 19
- cotangent: bfloat16 [10960, 1024], P(('dp', 'row'), 'col'), may hold values from -6 to 6
- triplet_master: float32 [2, 1024, 3, 1024], P(None, ('col', 'dp'), None, 'row'), may hold values from -0.1875 to 0.1875
- triplet_first: float32 [2, 1024, 3, 1024], P(None, ('col', 'dp'), None, 'row'), may hold values from -28 to 28
- triplet_second: float32 [2, 1024, 3, 1024], P(None, ('col', 'dp'), None, 'row'), may hold values from 1.7536 to 7.0144
- project_master: float32 [2, 1024, 1024], P(None, ('row', 'dp'), 'col'), may hold values from -0.375 to 0.375
- project_first: float32 [2, 1024, 1024], P(None, ('row', 'dp'), 'col'), may hold values from -28 to 28
- project_second: float32 [2, 1024, 1024], P(None, ('row', 'dp'), 'col'), may hold values from 1.7536 to 7.0144
- expand_master: float32 [2, 1024, 4096], P(None, ('col', 'dp'), 'row'), may hold values from -0.1875 to 0.1875
- expand_first: float32 [2, 1024, 4096], P(None, ('col', 'dp'), 'row'), may hold values from -28 to 28
- expand_second: float32 [2, 1024, 4096], P(None, ('col', 'dp'), 'row'), may hold values from 1.7536 to 7.0144
- shrink_master: float32 [2, 4096, 1024], P(None, ('row', 'dp'), 'col'), may hold values from -0.09375 to 0.09375
- shrink_first: float32 [2, 4096, 1024], P(None, ('row', 'dp'), 'col'), may hold values from -28 to 28
- shrink_second: float32 [2, 4096, 1024], P(None, ('row', 'dp'), 'col'), may hold values from 1.7536 to 7.0144
- vectors_master: float32 [2, 14336], P(None, ('dp', 'row', 'col')), may hold values from -0.6 to 1.5
- vectors_first: float32 [2, 14336], P(None, ('dp', 'row', 'col')), may hold values from -32 to 32
- vectors_second: float32 [2, 14336], P(None, ('dp', 'row', 'col')), may hold values from 2.74 to 10.96
Outputs:
- block_out: bfloat16 [10960, 1024], P(('dp', 'row'), 'col')
- input_grad: float32 [10960, 1024], P(('dp', 'row'), 'col')
- new_triplet_first: float32 [2, 1024, 3, 1024], P(None, ('col', 'dp'), None, 'row')
- new_triplet_second: float32 [2, 1024, 3, 1024], P(None, ('col', 'dp'), None, 'row')
- new_triplet_master: float32 [2, 1024, 3, 1024], P(None, ('col', 'dp'), None, 'row')
- new_project_first: float32 [2, 1024, 1024], P(None, ('row', 'dp'), 'col')
- new_project_second: float32 [2, 1024, 1024], P(None, ('row', 'dp'), 'col')
- new_project_master: float32 [2, 1024, 1024], P(None, ('row', 'dp'), 'col')
- new_expand_first: float32 [2, 1024, 4096], P(None, ('col', 'dp'), 'row')
- new_expand_second: float32 [2, 1024, 4096], P(None, ('col', 'dp'), 'row')
- new_expand_master: float32 [2, 1024, 4096], P(None, ('col', 'dp'), 'row')
- new_shrink_first: float32 [2, 4096, 1024], P(None, ('row', 'dp'), 'col')
- new_shrink_second: float32 [2, 4096, 1024], P(None, ('row', 'dp'), 'col')
- new_shrink_master: float32 [2, 4096, 1024], P(None, ('row', 'dp'), 'col')
- new_vectors_first: float32 [2, 14336], P(None, ('dp', 'row', 'col'))
- new_vectors_second: float32 [2, 14336], P(None, ('dp', 'row', 'col'))
- new_vectors_master: float32 [2, 14336], P(None, ('dp', 'row', 'col'))
The draws below stay inside these ranges and needn't reach their ends.
All inputs are finite; a program needn't handle non-finite values.
Results may differ from the reference program's by a relative error of at most 0.012.
Values may be sent and summed in bfloat16 or wider, within the bound.
A program may use at most 256 MiB of HBM per device.

```python
import math
import jax
import jax.numpy as jnp
from jax import lax

D = 1024
HEADS = 16
HEAD_DIM = 64
FF = 4096
LAYERS = 2
STEP = 10
SEQ = 1370
TOKENS = 10960


def draw_images(key, part):
    key = jax.random.fold_in(key, 11)
    place = jnp.arange(D, dtype=jnp.float32) / (D - 1)
    return (jax.random.truncated_normal(key, -4.0, 4.0, (TOKENS, D), jnp.float32) * (1.0 + 3.0 * place)).astype(jnp.bfloat16)


def draw_vectors_master(key, part):
    key = jax.random.fold_in(key, 23)
    width = 10 * D + FF
    place = jnp.arange(width)
    first, second = jax.random.split(key)
    signed = jnp.clip(0.5 * jax.random.normal(first, (LAYERS, width), jnp.float32), -1.0, 1.0)
    level = jax.random.uniform(second, (LAYERS, width), jnp.float32, 0.0, 1.0)
    gains = 0.6 + 0.8 * level
    scales = 0.5 * jnp.exp(jnp.log(3.0) * level)
    is_gain = (place < D) | (place >= 6 * D) & (place < 7 * D)
    is_scale = (place >= 5 * D) & (place < 6 * D) | (place >= 9 * D + FF)
    return jnp.where(is_gain, gains, jnp.where(is_scale, scales, 0.6 * signed))


def block_levels(key, shape, pieces, least, largest):
    def one(axis_at, parts):
        draws = jax.random.uniform(jax.random.fold_in(jax.random.fold_in(key, 6), axis_at), (parts,), jnp.float32, least / len(pieces), largest / len(pieces))
        return jnp.repeat(jnp.exp(draws), shape[axis_at] // parts).reshape((-1,) + (1,) * (len(shape) - axis_at - 1))

    level = one(*pieces[0])
    for cut in pieces[1:]:
        level = level * one(*cut)
    return level


def normal_values(own_key, dims, deviation, bound, cuts=(), kind=jnp.bfloat16):
    drawn = deviation * jax.random.normal(own_key, dims, jnp.float32)
    if cuts:
        drawn = drawn * block_levels(own_key, dims, cuts, -0.22, 0.18)
    return jnp.clip(drawn, -bound, bound).astype(kind)


def setup_inputs(seed: int = 0) -> dict:
    streams_of = jax.random.split(jax.random.key(seed), 18)
    return {
        "images": draw_images(jax.random.fold_in(streams_of[17], 71), 0),
        "cotangent": normal_values(streams_of[1], (TOKENS, D), 1.0, 6.0, ((0, 16), (1, 2))),
        "triplet_master": normal_values(streams_of[2], (LAYERS, D, 3, D), D ** -0.5, 0.1875, ((1, 16), (3, 2)), jnp.float32),
        "triplet_first": normal_values(streams_of[3], (LAYERS, D, 3, D), (0.044 * TOKENS ** 0.5), 28.0, ((1, 16), (3, 2)), jnp.float32),
        "triplet_second": jnp.clip(jnp.exp(math.log(7.0144) - 1.3862944 * jax.random.uniform(streams_of[4], (LAYERS, D, 3, D), jnp.float32) ** block_levels(streams_of[4], (LAYERS, D, 3, D), ((1, 16), (3, 2)), -0.2, 0.2)), 1.7536, 7.0144),
        "project_master": normal_values(streams_of[5], (LAYERS, D, D), (D // 4) ** -0.5, 0.375, ((1, 16), (2, 2)), jnp.float32),
        "project_first": normal_values(streams_of[6], (LAYERS, D, D), (0.044 * TOKENS ** 0.5), 28.0, ((1, 16), (2, 2)), jnp.float32),
        "project_second": jnp.clip(jnp.exp(math.log(7.0144) - 1.3862944 * jax.random.uniform(streams_of[7], (LAYERS, D, D), jnp.float32) ** block_levels(streams_of[7], (LAYERS, D, D), ((1, 16), (2, 2)), -0.2, 0.2)), 1.7536, 7.0144),
        "expand_master": normal_values(streams_of[8], (LAYERS, D, FF), D ** -0.5, 0.1875, ((1, 16), (2, 2)), jnp.float32),
        "expand_first": normal_values(streams_of[9], (LAYERS, D, FF), (0.044 * TOKENS ** 0.5), 28.0, ((1, 16), (2, 2)), jnp.float32),
        "expand_second": jnp.clip(jnp.exp(math.log(7.0144) - 1.3862944 * jax.random.uniform(streams_of[10], (LAYERS, D, FF), jnp.float32) ** block_levels(streams_of[10], (LAYERS, D, FF), ((1, 16), (2, 2)), -0.2, 0.2)), 1.7536, 7.0144),
        "shrink_master": normal_values(streams_of[11], (LAYERS, FF, D), FF ** -0.5, 0.09375, ((1, 16), (2, 2)), jnp.float32),
        "shrink_first": normal_values(streams_of[12], (LAYERS, FF, D), (0.044 * TOKENS ** 0.5), 28.0, ((1, 16), (2, 2)), jnp.float32),
        "shrink_second": jnp.clip(jnp.exp(math.log(7.0144) - 1.3862944 * jax.random.uniform(streams_of[13], (LAYERS, FF, D), jnp.float32) ** block_levels(streams_of[13], (LAYERS, FF, D), ((1, 16), (2, 2)), -0.2, 0.2)), 1.7536, 7.0144),
        "vectors_master": draw_vectors_master(jax.random.fold_in(streams_of[17], 71), 0),
        "vectors_first": normal_values(streams_of[15], (LAYERS, 10 * D + FF), (0.055 * TOKENS ** 0.5), 32.0, ((1, 32),), jnp.float32),
        "vectors_second": jnp.clip(jnp.exp(math.log(10.96) - 1.3862944 * jax.random.uniform(streams_of[16], (LAYERS, 10 * D + FF), jnp.float32) ** block_levels(streams_of[16], (LAYERS, 10 * D + FF), ((1, 32),), -0.2, 0.2)), 2.74, 10.96),
    }


@jax.custom_vjp
def low(v):
    return lax.optimization_barrier(v.astype(jnp.bfloat16)).astype(jnp.float32)

@jax.custom_vjp
def low_back(v):
    return v

def low_keep(v):
    return (low(v), None)

def low_pass(kept, grad):
    return (grad,)

def back_keep(v):
    return (v, None)

def back_low(kept, grad):
    return (low(grad),)
low.defvjp(low_keep, low_pass)
low_back.defvjp(back_keep, back_low)
highest = lax.Precision.HIGHEST
norm_epsilon = 1e-06
beta_first = 0.9
beta_second = 0.999
adam_epsilon = 1e-08
learn_rate = 0.02
vector_rate = 0.1
decay_rate = 0.05

def product(left, right):
    return jnp.dot(left, right, precision=highest)

def split_vector(vector):
    marks = [0, D, 2 * D, 3 * D, 4 * D, 5 * D, 6 * D, 7 * D, 8 * D, 8 * D + FF, 9 * D + FF, 10 * D + FF]
    return [vector[marks[place]:marks[place + 1]] for place in range(11)]

def normalize(values, gain, shift):
    centre = lax.optimization_barrier(jnp.mean(values, axis=1, keepdims=True))
    spread = lax.optimization_barrier(jnp.mean(values * values, axis=1, keepdims=True)) - centre * centre
    return (values - centre) * lax.rsqrt(spread + norm_epsilon) * gain + shift

def head_attend(block):
    scores = low_back(product(block[0], block[1].T) * HEAD_DIM ** (-0.5))
    probs = jax.nn.softmax(scores, axis=1)
    return product(low(probs), block[2])

def layer(state, triplet_w, project_w, expand_w, shrink_w, vector):
    norm_gain, norm_shift, query_bias, value_bias, mixer_bias, branch_scale, second_gain, second_shift, hidden_bias, output_bias, output_scale = split_vector(vector)
    normed = low(normalize(state, norm_gain, norm_shift))
    biases = jnp.stack([query_bias, jnp.zeros_like(query_bias), value_bias])
    triple = low_back(low(jnp.einsum('sd,dke->ske', normed, low(triplet_w), precision=highest) + biases))
    heads = triple.reshape(SEQ, 3, HEADS, HEAD_DIM).transpose(2, 1, 0, 3)
    results = lax.map(jax.checkpoint(head_attend), heads)
    mixed = low_back(low(results.transpose(1, 0, 2).reshape(SEQ, D)))
    branch = low_back(product(mixed, low(project_w)) + mixer_bias)
    middle = state + branch_scale * branch
    normed_two = low(normalize(middle, second_gain, second_shift))
    inner = low_back(product(normed_two, low(expand_w)) + hidden_bias)
    active = low(jax.nn.gelu(inner, approximate=False))
    output = low_back(product(active, low(shrink_w)) + output_bias)
    return middle + output_scale * output

def forward(state, masters):
    triplet_w, project_w, expand_w, shrink_w, vectors = masters
    for index in range(LAYERS):
        state = layer(state, triplet_w[index], project_w[index], expand_w[index], shrink_w[index], vectors[index])
    return state

def adam_step(master, first, second, grad, rate, decay):
    first_new = beta_first * first + (1.0 - beta_first) * grad
    second_new = beta_second * second + (1.0 - beta_second) * grad * grad
    ratio = first_new / (1.0 - beta_first ** STEP) / (jnp.sqrt(second_new / (1.0 - beta_second ** STEP)) + adam_epsilon)
    return (first_new, second_new, master - rate * (ratio + decay * master))

def reference(images, cotangent, triplet_master, triplet_first, triplet_second, project_master, project_first, project_second, expand_master, expand_first, expand_second, shrink_master, shrink_first, shrink_second, vectors_master, vectors_first, vectors_second):
    masters = (triplet_master, project_master, expand_master, shrink_master, vectors_master)
    count = TOKENS // SEQ
    inputs = images.astype(jnp.float32).reshape(count, SEQ, D)
    backs = cotangent.astype(jnp.float32).reshape(count, SEQ, D)

    def one_image(totals, pair):
        result, pullback = jax.vjp(forward, pair[0], masters)
        grad_input, grad_masters = pullback(pair[1])
        return (jax.tree.map(jnp.add, totals, grad_masters), (result, grad_input))
    totals, outcome = lax.scan(one_image, jax.tree.map(jnp.zeros_like, masters), (inputs, backs))
    results, grad_inputs = outcome
    triplet_out = adam_step(triplet_master, triplet_first, triplet_second, totals[0], learn_rate, decay_rate)
    project_out = adam_step(project_master, project_first, project_second, totals[1], learn_rate, decay_rate)
    expand_out = adam_step(expand_master, expand_first, expand_second, totals[2], learn_rate, decay_rate)
    shrink_out = adam_step(shrink_master, shrink_first, shrink_second, totals[3], learn_rate, decay_rate)
    vector_out = adam_step(vectors_master, vectors_first, vectors_second, totals[4], vector_rate, 0.0)
    return (results.reshape(TOKENS, D).astype(jnp.bfloat16), grad_inputs.reshape(TOKENS, D), triplet_out[0], triplet_out[1], triplet_out[2], project_out[0], project_out[1], project_out[2], expand_out[0], expand_out[1], expand_out[2], shrink_out[0], shrink_out[1], shrink_out[2], vector_out[0], vector_out[1], vector_out[2])
```

```python
import jax
import jax.numpy as jnp
from jax import lax
from jax.sharding import PartitionSpec as P

D = 1024
HEAD_DIM = 64
FF = 4096
LAYERS = 2
STEP = 10
TILE = 16

norm_epsilon = 1e-06
beta_first = 0.9
beta_second = 0.999
adam_epsilon = 1e-08
learn_rate = 0.02
vector_rate = 0.1
decay_rate = 0.05
bf16 = jnp.bfloat16
f32 = jnp.float32


def contract(left, right, left_dims, right_dims):
    return lax.dot_general(
        left, right, ((left_dims, right_dims), ((), ())), preferred_element_type=f32
    )


def swap(values, axis):
    return lax.ppermute(values, axis, [(0, 1), (1, 0)])


def pair_swap(values):
    count = lax.axis_size("dp")
    return lax.ppermute(values, "dp", [(at, at ^ 1) for at in range(count)])


def shifted(values, step):
    count = lax.axis_size("dp")
    return lax.ppermute(values, "dp", [(at, (at + step) % count) for at in range(count)])


def ordered(mine, other, place, axis):
    return jnp.where(
        place == 0,
        jnp.concatenate([mine, other], axis),
        jnp.concatenate([other, mine], axis),
    )


def dp_gather(block):
    count = lax.axis_size("dp")
    at = lax.axis_index("dp")
    place = at % 2
    line = jnp.stack([block] + [shifted(block, step) for step in range(2, count, 2)])
    both = ordered(line[:, None], pair_swap(line)[:, None], place, 1)
    pairs = count // 2
    back = (at // 2 - jnp.arange(pairs)) % pairs
    return jnp.take(both, back, axis=0).reshape((count,) + block.shape)


def dp_scatter(blocks):
    count = lax.axis_size("dp")
    at = lax.axis_index("dp")
    place = at % 2
    split = blocks.reshape((count // 2, 2) + blocks.shape[1:])
    mine = lax.dynamic_index_in_dim(split, place, 1, False)
    other = lax.dynamic_index_in_dim(split, 1 - place, 1, False)
    summed = (mine.astype(f32) + pair_swap(other).astype(f32)).astype(blocks.dtype)
    total = lax.dynamic_index_in_dim(summed, at // 2, 0, False).astype(f32)
    for step in range(1, count // 2):
        part = lax.dynamic_index_in_dim(summed, (at // 2 + step) % (count // 2), 0, False)
        total = total + shifted(part, 2 * step).astype(f32)
    return total


def gelu_value(values):
    return jax.nn.gelu(values, approximate=False)


def norm_forward(values, gain, shift):
    centre = jnp.sum(values, 1, keepdims=True) / D
    spread = jnp.sum(values * values, 1, keepdims=True) / D - centre * centre
    inverse = lax.rsqrt(spread + norm_epsilon)
    unit = (values - centre) * inverse
    return ((unit * gain + shift).astype(bf16), unit, inverse)


def norm_backward(grad, unit, inverse, gain):
    scaled = grad * gain
    first = jnp.sum(scaled, 1, keepdims=True)
    second = jnp.sum(scaled * unit, 1, keepdims=True)
    return inverse * (scaled - first / D - unit * (second / D))


def attend_forward(stacked, bias):
    factor = HEAD_DIM ** (-0.5)

    def one_head(block):
        scores = contract(block[0], block[1], (1,), (1,)) * factor + bias
        peak = jnp.max(scores, 1, keepdims=True)
        weights = jnp.exp(scores - peak)
        total = jnp.sum(weights, 1, keepdims=True)
        probs = (weights / total).astype(bf16)
        return (
            jnp.dot(probs, block[2], preferred_element_type=f32),
            (peak + jnp.log(total))[:, 0],
        )

    return lax.map(one_head, stacked)


def attend_backward(stacked, logsum, grads, bias):
    factor = HEAD_DIM ** (-0.5)

    def one_head(pack):
        block, norm_log, back = pack
        scores = contract(block[0], block[1], (1,), (1,)) * factor + bias
        probs = jnp.exp(scores - norm_log[:, None])
        back_probs = contract(back, block[2], (1,), (1,))
        inner = jnp.sum(probs * back_probs, 1, keepdims=True)
        back_scores = (probs * (back_probs - inner)).astype(bf16)
        grad_query = jnp.dot(back_scores, block[1], preferred_element_type=f32) * factor
        grad_key = contract(back_scores, block[0], (0,), (0,)) * factor
        grad_value = contract(probs.astype(bf16), back, (0,), (0,))
        return jnp.stack([grad_query, grad_key, grad_value])

    return lax.map(one_head, (stacked, logsum, grads))


def adam_step(master, first, second, grad, rate, decay):
    first_new = beta_first * first + (1.0 - beta_first) * grad
    second_new = beta_second * second + (1.0 - beta_second) * grad * grad
    ratio = (
        first_new
        / (1.0 - beta_first**STEP)
        / (jnp.sqrt(second_new / (1.0 - beta_second**STEP)) + adam_epsilon)
    )
    return (first_new, second_new, master - rate * (ratio + decay * master))


MARKS = [0, D, 2 * D, 3 * D, 4 * D, 5 * D, 6 * D, 7 * D, 8 * D, 8 * D + FF, 9 * D + FF, 10 * D + FF]


def local(
    images,
    cotangent,
    triplet_master,
    triplet_first,
    triplet_second,
    project_master,
    project_first,
    project_second,
    expand_master,
    expand_first,
    expand_second,
    shrink_master,
    shrink_first,
    shrink_second,
    vectors_master,
    vectors_first,
    vectors_second,
):
    count = lax.axis_size("dp")
    row_at = lax.axis_index("row")
    col_at = lax.axis_index("col")
    tokens, features = images.shape
    rows = -(-tokens // (2 * TILE)) * TILE
    group = 2 * rows
    half = D // 2
    heads = half // 2 // HEAD_DIM
    width = heads * HEAD_DIM

    def to_tokens(values):
        padded = jnp.pad(values, ((0, 2 * rows - tokens), (0, 0))).reshape(2, rows, features)
        mine = lax.dynamic_index_in_dim(padded, col_at, 0, False)
        other = swap(lax.dynamic_index_in_dim(padded, 1 - col_at, 0, False), "col")
        return ordered(mine, other, col_at, 1)

    def to_features(values):
        split = values.reshape(rows, 2, features).transpose(1, 0, 2)
        mine = lax.dynamic_index_in_dim(split, col_at, 0, False)
        other = swap(lax.dynamic_index_in_dim(split, 1 - col_at, 0, False), "col")
        return ordered(mine, other, col_at, 0)[:tokens]

    def row_rows(values):
        return jnp.concatenate([values, swap(values, "row")], 0)

    def row_sum(partial):
        return partial[:rows] + swap(partial[rows:].astype(bf16), "row").astype(f32)

    shard_shapes = [
        values.shape[1:] for values in (triplet_master, project_master, expand_master, shrink_master)
    ]
    lane = half

    def flat(parts):
        return jnp.concatenate([part.reshape(-1, lane) for part in parts], 0)

    def unflat(values, lead=()):
        parts = []
        at = 0
        for shape in shard_shapes:
            size = 1
            for side in shape:
                size *= side
            size //= lane
            parts.append(values[..., at : at + size, :].reshape(lead + shape))
            at += size
        return parts

    weights = []
    for layer in range(LAYERS):
        block = flat(
            [
                values[layer].astype(bf16)
                for values in (triplet_master, project_master, expand_master, shrink_master)
            ]
        )
        column = dp_gather(block)
        both = ordered(column[None], swap(column, "col")[None], col_at, 0)
        qkv, mix, up, down = unflat(both, (2, count))
        weights.append(
            (
                qkv.reshape(D, 3, half),
                mix.transpose(1, 2, 0, 3).reshape(half, D),
                up.reshape(D, FF // 2),
                down.transpose(1, 2, 0, 3).reshape(FF // 2, D),
            )
        )

    spot = vectors_master
    spot = ordered(spot[:, None], swap(spot, "col")[:, None], col_at, 1)
    spot = ordered(spot[:, None], swap(spot, "row")[:, None], row_at, 1)
    vectors = dp_gather(spot).transpose(1, 0, 2, 3, 4).reshape(LAYERS, -1)

    place = jnp.arange(2 * group) % rows
    late = jnp.arange(2 * group) // group
    valid = place + late * rows < tokens
    bias = jnp.where(valid, 0.0, -1e30).astype(f32)[None]

    def to_heads(values, parts):
        split = values.reshape(group, parts, 2, width).transpose(2, 0, 1, 3)
        mine = lax.dynamic_index_in_dim(split, col_at, 0, False)
        other = swap(lax.dynamic_index_in_dim(split, 1 - col_at, 0, False), "col")
        return (
            ordered(mine, other, col_at, 0)
            .reshape(2 * group, parts, heads, HEAD_DIM)
            .transpose(2, 1, 0, 3)
        )

    def from_heads(values):
        parts = values.shape[1]
        split = values.transpose(2, 1, 0, 3).reshape(2, group, parts, width)
        mine = lax.dynamic_index_in_dim(split, col_at, 0, False)
        other = swap(lax.dynamic_index_in_dim(split, 1 - col_at, 0, False), "col")
        return ordered(mine[:, :, None], other[:, :, None], col_at, 2).reshape(group, parts, half)

    head_start = row_at * half + col_at * width

    def pieces(vector):
        return [vector[MARKS[at] : MARKS[at + 1]] for at in range(11)]

    state = to_tokens(images).astype(f32)
    kept = []
    layer_pieces = []
    for layer in range(LAYERS):
        parts = pieces(vectors[layer])
        layer_pieces.append(parts)
        triplet_w, project_w, expand_w, shrink_w = weights[layer]
        normed, unit_one, inverse_one = norm_forward(state, parts[0], parts[1])
        normed_all = row_rows(normed)
        half_start = row_at * half
        biases = jnp.stack(
            [
                lax.dynamic_slice_in_dim(parts[2], half_start, half),
                jnp.zeros((half,), f32),
                lax.dynamic_slice_in_dim(parts[3], half_start, half),
            ]
        )
        triple = (contract(normed_all, triplet_w, (1,), (0,)) + biases).astype(bf16)
        stacked = to_heads(triple, 3)
        results, logsum = attend_forward(stacked, bias)
        mixed = from_heads(results.astype(bf16)[:, None])[:, 0]
        branch = row_sum(contract(mixed, project_w, (1,), (0,))) + parts[4]
        middle = state + parts[5] * branch
        normed_two, unit_two, inverse_two = norm_forward(middle, parts[6], parts[7])
        normed_two_all = row_rows(normed_two)
        hidden_bias = lax.dynamic_slice_in_dim(parts[8], row_at * (FF // 2), FF // 2)
        inner = contract(normed_two_all, expand_w, (1,), (0,)) + hidden_bias
        active = gelu_value(inner).astype(bf16)
        output = row_sum(contract(active, shrink_w, (1,), (0,))) + parts[9]
        kept.append(
            (
                unit_one,
                inverse_one,
                normed_all,
                stacked,
                logsum,
                mixed,
                branch,
                unit_two,
                inverse_two,
                normed_two_all,
                inner,
                active,
                output,
            )
        )
        state = middle + parts[10] * output
    block_out = to_features(state.astype(bf16))
    grad = to_tokens(cotangent).astype(f32)
    reduced = [None] * LAYERS
    vector_grads = [None] * LAYERS
    for layer in reversed(range(LAYERS)):
        (
            unit_one,
            inverse_one,
            normed_all,
            stacked,
            logsum,
            mixed,
            branch,
            unit_two,
            inverse_two,
            normed_two_all,
            inner,
            active,
            output,
        ) = kept[layer]
        parts = layer_pieces[layer]
        triplet_w, project_w, expand_w, shrink_w = weights[layer]
        output_scale_grad = jnp.sum(grad * output, 0)
        back_out = (parts[10] * grad).astype(bf16)
        output_bias_grad = jnp.sum(back_out.astype(f32), 0)
        back_out_all = row_rows(back_out)
        shrink_grad = contract(active, back_out_all, (0,), (0,)).astype(bf16)
        back_active = contract(back_out_all, shrink_w, (1,), (1,))
        back_inner = jax.vjp(gelu_value, inner)[1](back_active)[0].astype(bf16)
        hidden_bias_grad = jnp.sum(back_inner.astype(f32), 0)
        expand_grad = contract(normed_two_all, back_inner, (0,), (0,)).astype(bf16)
        back_two = row_sum(contract(back_inner, expand_w, (1,), (1,)))
        second_gain_grad = jnp.sum(back_two * unit_two, 0)
        second_shift_grad = jnp.sum(back_two, 0)
        grad_middle = grad + norm_backward(back_two, unit_two, inverse_two, parts[6])
        branch_scale_grad = jnp.sum(grad_middle * branch, 0)
        back_branch = (parts[5] * grad_middle).astype(bf16)
        mixer_bias_grad = jnp.sum(back_branch.astype(f32), 0)
        back_branch_all = row_rows(back_branch)
        project_grad = contract(mixed, back_branch_all, (0,), (0,)).astype(bf16)
        back_mixed = contract(back_branch_all, project_w, (1,), (1,)).astype(bf16)
        back_heads = to_heads(back_mixed[:, None], 1)[:, 0]
        back_stacked = attend_backward(stacked, logsum, back_heads, bias).astype(bf16)
        triple_sums = jnp.sum(back_stacked.astype(f32), 2)
        back_triple = from_heads(back_stacked)
        triplet_grad = contract(normed_all, back_triple, (0,), (0,)).astype(bf16)
        back_one = row_sum(contract(back_triple, triplet_w, (1, 2), (1, 2)))
        norm_gain_grad = jnp.sum(back_one * unit_one, 0)
        norm_shift_grad = jnp.sum(back_one, 0)
        grad = grad_middle + norm_backward(back_one, unit_one, inverse_one, parts[0])

        def spread(values, size, start):
            return lax.dynamic_update_slice_in_dim(jnp.zeros((size,), f32), values, start, 0)

        vector_grads[layer] = jnp.concatenate(
            [
                norm_gain_grad,
                norm_shift_grad,
                spread(triple_sums[:, 0].reshape(width), D, head_start),
                spread(triple_sums[:, 2].reshape(width), D, head_start),
                mixer_bias_grad,
                branch_scale_grad,
                second_gain_grad,
                second_shift_grad,
                spread(hidden_bias_grad, FF, row_at * (FF // 2)),
                output_bias_grad,
                output_scale_grad,
            ]
        )
        wide = [
            triplet_grad.reshape(2, count, -1, lane),
            project_grad.reshape(count, -1, 2, lane).transpose(2, 0, 1, 3),
            expand_grad.reshape(2, count, -1, lane),
            shrink_grad.reshape(count, -1, 2, lane).transpose(2, 0, 1, 3),
        ]
        blocks = jnp.concatenate(wide, 2)
        mine = lax.dynamic_index_in_dim(blocks, col_at, 0, False)
        other = swap(lax.dynamic_index_in_dim(blocks, 1 - col_at, 0, False), "col")
        reduced[layer] = unflat(
            dp_scatter((mine.astype(f32) + other.astype(f32)).astype(bf16))
        )
    grad_out = to_features(grad)

    spots = jnp.stack(vector_grads).reshape(LAYERS, count, 2, 2, -1)
    for axis, at, dim in (("col", col_at, 3), ("row", row_at, 2)):
        mine = lax.dynamic_index_in_dim(spots, at, dim, False)
        spots = mine + swap(lax.dynamic_index_in_dim(spots, 1 - at, dim, False), axis)
    vector_reduced = dp_scatter(spots.transpose(1, 0, 2))

    outs = []
    states = (
        (triplet_master, triplet_first, triplet_second),
        (project_master, project_first, project_second),
        (expand_master, expand_first, expand_second),
        (shrink_master, shrink_first, shrink_second),
    )
    for kind, (master, first, second) in enumerate(states):
        total = jnp.stack([reduced[layer][kind] for layer in range(LAYERS)])
        outs += adam_step(master, first, second, total, learn_rate, decay_rate)
    outs += adam_step(
        vectors_master, vectors_first, vectors_second, vector_reduced, vector_rate, 0.0
    )
    return (block_out, grad_out, *outs)


def solution(mesh):
    tokens = P(("dp", "row"), "col")
    triplet = P(None, ("col", "dp"), None, "row")
    narrow = P(None, ("row", "dp"), "col")
    wide = P(None, ("col", "dp"), "row")
    vector = P(None, ("dp", "row", "col"))
    states = (triplet,) * 3 + (narrow,) * 3 + (wide,) * 3 + (narrow,) * 3 + (vector,) * 3
    return jax.shard_map(
        local,
        mesh=mesh,
        in_specs=(tokens, tokens) + states,
        out_specs=(tokens, tokens) + states,
        check_vma=False,
    )
```

```python
import functools

import jax
import jax.numpy as jnp
from jax import lax
from jax.experimental import pallas as pl
from jax.experimental.pallas import tpu as pltpu
from jax.sharding import PartitionSpec as P

D = 1024
HEAD_DIM = 64
FF = 4096
LAYERS = 2
STEP = 10
TILE = 16

norm_epsilon = 1e-06
beta_first = 0.9
beta_second = 0.999
adam_epsilon = 1e-08
learn_rate = 0.02
vector_rate = 0.1
decay_rate = 0.05
bf16 = jnp.bfloat16
f32 = jnp.float32


def contract(left, right, left_dims, right_dims):
    return lax.dot_general(
        left, right, ((left_dims, right_dims), ((), ())), preferred_element_type=f32
    )


def swap(values, axis):
    return lax.ppermute(values, axis, [(0, 1), (1, 0)])


def pair_swap(values):
    count = lax.axis_size("dp")
    return lax.ppermute(values, "dp", [(at, at ^ 1) for at in range(count)])


def shifted(values, step):
    count = lax.axis_size("dp")
    return lax.ppermute(values, "dp", [(at, (at + step) % count) for at in range(count)])


def ordered(mine, other, place, axis):
    return jnp.where(
        place == 0,
        jnp.concatenate([mine, other], axis),
        jnp.concatenate([other, mine], axis),
    )


def dp_gather(block):
    count = lax.axis_size("dp")
    at = lax.axis_index("dp")
    place = at % 2
    line = jnp.stack([block] + [shifted(block, step) for step in range(2, count, 2)])
    both = ordered(line[:, None], pair_swap(line)[:, None], place, 1)
    pairs = count // 2
    back = (at // 2 - jnp.arange(pairs)) % pairs
    return jnp.take(both, back, axis=0).reshape((count,) + block.shape)


def dp_scatter(blocks):
    count = lax.axis_size("dp")
    at = lax.axis_index("dp")
    place = at % 2
    split = blocks.reshape((count // 2, 2) + blocks.shape[1:])
    mine = lax.dynamic_index_in_dim(split, place, 1, False)
    other = lax.dynamic_index_in_dim(split, 1 - place, 1, False)
    summed = (mine.astype(f32) + pair_swap(other).astype(f32)).astype(blocks.dtype)
    total = lax.dynamic_index_in_dim(summed, at // 2, 0, False).astype(f32)
    for step in range(1, count // 2):
        part = lax.dynamic_index_in_dim(summed, (at // 2 + step) % (count // 2), 0, False)
        total = total + shifted(part, 2 * step).astype(f32)
    return total


def gelu_value(values):
    return jax.nn.gelu(values, approximate=False)


def norm_forward(values, gain, shift):
    centre = jnp.sum(values, 1, keepdims=True) / D
    spread = jnp.sum(values * values, 1, keepdims=True) / D - centre * centre
    inverse = lax.rsqrt(spread + norm_epsilon)
    unit = (values - centre) * inverse
    return ((unit * gain + shift).astype(bf16), unit, inverse)


def norm_backward(grad, unit, inverse, gain):
    scaled = grad * gain
    first = jnp.sum(scaled, 1, keepdims=True)
    second = jnp.sum(scaled * unit, 1, keepdims=True)
    return inverse * (scaled - first / D - unit * (second / D))


def attend_forward(stacked, bias):
    factor = HEAD_DIM ** (-0.5)

    def one_head(block):
        scores = contract(block[0], block[1], (1,), (1,)) * factor + bias
        peak = jnp.max(scores, 1, keepdims=True)
        weights = jnp.exp(scores - peak)
        total = jnp.sum(weights, 1, keepdims=True)
        probs = (weights / total).astype(bf16)
        return (
            jnp.dot(probs, block[2], preferred_element_type=f32),
            (peak + jnp.log(total))[:, 0],
        )

    return lax.map(one_head, stacked)


def attend_backward(stacked, logsum, grads, bias):
    factor = HEAD_DIM ** (-0.5)

    def one_head(pack):
        block, norm_log, back = pack
        scores = contract(block[0], block[1], (1,), (1,)) * factor + bias
        probs = jnp.exp(scores - norm_log[:, None])
        back_probs = contract(back, block[2], (1,), (1,))
        inner = jnp.sum(probs * back_probs, 1, keepdims=True)
        back_scores = (probs * (back_probs - inner)).astype(bf16)
        grad_query = jnp.dot(back_scores, block[1], preferred_element_type=f32) * factor
        grad_key = contract(back_scores, block[0], (0,), (0,)) * factor
        grad_value = contract(probs.astype(bf16), back, (0,), (0,))
        return jnp.stack([grad_query, grad_key, grad_value])

    return lax.map(one_head, (stacked, logsum, grads))


def adam_step(master, first, second, grad, rate, decay):
    first_new = beta_first * first + (1.0 - beta_first) * grad
    second_new = beta_second * second + (1.0 - beta_second) * grad * grad
    ratio = (
        first_new
        / (1.0 - beta_first**STEP)
        / (jnp.sqrt(second_new / (1.0 - beta_second**STEP)) + adam_epsilon)
    )
    return (first_new, second_new, master - rate * (ratio + decay * master))


MARKS = [0, D, 2 * D, 3 * D, 4 * D, 5 * D, 6 * D, 7 * D, 8 * D, 8 * D + FF, 9 * D + FF, 10 * D + FF]


MESH = pl.DeviceIdType.MESH
KINDS = 4
GROUPS = LAYERS * KINDS
SPLIT = 2
ANY = pl.BlockSpec(memory_space=pl.ANY)
WHOLE = pl.BlockSpec(memory_space=pltpu.VMEM)


def nt(left, right):
    return contract(left, right, (1,), (1,))


def nn(left, right):
    return contract(left, right, (1,), (0,))


def tn(left, right):
    return contract(left, right, (0,), (0,))


class Place:
    def __init__(self, count):
        self.count = count
        self.line = count // 2
        self.dp = lax.axis_index("dp")
        self.row = lax.axis_index("row")
        self.col = lax.axis_index("col")
        self.pair = lax.rem(self.dp, 2)
        self.outer = lax.div(self.dp, 2)
        self.x_dp = self.dp + 1 - 2 * self.pair
        self.x_peer = (self.x_dp, self.row, self.col)
        self.y_peer = (self.dp, 1 - self.row, self.col)
        self.c_peer = (self.dp, self.row, 1 - self.col)

    def ahead(self, step):
        return lax.rem(self.dp + 2 * step, self.count)

    def behind(self, step):
        return lax.rem(self.dp + self.count - 2 * step, self.count)

    def z_peer(self, step):
        return (self.ahead(step), self.row, self.col)

    def greet(self):
        barrier = pltpu.get_barrier_semaphore()
        peers = [self.z_peer(step) for step in range(1, self.line)]
        peers += [self.x_peer, self.y_peer, self.c_peer]
        for peer in peers:
            pl.semaphore_signal(barrier, inc=1, device_id=peer, device_id_type=MESH)
        pl.semaphore_wait(barrier, len(peers))


def remote(source, target, send, recv, peer):
    return pltpu.make_async_remote_copy(
        source, target, send, recv, device_id=peer, device_id_type=MESH
    )


def aligned(value, by=128):
    return pl.multiple_of(value, by)


def weight_view(kind, ref, layer, place, dp, col):
    if kind in (0, 2):
        size = ref.shape[1] // (2 * place.count)
        return ref.at[layer, pl.ds(aligned((col * place.count + dp) * size, 16), size), :]
    size = ref.shape[1] // place.count
    return ref.at[
        layer,
        pl.ds(aligned(dp * size, 16), size),
        pl.ds(aligned(col * (D // 2)), D // 2),
    ]


def column_view(kind, ref, layer, col):
    if kind in (0, 2):
        return ref.at[layer, pl.ds(aligned(col * (D // 2), 16), D // 2), :]
    return ref.at[layer, :, pl.ds(aligned(col * (D // 2)), D // 2)]


class Gather:
    def __init__(self, place, shards, wholes, send, recv, own):
        self.place, self.shards, self.wholes = place, shards, wholes
        self.send, self.recv, self.own = send, recv, own

    def line_copy(self, group, step):
        layer, kind = divmod(group, KINDS)
        place = self.place
        return remote(
            self.shards[kind].at[layer],
            weight_view(kind, self.wholes[kind], layer, place, place.dp, place.col),
            self.send.at[group, step - 1],
            self.recv.at[group, step - 1],
            place.z_peer(step),
        )

    def pair_copy(self, group, step):
        layer, kind = divmod(group, KINDS)
        place = self.place
        view = weight_view(kind, self.wholes[kind], layer, place, place.behind(step), place.col)
        at = place.line - 1 + step
        return remote(
            self.shards[kind].at[layer] if step == 0 else view,
            view,
            self.send.at[group, at],
            self.recv.at[group, at],
            place.x_peer,
        )

    def core_copy(self, group):
        layer, kind = divmod(group, KINDS)
        place = self.place
        view = column_view(kind, self.wholes[kind], layer, place.col)
        at = 2 * place.line - 1
        return remote(
            view, view, self.send.at[group, at], self.recv.at[group, at], place.c_peer
        )

    def own_copy(self, group):
        layer, kind = divmod(group, KINDS)
        place = self.place
        return pltpu.make_async_copy(
            self.shards[kind].at[layer],
            weight_view(kind, self.wholes[kind], layer, place, place.dp, place.col),
            self.own.at[group],
        )

    def start(self, group):
        for step in range(1, self.place.line):
            self.line_copy(group, step).start()
        self.pair_copy(group, 0).start()
        self.own_copy(group).start()

    def to_pair(self, group):
        for step in range(1, self.place.line):
            self.line_copy(group, step).wait_recv()
            self.pair_copy(group, step).start()

    def to_core(self, group):
        self.own_copy(group).wait()
        for step in range(self.place.line):
            self.pair_copy(group, step).wait_recv()
        self.core_copy(group).start()

    def arrive(self, group):
        self.core_copy(group).wait_recv()

    def finish(self):
        for group in range(GROUPS):
            for step in range(1, self.place.line):
                self.line_copy(group, step).wait_send()
            for step in range(self.place.line):
                self.pair_copy(group, step).wait_send()
            self.core_copy(group).wait_send()


def gather_vectors(place, spot, spare, raw, vecs, send, recv):
    for at, peer in enumerate((place.c_peer, place.y_peer, place.x_peer)):
        copy = remote(spot, spare.at[at], send.at[at], recv.at[at], peer)
        copy.start()
        copy.wait()
        spot[...] = spot[...] + spare[at]
    copies = []
    for step in range(1, place.line):
        copy = remote(
            spot, raw.at[place.outer], send.at[2 + step], recv.at[2 + step], place.z_peer(step)
        )
        copy.start()
        copies.append(copy)
    raw[place.outer] = spot[...]
    for copy in copies:
        copy.wait()
    used = vecs.shape[1] // 128 // place.line
    for outer in range(place.line):
        for layer in range(LAYERS):
            for at in range(used):
                start = (outer * used + at) * 128
                vecs[layer : layer + 1, start : start + 128] = raw[outer, layer, at : at + 1, :]


def norm_rows(source, gain, shift, unit, inverse, target, rows):
    size = 32

    def step(at, carry):
        place = pl.ds(aligned(at * size, size), size)
        values = source[place, :].astype(f32)
        centre = jnp.sum(values, 1, keepdims=True) * (1.0 / D)
        spread = jnp.sum(values * values, 1, keepdims=True) * (1.0 / D) - centre * centre
        scale = lax.rsqrt(spread + norm_epsilon)
        norm = (values - centre) * scale
        unit[place, :] = norm
        inverse[place, :] = jnp.broadcast_to(scale, (size, 128))
        target[place, :] = (norm * gain + shift).astype(bf16)
        return carry

    lax.fori_loop(0, rows // size, step, 0)


def gelu_both(values):
    normal = 0.5 + 0.5 * lax.erf(values * (0.5**0.5))
    density = jnp.exp(-0.5 * values * values) * 0.3989422804014327
    return values * normal, normal + values * density


def forward_kernel(count, tokens, *refs):
    (
        state_in,
        spot_in,
        bias_in,
        shard_a,
        shard_b,
        shard_c,
        shard_d,
        w_a,
        w_b,
        w_c,
        w_d,
        vecs_out,
        unit_one_out,
        inv_one_out,
        normed_out,
        heads_out,
        lse_out,
        mixed_out,
        branch_out,
        unit_two_out,
        inv_two_out,
        normed_two_out,
        active_out,
        slope_out,
        output_out,
        block_out,
        state,
        spot,
        spare,
        raw,
        vecs,
        wq,
        wm,
        wu,
        wd,
        unit,
        inverse,
        unit_two,
        inverse_two,
        normed,
        normed_two,
        heads_all,
        head_tx,
        head_mix,
        lse,
        mixed_all,
        branch,
        output,
        active,
        slope,
        tx,
        rx,
        part,
        g_send,
        g_recv,
        g_own,
        v_send,
        v_recv,
        y_send,
        y_recv,
        c_send,
        c_recv,
        stage_sem,
        save_sem,
    ) = refs
    rows = state_in.shape[0]
    group = 2 * rows
    half = D // 2
    width = half // 2
    place = Place(count)
    row, col = place.row, place.col
    wholes = (w_a, w_b, w_c, w_d)
    gather = Gather(place, (shard_a, shard_b, shard_c, shard_d), wholes, g_send, g_recv, g_own)
    place.greet()
    gather.start(0)
    gather.start(1)

    pending = {}

    def save(name, at, source, target):
        settle(name)
        copy = pltpu.make_async_copy(source, target, save_sem.at[at])
        copy.start()
        pending[name] = copy

    def settle(*names):
        for name in names:
            if name in pending:
                pending.pop(name).wait()

    staged = {}

    def stage(kind, layer):
        gather.arrive(layer * KINDS + kind)
        buffer = (wq, wm, wu, wd)[kind]
        copy = pltpu.make_async_copy(wholes[kind].at[layer], buffer, stage_sem.at[kind])
        copy.start()
        staged[kind] = copy

    def ready(kind):
        staged.pop(kind).wait()

    y_at = [0]

    def y_copy(source, target):
        at = y_at[0]
        y_at[0] += 1
        return remote(source, target, y_send.at[at], y_recv.at[at], place.y_peer)

    chunk = rows // SPLIT

    def exchange_rows(buffer):
        copies = []
        for at in range(SPLIT):
            copies.append(
                y_copy(
                    buffer.at[pl.ds(at * chunk, chunk), :],
                    buffer.at[pl.ds(rows + at * chunk, chunk), :],
                )
            )
            copies[-1].start()
        return copies

    spot[...] = spot_in[...]
    state[...] = state_in[...].astype(f32)
    gather_vectors(place, spot, spare, raw, vecs, v_send, v_recv)
    save("vecs", 11, vecs, vecs_out)
    gather.to_pair(0)
    gather.start(2)

    plan = {
        (0, "norm"): ((gather.to_core, 0), (stage, 0, 0), (gather.to_pair, 1), (gather.start, 3)),
        (0, "triple"): ((gather.to_core, 1),),
        (0, "attend"): ((gather.to_pair, 2), (stage, 1, 0), (gather.start, 4)),
        (0, "project"): ((gather.to_core, 2),),
        (0, "branch"): ((gather.to_pair, 3), (gather.start, 5), (stage, 2, 0)),
        (0, "expand"): ((gather.to_core, 3), (gather.start, 6)),
        (0, "shrink"): ((gather.to_pair, 4),),
        (0, "output"): ((gather.to_core, 4), (stage, 0, 1), (gather.to_pair, 5), (gather.start, 7)),
        (1, "norm"): ((gather.to_core, 5),),
        (1, "triple"): ((stage, 1, 1), (gather.to_pair, 6)),
        (1, "attend"): ((gather.to_core, 6),),
        (1, "project"): ((gather.to_pair, 7),),
        (1, "branch"): ((stage, 2, 1),),
        (1, "expand"): ((gather.to_core, 7),),
    }

    lane = lax.broadcasted_iota(jnp.int32, (1, 128), 1) < HEAD_DIM
    valid = lax.broadcasted_iota(jnp.int32, (rows, 1), 0) < tokens - col * rows

    def vector(layer, at):
        return vecs[layer : layer + 1, at * D : (at + 1) * D]

    for layer in range(LAYERS):

        def pump(name, layer=layer):
            for action, *args in plan.get((layer, name), ()):
                action(*args)

        settle("unit", "inverse", "normed")
        norm_rows(state, vector(layer, 0), vector(layer, 1), unit, inverse, normed, rows)
        copies = exchange_rows(normed)
        save("unit", 0, unit, unit_one_out.at[layer])
        save("inverse", 1, inverse, inv_one_out.at[layer])
        pump("norm")
        ready(0)
        heads, mixed = heads_all.at[layer], mixed_all.at[layer]

        def triple(start):
            def step(at, carry):
                part_at = lax.rem(at, 3)
                mine = lax.div(at, 3)
                owner = jnp.where(mine == 1, col, 1 - col)
                column = aligned(part_at * half + owner * width)
                value = nn(normed[start : start + rows, :], wq[:, pl.ds(column, width)])
                bias_at = aligned(
                    jnp.where(part_at == 2, 3 * D, 2 * D) + row * half + owner * width
                )
                bias = vecs[layer : layer + 1, pl.ds(bias_at, width)]
                bias = bias * jnp.where(part_at == 1, 0.0, 1.0)
                value = jnp.where(valid, value + bias, 0.0).astype(bf16)
                lanes = pl.ds(aligned(part_at * width), width)

                @pl.when(mine == 0)
                def _():
                    head_tx[start : start + rows, lanes] = value

                @pl.when(mine == 1)
                def _():
                    heads[pl.ds(aligned(col * group + start, 16), rows), lanes] = value

                return carry

            lax.fori_loop(0, 6, step, 0)

        core_copies = []

        def send_heads(start):
            at = layer * 3 + (start > 0)
            core_copies.append(
                remote(
                    head_tx.at[pl.ds(start, rows), :],
                    heads.at[pl.ds(aligned(col * group + start, 16), rows), :],
                    c_send.at[at],
                    c_recv.at[at],
                    place.c_peer,
                )
            )
            core_copies[-1].start()

        triple(0)
        send_heads(0)
        for copy in copies:
            copy.wait()
        save("normed", 2, normed, normed_out.at[layer])
        triple(rows)
        send_heads(rows)
        pump("triple")
        for copy in core_copies:
            copy.wait()
        save("heads", 3, heads, heads_out.at[layer])
        settle("lse")

        def attend(owner):
            tile = rows // 2

            def step(at, carry):
                place_rows = pl.ds(aligned(owner * group + at * tile, 16), tile)
                for pair in range(width // 128):
                    lanes = slice(pair * 128, pair * 128 + 128)
                    query = heads[place_rows, lanes] * jnp.asarray(HEAD_DIM**-0.5, bf16)
                    zero = jnp.zeros_like(query)
                    both = jnp.concatenate(
                        [jnp.where(lane, query, zero), jnp.where(lane, zero, query)], 0
                    )
                    key = heads[:, width + pair * 128 : width + pair * 128 + 128]
                    value = heads[:, 2 * width + pair * 128 : 2 * width + pair * 128 + 128]
                    scores = nt(both, key) + bias_in[...]
                    peak = jnp.max(scores, 1, keepdims=True)
                    weights = jnp.exp(scores - peak)
                    total = jnp.sum(weights, 1, keepdims=True)
                    result = nn(weights.astype(bf16), value) / total
                    logsum = peak + jnp.log(total)
                    head_mix[place_rows, lanes] = jnp.where(
                        lane, result[:tile], result[tile:]
                    ).astype(bf16)
                    lse[place_rows, lanes] = jnp.where(lane, logsum[:tile], logsum[tile:])
                return carry

            lax.fori_loop(0, group // tile, step, 0)

        attend(1 - col)
        lanes = pl.ds(aligned(col * width), width)
        back = remote(
            head_mix.at[pl.ds(aligned((1 - col) * group, 16), group), :],
            mixed.at[:, lanes],
            c_send.at[layer * 3 + 2],
            c_recv.at[layer * 3 + 2],
            place.c_peer,
        )
        back.start()
        pump("attend")
        attend(col)
        mixed[:, lanes] = head_mix[pl.ds(aligned(col * group, 16), group), :]
        back.wait()
        save("lse", 4, lse, lse_out.at[layer])
        save("mixed", 5, mixed, mixed_out.at[layer])
        ready(1)
        pump("project")
        settle("normed_two")

        def project(start, size, target, target_at):
            def step(at, carry):
                lanes = pl.ds(aligned(at * half), half)
                value = nn(mixed[start : start + size, :], wm[:, lanes])
                target[pl.ds(target_at, size), lanes] = value.astype(target.dtype)
                return carry

            lax.fori_loop(0, 2, step, 0)

        copies = []
        for at in range(SPLIT):
            project(rows + at * chunk, chunk, tx, at * chunk)
            view = pl.ds(at * chunk, chunk)
            copies.append(y_copy(tx.at[view, :], rx.at[view, :]))
            copies[-1].start()
        project(0, rows, part, 0)
        pump("branch")
        for copy in copies:
            copy.wait()
        settle("branch", "unit_two", "inverse_two")
        branch[...] = part[...] + rx[...].astype(f32) + vector(layer, 4)
        state[...] = state[...] + vector(layer, 5) * branch[...]
        save("branch", 6, branch, branch_out.at[layer])
        norm_rows(
            state, vector(layer, 6), vector(layer, 7), unit_two, inverse_two, normed_two, rows
        )
        copies = exchange_rows(normed_two)
        save("unit_two", 7, unit_two, unit_two_out.at[layer])
        save("inverse_two", 8, inverse_two, inv_two_out.at[layer])
        pump("expand")
        ready(2)
        settle("active", "slope")

        def expand(start, size):
            def step(at, carry):
                lanes = pl.ds(aligned(at * half), half)
                bias_at = aligned(8 * D + row * (FF // 2) + at * half)
                value = nn(normed_two[start : start + size, :], wu[:, lanes])
                value = value + vecs[layer : layer + 1, pl.ds(bias_at, half)]
                act, grad = gelu_both(value)
                active[start : start + size, lanes] = act.astype(bf16)
                slope[start : start + size, lanes] = grad.astype(bf16)
                return carry

            lax.fori_loop(0, FF // 2 // half, step, 0)

        def shrink(start, size, target, target_at):
            def step(at, carry):
                lanes = pl.ds(aligned(at * half), half)
                value = nn(active[start : start + size, :], wd[:, lanes])
                target[pl.ds(target_at, size), lanes] = value.astype(target.dtype)
                return carry

            lax.fori_loop(0, 2, step, 0)

        expand(0, rows)
        stage(3, layer)
        settle("normed")
        ready(3)
        shrink(0, rows, part, 0)
        pump("shrink")
        back_copies = []
        for at in range(SPLIT):
            copies[at].wait()
            start = rows + at * chunk
            expand(start, chunk)
            shrink(start, chunk, tx, at * chunk)
            view = pl.ds(at * chunk, chunk)
            back_copies.append(y_copy(tx.at[view, :], rx.at[view, :]))
            back_copies[-1].start()
        save("normed_two", 9, normed_two, normed_two_out.at[layer])
        save("active", 10, active, active_out.at[layer])
        save("slope", 12, slope, slope_out.at[layer])
        pump("output")
        for copy in back_copies:
            copy.wait()
        settle("output")
        output[...] = part[...] + rx[...].astype(f32) + vector(layer, 12)
        state[...] = state[...] + vector(layer, 13) * output[...]
        save("output", 13, output, output_out.at[layer])
    block_out[...] = state[...].astype(bf16)
    gather.finish()
    settle(*list(pending))


def forward_call(mesh_count, tokens, state, spot, bias, shards):
    rows = state.shape[0]
    group = 2 * rows
    half = D // 2
    width = half // 2
    line = mesh_count // 2

    def shape(*dims, kind=f32):
        return jax.ShapeDtypeStruct(dims, kind)

    outs = [
        shape(LAYERS, D, 3 * half, kind=bf16),
        shape(LAYERS, half, D, kind=bf16),
        shape(LAYERS, D, FF // 2, kind=bf16),
        shape(LAYERS, FF // 2, D, kind=bf16),
        shape(LAYERS, 10 * D + FF),
        shape(LAYERS, rows, D),
        shape(LAYERS, rows, 128),
        shape(LAYERS, group, D, kind=bf16),
        shape(LAYERS, 2 * group, 3 * width, kind=bf16),
        shape(LAYERS, 2 * group, width),
        shape(LAYERS, group, half, kind=bf16),
        shape(LAYERS, rows, D),
        shape(LAYERS, rows, D),
        shape(LAYERS, rows, 128),
        shape(LAYERS, group, D, kind=bf16),
        shape(LAYERS, group, FF // 2, kind=bf16),
        shape(LAYERS, group, FF // 2, kind=bf16),
        shape(LAYERS, rows, D),
        shape(rows, D, kind=bf16),
    ]
    dma = pltpu.SemaphoreType.DMA
    scratch = [
        pltpu.VMEM((rows, D), f32),
        pltpu.VMEM(spot.shape, f32),
        pltpu.VMEM((3,) + spot.shape, f32),
        pltpu.VMEM((line,) + spot.shape, f32),
        pltpu.VMEM((LAYERS, 10 * D + FF), f32),
        pltpu.VMEM((D, 3 * half), bf16),
        pltpu.VMEM((half, D), bf16),
        pltpu.VMEM((D, FF // 2), bf16),
        pltpu.VMEM((FF // 2, D), bf16),
        pltpu.VMEM((rows, D), f32),
        pltpu.VMEM((rows, 128), f32),
        pltpu.VMEM((rows, D), f32),
        pltpu.VMEM((rows, 128), f32),
        pltpu.VMEM((group, D), bf16),
        pltpu.VMEM((group, D), bf16),
        pltpu.VMEM((LAYERS, 2 * group, 3 * width), bf16),
        pltpu.VMEM((group, 3 * width), bf16),
        pltpu.VMEM((2 * group, width), bf16),
        pltpu.VMEM((2 * group, width), f32),
        pltpu.VMEM((LAYERS, group, half), bf16),
        pltpu.VMEM((rows, D), f32),
        pltpu.VMEM((rows, D), f32),
        pltpu.VMEM((group, FF // 2), bf16),
        pltpu.VMEM((group, FF // 2), bf16),
        pltpu.VMEM((rows, D), bf16),
        pltpu.VMEM((rows, D), bf16),
        pltpu.VMEM((rows, D), f32),
        dma((GROUPS, 2 * line)),
        dma((GROUPS, 2 * line)),
        dma((GROUPS,)),
        dma((line + 2,)),
        dma((line + 2,)),
        dma((LAYERS * 4 * SPLIT,)),
        dma((LAYERS * 4 * SPLIT,)),
        dma((LAYERS * 3,)),
        dma((LAYERS * 3,)),
        dma((KINDS,)),
        dma((14,)),
    ]
    return pl.pallas_call(
        functools.partial(forward_kernel, mesh_count, tokens),
        out_shape=outs,
        in_specs=[WHOLE] * 3 + [ANY] * 4,
        out_specs=[ANY] * 18 + [WHOLE],
        scratch_shapes=scratch,
        compiler_params=pltpu.CompilerParams(
            collective_id=0, has_side_effects=True, vmem_limit_bytes=60 << 20
        ),
        name="forward",
    )(state, spot, bias, *shards)


def local(
    images,
    cotangent,
    triplet_master,
    triplet_first,
    triplet_second,
    project_master,
    project_first,
    project_second,
    expand_master,
    expand_first,
    expand_second,
    shrink_master,
    shrink_first,
    shrink_second,
    vectors_master,
    vectors_first,
    vectors_second,
):
    count = lax.axis_size("dp")
    row_at = lax.axis_index("row")
    col_at = lax.axis_index("col")
    tokens, features = images.shape
    rows = -(-tokens // (2 * TILE)) * TILE
    group = 2 * rows
    half = D // 2
    heads = half // 2 // HEAD_DIM
    width = heads * HEAD_DIM

    def to_tokens(values):
        padded = jnp.pad(values, ((0, 2 * rows - tokens), (0, 0))).reshape(2, rows, features)
        mine = lax.dynamic_index_in_dim(padded, col_at, 0, False)
        other = swap(lax.dynamic_index_in_dim(padded, 1 - col_at, 0, False), "col")
        return ordered(mine, other, col_at, 1)

    def to_features(values):
        split = values.reshape(rows, 2, features).transpose(1, 0, 2)
        mine = lax.dynamic_index_in_dim(split, col_at, 0, False)
        other = swap(lax.dynamic_index_in_dim(split, 1 - col_at, 0, False), "col")
        return ordered(mine, other, col_at, 0)[:tokens]

    def row_rows(values):
        return jnp.concatenate([values, swap(values, "row")], 0)

    def row_sum(partial):
        return partial[:rows] + swap(partial[rows:].astype(bf16), "row").astype(f32)

    shard_shapes = [
        values.shape[1:] for values in (triplet_master, project_master, expand_master, shrink_master)
    ]
    lane = half

    def flat(parts):
        return jnp.concatenate([part.reshape(-1, lane) for part in parts], 0)

    def unflat(values, lead=()):
        parts = []
        at = 0
        for shape in shard_shapes:
            size = 1
            for side in shape:
                size *= side
            size //= lane
            parts.append(values[..., at : at + size, :].reshape(lead + shape))
            at += size
        return parts


    shards = [
        triplet_master.astype(bf16).reshape(LAYERS, -1, 3 * half),
        project_master.astype(bf16),
        expand_master.astype(bf16),
        shrink_master.astype(bf16),
    ]
    piece = vectors_master.shape[1]
    line_at = (lax.axis_index("dp") % 2 * 2 + row_at) * 2 + col_at
    spot = lax.dynamic_update_slice_in_dim(
        jnp.zeros((LAYERS, 8 * piece), f32), vectors_master, line_at * piece, 1
    ).reshape(LAYERS, -1, 128)
    spot = jnp.pad(spot, ((0, 0), (0, -spot.shape[1] % 8), (0, 0)))
    place = jnp.arange(2 * group) % rows
    late = jnp.arange(2 * group) // group
    valid = place + late * rows < tokens
    bias = jnp.where(valid, 0.0, -1e30).astype(f32)[None]

    def to_heads(values, parts):
        split = values.reshape(group, parts, 2, width).transpose(2, 0, 1, 3)
        mine = lax.dynamic_index_in_dim(split, col_at, 0, False)
        other = swap(lax.dynamic_index_in_dim(split, 1 - col_at, 0, False), "col")
        return (
            ordered(mine, other, col_at, 0)
            .reshape(2 * group, parts, heads, HEAD_DIM)
            .transpose(2, 1, 0, 3)
        )

    def from_heads(values):
        parts = values.shape[1]
        split = values.transpose(2, 1, 0, 3).reshape(2, group, parts, width)
        mine = lax.dynamic_index_in_dim(split, col_at, 0, False)
        other = swap(lax.dynamic_index_in_dim(split, 1 - col_at, 0, False), "col")
        return ordered(mine[:, :, None], other[:, :, None], col_at, 2).reshape(group, parts, half)

    head_start = row_at * half + col_at * width

    def pieces(vector):
        return [vector[MARKS[at] : MARKS[at + 1]] for at in range(11)]

    kept_all = forward_call(count, tokens, to_tokens(images), spot, bias, shards)
    (w_a, w_b, w_c, w_d, vectors, *saved, block_rows) = kept_all
    layer_pieces = [pieces(vectors[layer]) for layer in range(LAYERS)]
    kept = []
    weights = []
    for layer in range(LAYERS):
        (unit_one, inverse_one, normed_all, heads_all, lse, mixed, branch, unit_two, inverse_two,
         normed_two_all, active, slope, output) = [value[layer] for value in saved]
        weights.append((w_a[layer].reshape(D, 3, half), w_b[layer], w_c[layer], w_d[layer]))
        stacked = heads_all.reshape(2 * group, 3, heads, HEAD_DIM).transpose(2, 1, 0, 3)
        logsum = lse.reshape(2 * group, heads, HEAD_DIM)[:, :, 0].T
        kept.append((unit_one, inverse_one[:, :1], normed_all, stacked, logsum, mixed, branch, unit_two,
            inverse_two[:, :1], normed_two_all, slope, active, output))
    block_out = to_features(block_rows)
    grad = to_tokens(cotangent).astype(f32)
    reduced = [None] * LAYERS
    vector_grads = [None] * LAYERS
    for layer in reversed(range(LAYERS)):
        (
            unit_one,
            inverse_one,
            normed_all,
            stacked,
            logsum,
            mixed,
            branch,
            unit_two,
            inverse_two,
            normed_two_all,
            slope,
            active,
            output,
        ) = kept[layer]
        parts = layer_pieces[layer]
        triplet_w, project_w, expand_w, shrink_w = weights[layer]
        output_scale_grad = jnp.sum(grad * output, 0)
        back_out = (parts[10] * grad).astype(bf16)
        output_bias_grad = jnp.sum(back_out.astype(f32), 0)
        back_out_all = row_rows(back_out)
        shrink_grad = contract(active, back_out_all, (0,), (0,)).astype(bf16)
        back_active = contract(back_out_all, shrink_w, (1,), (1,))
        back_inner = (slope.astype(f32) * back_active).astype(bf16)
        hidden_bias_grad = jnp.sum(back_inner.astype(f32), 0)
        expand_grad = contract(normed_two_all, back_inner, (0,), (0,)).astype(bf16)
        back_two = row_sum(contract(back_inner, expand_w, (1,), (1,)))
        second_gain_grad = jnp.sum(back_two * unit_two, 0)
        second_shift_grad = jnp.sum(back_two, 0)
        grad_middle = grad + norm_backward(back_two, unit_two, inverse_two, parts[6])
        branch_scale_grad = jnp.sum(grad_middle * branch, 0)
        back_branch = (parts[5] * grad_middle).astype(bf16)
        mixer_bias_grad = jnp.sum(back_branch.astype(f32), 0)
        back_branch_all = row_rows(back_branch)
        project_grad = contract(mixed, back_branch_all, (0,), (0,)).astype(bf16)
        back_mixed = contract(back_branch_all, project_w, (1,), (1,)).astype(bf16)
        back_heads = to_heads(back_mixed[:, None], 1)[:, 0]
        back_stacked = attend_backward(stacked, logsum, back_heads, bias).astype(bf16)
        triple_sums = jnp.sum(back_stacked.astype(f32), 2)
        back_triple = from_heads(back_stacked)
        triplet_grad = contract(normed_all, back_triple, (0,), (0,)).astype(bf16)
        back_one = row_sum(contract(back_triple, triplet_w, (1, 2), (1, 2)))
        norm_gain_grad = jnp.sum(back_one * unit_one, 0)
        norm_shift_grad = jnp.sum(back_one, 0)
        grad = grad_middle + norm_backward(back_one, unit_one, inverse_one, parts[0])

        def spread(values, size, start):
            return lax.dynamic_update_slice_in_dim(jnp.zeros((size,), f32), values, start, 0)

        vector_grads[layer] = jnp.concatenate(
            [
                norm_gain_grad,
                norm_shift_grad,
                spread(triple_sums[:, 0].reshape(width), D, head_start),
                spread(triple_sums[:, 2].reshape(width), D, head_start),
                mixer_bias_grad,
                branch_scale_grad,
                second_gain_grad,
                second_shift_grad,
                spread(hidden_bias_grad, FF, row_at * (FF // 2)),
                output_bias_grad,
                output_scale_grad,
            ]
        )
        wide = [
            triplet_grad.reshape(2, count, -1, lane),
            project_grad.reshape(count, -1, 2, lane).transpose(2, 0, 1, 3),
            expand_grad.reshape(2, count, -1, lane),
            shrink_grad.reshape(count, -1, 2, lane).transpose(2, 0, 1, 3),
        ]
        blocks = jnp.concatenate(wide, 2)
        mine = lax.dynamic_index_in_dim(blocks, col_at, 0, False)
        other = swap(lax.dynamic_index_in_dim(blocks, 1 - col_at, 0, False), "col")
        reduced[layer] = unflat(
            dp_scatter((mine.astype(f32) + other.astype(f32)).astype(bf16))
        )
    grad_out = to_features(grad)

    spots = jnp.stack(vector_grads).reshape(LAYERS, count, 2, 2, -1)
    for axis, at, dim in (("col", col_at, 3), ("row", row_at, 2)):
        mine = lax.dynamic_index_in_dim(spots, at, dim, False)
        spots = mine + swap(lax.dynamic_index_in_dim(spots, 1 - at, dim, False), axis)
    vector_reduced = dp_scatter(spots.transpose(1, 0, 2))

    outs = []
    states = (
        (triplet_master, triplet_first, triplet_second),
        (project_master, project_first, project_second),
        (expand_master, expand_first, expand_second),
        (shrink_master, shrink_first, shrink_second),
    )
    for kind, (master, first, second) in enumerate(states):
        total = jnp.stack([reduced[layer][kind] for layer in range(LAYERS)])
        outs += adam_step(master, first, second, total, learn_rate, decay_rate)
    outs += adam_step(
        vectors_master, vectors_first, vectors_second, vector_reduced, vector_rate, 0.0
    )
    return (block_out, grad_out, *outs)


def solution(mesh):
    tokens = P(("dp", "row"), "col")
    triplet = P(None, ("col", "dp"), None, "row")
    narrow = P(None, ("row", "dp"), "col")
    wide = P(None, ("col", "dp"), "row")
    vector = P(None, ("dp", "row", "col"))
    states = (triplet,) * 3 + (narrow,) * 3 + (wide,) * 3 + (narrow,) * 3 + (vector,) * 3
    return jax.shard_map(
        local,
        mesh=mesh,
        in_specs=(tokens, tokens) + states,
        out_specs=(tokens, tokens) + states,
        check_vma=False,
    )
```

```python
import functools

import jax
import jax.numpy as jnp
from jax import lax
from jax.experimental import pallas as pl
from jax.experimental.pallas import tpu as pltpu
from jax.sharding import PartitionSpec as P

D = 1024
HEAD_DIM = 64
FF = 4096
LAYERS = 2
STEP = 10
TILE = 16

norm_epsilon = 1e-06
beta_first = 0.9
beta_second = 0.999
adam_epsilon = 1e-08
learn_rate = 0.02
vector_rate = 0.1
decay_rate = 0.05
bf16 = jnp.bfloat16
f32 = jnp.float32


def contract(left, right, left_dims, right_dims):
    return lax.dot_general(
        left, right, ((left_dims, right_dims), ((), ())), preferred_element_type=f32
    )


def swap(values, axis):
    return lax.ppermute(values, axis, [(0, 1), (1, 0)])


def ordered(mine, other, place, axis):
    return jnp.where(
        place == 0,
        jnp.concatenate([mine, other], axis),
        jnp.concatenate([other, mine], axis),
    )


def adam_step(master, first, second, grad, rate, decay):
    first_new = beta_first * first + (1.0 - beta_first) * grad
    second_new = beta_second * second + (1.0 - beta_second) * grad * grad
    ratio = (
        first_new
        / (1.0 - beta_first**STEP)
        / (jnp.sqrt(second_new / (1.0 - beta_second**STEP)) + adam_epsilon)
    )
    return (first_new, second_new, master - rate * (ratio + decay * master))


MESH = pl.DeviceIdType.MESH
KINDS = 4
GROUPS = LAYERS * KINDS
SPLIT = 2
ANY = pl.BlockSpec(memory_space=pl.ANY)
WHOLE = pl.BlockSpec(memory_space=pltpu.VMEM)


def nt(left, right):
    return contract(left, right, (1,), (1,))


def nn(left, right):
    return contract(left, right, (1,), (0,))


def tn(left, right):
    return contract(left, right, (0,), (0,))


class Place:
    def __init__(self, count):
        self.count = count
        self.line = count // 2
        self.dp = lax.axis_index("dp")
        self.row = lax.axis_index("row")
        self.col = lax.axis_index("col")
        self.pair = lax.rem(self.dp, 2)
        self.outer = lax.div(self.dp, 2)
        self.x_dp = self.dp + 1 - 2 * self.pair
        self.x_peer = (self.x_dp, self.row, self.col)
        self.y_peer = (self.dp, 1 - self.row, self.col)
        self.c_peer = (self.dp, self.row, 1 - self.col)

    def ahead(self, step):
        return lax.rem(self.dp + 2 * step, self.count)

    def behind(self, step):
        return lax.rem(self.dp + self.count - 2 * step, self.count)

    def z_peer(self, step):
        return (self.ahead(step), self.row, self.col)

    def greet(self):
        barrier = pltpu.get_barrier_semaphore()
        peers = [self.z_peer(step) for step in range(1, self.line)]
        peers += [self.x_peer, self.y_peer, self.c_peer]
        for peer in peers:
            pl.semaphore_signal(barrier, inc=1, device_id=peer, device_id_type=MESH)
        pl.semaphore_wait(barrier, len(peers))


def remote(source, target, send, recv, peer):
    return pltpu.make_async_remote_copy(
        source, target, send, recv, device_id=peer, device_id_type=MESH
    )


def aligned(value, by=128):
    return pl.multiple_of(value, by)


def weight_view(kind, ref, layer, place, dp, col):
    if kind in (0, 2):
        size = ref.shape[1] // (2 * place.count)
        return ref.at[layer, pl.ds(aligned((col * place.count + dp) * size, 16), size), :]
    size = ref.shape[1] // place.count
    return ref.at[
        layer,
        pl.ds(aligned(dp * size, 16), size),
        pl.ds(aligned(col * (D // 2)), D // 2),
    ]


def column_view(kind, ref, layer, col):
    if kind in (0, 2):
        return ref.at[layer, pl.ds(aligned(col * (D // 2), 16), D // 2), :]
    return ref.at[layer, :, pl.ds(aligned(col * (D // 2)), D // 2)]


class Gather:
    def __init__(self, place, shards, wholes, send, recv, own):
        self.place, self.shards, self.wholes = place, shards, wholes
        self.send, self.recv, self.own = send, recv, own

    def line_copy(self, group, step):
        layer, kind = divmod(group, KINDS)
        place = self.place
        return remote(
            self.shards[kind].at[layer],
            weight_view(kind, self.wholes[kind], layer, place, place.dp, place.col),
            self.send.at[group, step - 1],
            self.recv.at[group, step - 1],
            place.z_peer(step),
        )

    def pair_copy(self, group, step):
        layer, kind = divmod(group, KINDS)
        place = self.place
        view = weight_view(kind, self.wholes[kind], layer, place, place.behind(step), place.col)
        at = place.line - 1 + step
        return remote(
            self.shards[kind].at[layer] if step == 0 else view,
            view,
            self.send.at[group, at],
            self.recv.at[group, at],
            place.x_peer,
        )

    def core_copy(self, group):
        layer, kind = divmod(group, KINDS)
        place = self.place
        view = column_view(kind, self.wholes[kind], layer, place.col)
        at = 2 * place.line - 1
        return remote(
            view, view, self.send.at[group, at], self.recv.at[group, at], place.c_peer
        )

    def own_copy(self, group):
        layer, kind = divmod(group, KINDS)
        place = self.place
        return pltpu.make_async_copy(
            self.shards[kind].at[layer],
            weight_view(kind, self.wholes[kind], layer, place, place.dp, place.col),
            self.own.at[group],
        )

    def start(self, group):
        for step in range(1, self.place.line):
            self.line_copy(group, step).start()
        self.pair_copy(group, 0).start()
        self.own_copy(group).start()

    def to_pair(self, group):
        for step in range(1, self.place.line):
            self.line_copy(group, step).wait_recv()
            self.pair_copy(group, step).start()

    def to_core(self, group):
        self.own_copy(group).wait()
        for step in range(self.place.line):
            self.pair_copy(group, step).wait_recv()
        self.core_copy(group).start()

    def arrive(self, group):
        self.core_copy(group).wait_recv()

    def finish(self):
        for group in range(GROUPS):
            for step in range(1, self.place.line):
                self.line_copy(group, step).wait_send()
            for step in range(self.place.line):
                self.pair_copy(group, step).wait_send()
            self.core_copy(group).wait_send()


def gather_vectors(place, spot, spare, raw, vecs, send, recv):
    for at, peer in enumerate((place.c_peer, place.y_peer, place.x_peer)):
        copy = remote(spot, spare.at[at], send.at[at], recv.at[at], peer)
        copy.start()
        copy.wait()
        spot[...] = spot[...] + spare[at]
    copies = []
    for step in range(1, place.line):
        copy = remote(
            spot, raw.at[place.outer], send.at[2 + step], recv.at[2 + step], place.z_peer(step)
        )
        copy.start()
        copies.append(copy)
    raw[place.outer] = spot[...]
    for copy in copies:
        copy.wait()
    used = vecs.shape[1] // 128 // place.line
    for outer in range(place.line):
        for layer in range(LAYERS):
            for at in range(used):
                start = (outer * used + at) * 128
                vecs[layer : layer + 1, start : start + 128] = raw[outer, layer, at : at + 1, :]


def norm_rows(source, gain, shift, unit, inverse, target, rows):
    size = 32

    def step(at, carry):
        place = pl.ds(aligned(at * size, size), size)
        values = source[place, :].astype(f32)
        centre = jnp.sum(values, 1, keepdims=True) * (1.0 / D)
        spread = jnp.sum(values * values, 1, keepdims=True) * (1.0 / D) - centre * centre
        scale = lax.rsqrt(spread + norm_epsilon)
        norm = (values - centre) * scale
        unit[place, :] = norm
        inverse[place, :] = jnp.broadcast_to(scale, (size, 128))
        target[place, :] = (norm * gain + shift).astype(bf16)
        return carry

    lax.fori_loop(0, rows // size, step, 0)


def gelu_both(values):
    normal = 0.5 + 0.5 * lax.erf(values * (0.5**0.5))
    density = jnp.exp(-0.5 * values * values) * 0.3989422804014327
    return values * normal, normal + values * density


def forward_kernel(count, tokens, *refs):
    (
        state_in,
        spot_in,
        bias_in,
        shard_a,
        shard_b,
        shard_c,
        shard_d,
        w_a,
        w_b,
        w_c,
        w_d,
        vecs_out,
        unit_one_out,
        inv_one_out,
        normed_out,
        heads_out,
        lse_out,
        mixed_out,
        branch_out,
        unit_two_out,
        inv_two_out,
        normed_two_out,
        active_out,
        slope_out,
        output_out,
        head_mix_out,
        block_out,
        state,
        spot,
        spare,
        raw,
        vecs,
        wq,
        wm,
        wu,
        wd,
        unit,
        inverse,
        unit_two,
        inverse_two,
        normed,
        normed_two,
        heads_all,
        head_tx,
        head_mix,
        lse,
        mixed_all,
        branch,
        output,
        active,
        slope,
        tx,
        rx,
        part,
        g_send,
        g_recv,
        g_own,
        v_send,
        v_recv,
        y_send,
        y_recv,
        c_send,
        c_recv,
        stage_sem,
        save_sem,
    ) = refs
    rows = state_in.shape[0]
    group = 2 * rows
    half = D // 2
    width = half // 2
    place = Place(count)
    row, col = place.row, place.col
    wholes = (w_a, w_b, w_c, w_d)
    gather = Gather(place, (shard_a, shard_b, shard_c, shard_d), wholes, g_send, g_recv, g_own)
    place.greet()
    gather.start(0)
    gather.start(1)

    pending = {}

    def save(name, at, source, target):
        settle(name)
        copy = pltpu.make_async_copy(source, target, save_sem.at[at])
        copy.start()
        pending[name] = copy

    def settle(*names):
        for name in names:
            if name in pending:
                pending.pop(name).wait()

    staged = {}

    def stage(kind, layer):
        gather.arrive(layer * KINDS + kind)
        buffer = (wq, wm, wu, wd)[kind]
        copy = pltpu.make_async_copy(wholes[kind].at[layer], buffer, stage_sem.at[kind])
        copy.start()
        staged[kind] = copy

    def ready(kind):
        staged.pop(kind).wait()

    y_at = [0]

    def y_copy(source, target):
        at = y_at[0]
        y_at[0] += 1
        return remote(source, target, y_send.at[at], y_recv.at[at], place.y_peer)

    chunk = rows // SPLIT

    def exchange_rows(buffer):
        copies = []
        for at in range(SPLIT):
            copies.append(
                y_copy(
                    buffer.at[pl.ds(at * chunk, chunk), :],
                    buffer.at[pl.ds(rows + at * chunk, chunk), :],
                )
            )
            copies[-1].start()
        return copies

    spot[...] = spot_in[...]
    state[...] = state_in[...].astype(f32)
    gather_vectors(place, spot, spare, raw, vecs, v_send, v_recv)
    save("vecs", 11, vecs, vecs_out)
    gather.to_pair(0)
    gather.start(2)

    plan = {
        (0, "norm"): ((gather.to_core, 0), (stage, 0, 0), (gather.to_pair, 1), (gather.start, 3)),
        (0, "triple"): ((gather.to_core, 1),),
        (0, "attend"): ((gather.to_pair, 2), (stage, 1, 0), (gather.start, 4)),
        (0, "project"): ((gather.to_core, 2),),
        (0, "branch"): ((gather.to_pair, 3), (gather.start, 5), (stage, 2, 0)),
        (0, "expand"): ((gather.to_core, 3), (gather.start, 6)),
        (0, "shrink"): ((gather.to_pair, 4),),
        (0, "output"): ((gather.to_core, 4), (stage, 0, 1), (gather.to_pair, 5), (gather.start, 7)),
        (1, "norm"): ((gather.to_core, 5),),
        (1, "triple"): ((stage, 1, 1), (gather.to_pair, 6)),
        (1, "attend"): ((gather.to_core, 6),),
        (1, "project"): ((gather.to_pair, 7),),
        (1, "branch"): ((stage, 2, 1),),
        (1, "expand"): ((gather.to_core, 7),),
    }

    lane = lax.broadcasted_iota(jnp.int32, (1, 128), 1) < HEAD_DIM
    valid = lax.broadcasted_iota(jnp.int32, (rows, 1), 0) < tokens - col * rows

    def vector(layer, at):
        return vecs[layer : layer + 1, at * D : (at + 1) * D]

    for layer in range(LAYERS):

        def pump(name, layer=layer):
            for action, *args in plan.get((layer, name), ()):
                action(*args)

        settle("unit", "inverse", "normed")
        norm_rows(state, vector(layer, 0), vector(layer, 1), unit, inverse, normed, rows)
        copies = exchange_rows(normed)
        save("unit", 0, unit, unit_one_out.at[layer])
        save("inverse", 1, inverse, inv_one_out.at[layer])
        pump("norm")
        ready(0)
        heads, mixed = heads_all.at[layer], mixed_all.at[layer]

        def triple(start):
            def step(at, carry):
                part_at = lax.rem(at, 3)
                mine = lax.div(at, 3)
                owner = jnp.where(mine == 1, col, 1 - col)
                column = aligned(part_at * half + owner * width)
                value = nn(normed[start : start + rows, :], wq[:, pl.ds(column, width)])
                bias_at = aligned(
                    jnp.where(part_at == 2, 3 * D, 2 * D) + row * half + owner * width
                )
                bias = vecs[layer : layer + 1, pl.ds(bias_at, width)]
                bias = bias * jnp.where(part_at == 1, 0.0, 1.0)
                value = jnp.where(valid, value + bias, 0.0).astype(bf16)
                lanes = pl.ds(aligned(part_at * width), width)

                @pl.when(mine == 0)
                def _():
                    head_tx[start : start + rows, lanes] = value

                @pl.when(mine == 1)
                def _():
                    heads[pl.ds(aligned(col * group + start, 16), rows), lanes] = value

                return carry

            lax.fori_loop(0, 6, step, 0)

        core_copies = []

        def send_heads(start):
            at = layer * 3 + (start > 0)
            core_copies.append(
                remote(
                    head_tx.at[pl.ds(start, rows), :],
                    heads.at[pl.ds(aligned(col * group + start, 16), rows), :],
                    c_send.at[at],
                    c_recv.at[at],
                    place.c_peer,
                )
            )
            core_copies[-1].start()

        triple(0)
        send_heads(0)
        for copy in copies:
            copy.wait()
        save("normed", 2, normed, normed_out.at[layer])
        triple(rows)
        send_heads(rows)
        pump("triple")
        for copy in core_copies:
            copy.wait()
        save("heads", 3, heads, heads_out.at[layer])
        settle("lse", "head_mix")

        def attend(owner):
            tile = rows // 2

            def step(at, carry):
                place_rows = pl.ds(aligned(owner * group + at * tile, 16), tile)
                for pair in range(width // 128):
                    lanes = slice(pair * 128, pair * 128 + 128)
                    query = heads[place_rows, lanes] * jnp.asarray(HEAD_DIM**-0.5, bf16)
                    zero = jnp.zeros_like(query)
                    both = jnp.concatenate(
                        [jnp.where(lane, query, zero), jnp.where(lane, zero, query)], 0
                    )
                    key = heads[:, width + pair * 128 : width + pair * 128 + 128]
                    value = heads[:, 2 * width + pair * 128 : 2 * width + pair * 128 + 128]
                    scores = nt(both, key) + bias_in[...]
                    peak = jnp.max(scores, 1, keepdims=True)
                    weights = jnp.exp(scores - peak)
                    total = jnp.sum(weights, 1, keepdims=True)
                    result = nn(weights.astype(bf16), value) / total
                    logsum = peak + jnp.log(total)
                    head_mix[place_rows, lanes] = jnp.where(
                        lane, result[:tile], result[tile:]
                    ).astype(bf16)
                    lse[place_rows, lanes] = jnp.where(lane, logsum[:tile], logsum[tile:])
                return carry

            lax.fori_loop(0, group // tile, step, 0)

        attend(1 - col)
        lanes = pl.ds(aligned(col * width), width)
        back = remote(
            head_mix.at[pl.ds(aligned((1 - col) * group, 16), group), :],
            mixed.at[:, lanes],
            c_send.at[layer * 3 + 2],
            c_recv.at[layer * 3 + 2],
            place.c_peer,
        )
        back.start()
        pump("attend")
        attend(col)
        mixed[:, lanes] = head_mix[pl.ds(aligned(col * group, 16), group), :]
        back.wait()
        save("lse", 4, lse, lse_out.at[layer])
        save("head_mix", 14, head_mix, head_mix_out.at[layer])
        save("mixed", 5, mixed, mixed_out.at[layer])
        ready(1)
        pump("project")
        settle("normed_two")

        def project(start, size, target, target_at):
            def step(at, carry):
                lanes = pl.ds(aligned(at * half), half)
                value = nn(mixed[start : start + size, :], wm[:, lanes])
                target[pl.ds(target_at, size), lanes] = value.astype(target.dtype)
                return carry

            lax.fori_loop(0, 2, step, 0)

        copies = []
        for at in range(SPLIT):
            project(rows + at * chunk, chunk, tx, at * chunk)
            view = pl.ds(at * chunk, chunk)
            copies.append(y_copy(tx.at[view, :], rx.at[view, :]))
            copies[-1].start()
        project(0, rows, part, 0)
        pump("branch")
        for copy in copies:
            copy.wait()
        settle("branch", "unit_two", "inverse_two")
        branch[...] = part[...] + rx[...].astype(f32) + vector(layer, 4)
        state[...] = state[...] + vector(layer, 5) * branch[...]
        save("branch", 6, branch, branch_out.at[layer])
        norm_rows(
            state, vector(layer, 6), vector(layer, 7), unit_two, inverse_two, normed_two, rows
        )
        copies = exchange_rows(normed_two)
        save("unit_two", 7, unit_two, unit_two_out.at[layer])
        save("inverse_two", 8, inverse_two, inv_two_out.at[layer])
        pump("expand")
        ready(2)
        settle("active", "slope")

        def expand(start, size):
            def step(at, carry):
                lanes = pl.ds(aligned(at * half), half)
                bias_at = aligned(8 * D + row * (FF // 2) + at * half)
                value = nn(normed_two[start : start + size, :], wu[:, lanes])
                value = value + vecs[layer : layer + 1, pl.ds(bias_at, half)]
                act, grad = gelu_both(value)
                active[start : start + size, lanes] = act.astype(bf16)
                slope[start : start + size, lanes] = grad.astype(bf16)
                return carry

            lax.fori_loop(0, FF // 2 // half, step, 0)

        def shrink(start, size, target, target_at):
            def step(at, carry):
                lanes = pl.ds(aligned(at * half), half)
                value = nn(active[start : start + size, :], wd[:, lanes])
                target[pl.ds(target_at, size), lanes] = value.astype(target.dtype)
                return carry

            lax.fori_loop(0, 2, step, 0)

        expand(0, rows)
        stage(3, layer)
        settle("normed")
        ready(3)
        shrink(0, rows, part, 0)
        pump("shrink")
        back_copies = []
        for at in range(SPLIT):
            copies[at].wait()
            start = rows + at * chunk
            expand(start, chunk)
            shrink(start, chunk, tx, at * chunk)
            view = pl.ds(at * chunk, chunk)
            back_copies.append(y_copy(tx.at[view, :], rx.at[view, :]))
            back_copies[-1].start()
        save("normed_two", 9, normed_two, normed_two_out.at[layer])
        save("active", 10, active, active_out.at[layer])
        save("slope", 12, slope, slope_out.at[layer])
        pump("output")
        for copy in back_copies:
            copy.wait()
        settle("output")
        output[...] = part[...] + rx[...].astype(f32) + vector(layer, 12)
        state[...] = state[...] + vector(layer, 13) * output[...]
        save("output", 13, output, output_out.at[layer])
    block_out[...] = state[...].astype(bf16)
    gather.finish()
    settle(*list(pending))


def forward_call(mesh_count, tokens, state, spot, bias, shards):
    rows = state.shape[0]
    group = 2 * rows
    half = D // 2
    width = half // 2
    line = mesh_count // 2

    def shape(*dims, kind=f32):
        return jax.ShapeDtypeStruct(dims, kind)

    outs = [
        shape(LAYERS, D, 3 * half, kind=bf16),
        shape(LAYERS, half, D, kind=bf16),
        shape(LAYERS, D, FF // 2, kind=bf16),
        shape(LAYERS, FF // 2, D, kind=bf16),
        shape(LAYERS, 10 * D + FF),
        shape(LAYERS, rows, D),
        shape(LAYERS, rows, 128),
        shape(LAYERS, group, D, kind=bf16),
        shape(LAYERS, 2 * group, 3 * width, kind=bf16),
        shape(LAYERS, 2 * group, width),
        shape(LAYERS, group, half, kind=bf16),
        shape(LAYERS, rows, D),
        shape(LAYERS, rows, D),
        shape(LAYERS, rows, 128),
        shape(LAYERS, group, D, kind=bf16),
        shape(LAYERS, group, FF // 2, kind=bf16),
        shape(LAYERS, group, FF // 2, kind=bf16),
        shape(LAYERS, rows, D),
        shape(LAYERS, 2 * group, width, kind=bf16),
        shape(rows, D, kind=bf16),
    ]
    dma = pltpu.SemaphoreType.DMA
    scratch = [
        pltpu.VMEM((rows, D), f32),
        pltpu.VMEM(spot.shape, f32),
        pltpu.VMEM((3,) + spot.shape, f32),
        pltpu.VMEM((line,) + spot.shape, f32),
        pltpu.VMEM((LAYERS, 10 * D + FF), f32),
        pltpu.VMEM((D, 3 * half), bf16),
        pltpu.VMEM((half, D), bf16),
        pltpu.VMEM((D, FF // 2), bf16),
        pltpu.VMEM((FF // 2, D), bf16),
        pltpu.VMEM((rows, D), f32),
        pltpu.VMEM((rows, 128), f32),
        pltpu.VMEM((rows, D), f32),
        pltpu.VMEM((rows, 128), f32),
        pltpu.VMEM((group, D), bf16),
        pltpu.VMEM((group, D), bf16),
        pltpu.VMEM((LAYERS, 2 * group, 3 * width), bf16),
        pltpu.VMEM((group, 3 * width), bf16),
        pltpu.VMEM((2 * group, width), bf16),
        pltpu.VMEM((2 * group, width), f32),
        pltpu.VMEM((LAYERS, group, half), bf16),
        pltpu.VMEM((rows, D), f32),
        pltpu.VMEM((rows, D), f32),
        pltpu.VMEM((group, FF // 2), bf16),
        pltpu.VMEM((group, FF // 2), bf16),
        pltpu.VMEM((rows, D), bf16),
        pltpu.VMEM((rows, D), bf16),
        pltpu.VMEM((rows, D), f32),
        dma((GROUPS, 2 * line)),
        dma((GROUPS, 2 * line)),
        dma((GROUPS,)),
        dma((line + 2,)),
        dma((line + 2,)),
        dma((LAYERS * 4 * SPLIT,)),
        dma((LAYERS * 4 * SPLIT,)),
        dma((LAYERS * 3,)),
        dma((LAYERS * 3,)),
        dma((KINDS,)),
        dma((15,)),
    ]
    return pl.pallas_call(
        functools.partial(forward_kernel, mesh_count, tokens),
        out_shape=outs,
        in_specs=[WHOLE] * 3 + [ANY] * 4,
        out_specs=[ANY] * 19 + [WHOLE],
        scratch_shapes=scratch,
        compiler_params=pltpu.CompilerParams(
            collective_id=0, has_side_effects=True, vmem_limit_bytes=60 << 20
        ),
        name="forward",
    )(state, spot, bias, *shards)


def fold(values):
    return jnp.sum(values.reshape(-1, 8, values.shape[-1]), 0)


def total(values):
    return jnp.sum(values, 0, keepdims=True)


def flip(picks, values):
    high = values.astype(bf16)
    rest = values - high.astype(f32)
    middle = rest.astype(bf16)
    low = (rest - middle.astype(f32)).astype(bf16)
    return nt(picks, high) + nt(picks, middle) + nt(picks, low)


class Scatter:
    def __init__(self, place, sums, pair_rx, line_rx, outs, refs):
        self.place, self.sums, self.pair_rx, self.line_rx = place, sums, pair_rx, line_rx
        self.outs, self.result = outs, refs["result"]
        self.x_send, self.x_recv = refs["x_send"], refs["x_recv"]
        self.z_send, self.z_recv = refs["z_send"], refs["z_recv"]
        self.x_free, self.z_free, self.out_sem = refs["x_free"], refs["z_free"], refs["out_sem"]
        self.writing = {}

    def size(self, kind):
        return self.sums[kind].shape[0] // self.place.count

    def block(self, kind, dp):
        size = self.size(kind)
        return pl.ds(aligned(dp * size, 16), size)

    def x_copy(self, layer, kind, outer):
        place = self.place
        size = self.size(kind)
        at = layer * KINDS + kind
        return remote(
            self.sums[kind].at[self.block(kind, 2 * outer + 1 - place.pair), :],
            self.pair_rx[kind].at[pl.ds(outer * size, size), :],
            self.x_send.at[at, outer],
            self.x_recv.at[at, outer],
            place.x_peer,
        )

    def z_copy(self, layer, kind, step):
        place = self.place
        size = self.size(kind)
        at = layer * KINDS + kind
        outer = lax.rem(place.outer + step, place.line)
        return remote(
            self.pair_rx[kind].at[pl.ds(aligned(outer * size, 16), size), :],
            self.line_rx[kind].at[step - 1],
            self.z_send.at[at, step - 1],
            self.z_recv.at[at, step - 1],
            place.z_peer(step),
        )

    def x_start(self, layer, kind):
        if layer < LAYERS - 1:
            pl.semaphore_wait(self.x_free.at[kind], 1)
        for outer in range(self.place.line):
            self.x_copy(layer, kind, outer).start()

    def x_finish(self, layer, kind):
        place = self.place
        size = self.size(kind)
        for outer in range(place.line):
            self.x_copy(layer, kind, outer).wait()
        rows = min(size, 64)

        def step(at, carry):
            outer = lax.div(at, size // rows)
            inner = lax.rem(at, size // rows)
            here = pl.ds(aligned(outer * size + inner * rows, 16), rows)
            own = pl.ds(aligned((2 * outer + place.pair) * size + inner * rows, 16), rows)
            pair_rx = self.pair_rx[kind]
            value = pair_rx[here, :].astype(f32) + self.sums[kind][own, :].astype(f32)
            pair_rx[here, :] = value.astype(bf16)
            return carry

        lax.fori_loop(0, place.line * (size // rows), step, 0)
        if layer < LAYERS - 1:
            pl.semaphore_wait(self.z_free.at[kind], place.line - 1)
        for step_at in range(1, place.line):
            self.z_copy(layer, kind, step_at).start()

    def z_finish(self, layer, kind):
        place = self.place
        size = self.size(kind)
        for step_at in range(1, place.line):
            self.z_copy(layer, kind, step_at).wait()
        if kind in self.writing:
            self.writing.pop(kind).wait()
        rows = min(size, 64)

        def step(at, carry):
            here = pl.ds(aligned(at * rows, 16), rows)
            own = pl.ds(aligned(place.outer * size + at * rows, 16), rows)
            value = self.pair_rx[kind][own, :].astype(f32)
            for step_at in range(place.line - 1):
                value = value + self.line_rx[kind][step_at, here, :].astype(f32)
            self.result[kind][here, :] = value
            return carry

        lax.fori_loop(0, size // rows, step, 0)
        copy = pltpu.make_async_copy(
            self.result[kind], self.outs[kind].at[layer], self.out_sem.at[kind]
        )
        copy.start()
        self.writing[kind] = copy
        if layer == LAYERS - 1:
            pl.semaphore_signal(
                self.x_free.at[kind], inc=1, device_id=place.x_peer, device_id_type=MESH
            )
            for step_at in range(1, place.line):
                pl.semaphore_signal(
                    self.z_free.at[kind],
                    inc=1,
                    device_id=place.z_peer(step_at),
                    device_id_type=MESH,
                )

    def finish(self):
        for copy in self.writing.values():
            copy.wait()


def scatter_vectors(place, grads, packed, spare, spot, target, send, recv):
    used = grads.shape[1] // 128 // place.line
    packed[...] = jnp.zeros_like(packed)
    for outer in range(place.line):
        for layer in range(LAYERS):
            for at in range(used):
                start = (outer * used + at) * 128
                packed[outer, layer, at : at + 1, :] = grads[layer : layer + 1, start : start + 128]
    copies = []
    for step in range(1, place.line):
        outer = lax.rem(place.outer + step, place.line)
        copy = remote(
            packed.at[outer], spare.at[2 + step], send.at[2 + step], recv.at[2 + step], place.z_peer(step)
        )
        copy.start()
        copies.append(copy)
    for copy in copies:
        copy.wait()
    value = packed[place.outer]
    for step in range(1, place.line):
        value = value + spare[2 + step]
    spot[...] = value
    for at, peer in enumerate((place.x_peer, place.y_peer, place.c_peer)):
        copy = remote(spot, spare.at[at], send.at[at], recv.at[at], peer)
        copy.start()
        copy.wait()
        spot[...] = spot[...] + spare[at]
    target[...] = spot[...]


def backward_kernel(count, tokens, *refs):
    (
        grad_in,
        vecs,
        w_a,
        w_b,
        w_c,
        w_d,
        unit_one_in,
        inv_one_in,
        normed_in,
        heads_in,
        lse_in,
        mixed_in,
        branch_in,
        unit_two_in,
        inv_two_in,
        normed_two_in,
        active_in,
        slope_in,
        output_in,
        head_mix_in,
        grad_a,
        grad_b,
        grad_c,
        grad_d,
        grad_out,
        vec_out,
        wq,
        wm,
        wu,
        wd,
        active,
        slope,
        feed,
        heads,
        lse,
        head_mix,
        mixed,
        aside,
        unit,
        inverse,
        grad,
        back_out,
        back_branch,
        part,
        tx,
        rx,
        head_back,
        head_tx,
        head_grad,
        key_sum,
        value_sum,
        half_tx,
        sum_a,
        sum_b,
        sum_c,
        sum_d,
        pair_a,
        pair_b,
        pair_c,
        pair_d,
        line_a,
        line_b,
        line_c,
        line_d,
        result_a,
        result_b,
        result_c,
        result_d,
        vec_grads,
        packed,
        spare,
        spot,
        y_send,
        y_recv,
        c_send,
        c_recv,
        x_send,
        x_recv,
        z_send,
        z_recv,
        x_free,
        z_free,
        out_sem,
        v_send,
        v_recv,
        load_sem,
    ) = refs
    rows = grad_in.shape[0]
    group = 2 * rows
    half = D // 2
    width = half // 2
    pairs = width // 128
    place = Place(count)
    row, col = place.row, place.col
    sums = (sum_a, sum_b, sum_c, sum_d)
    place.greet()
    scatter = Scatter(
        place,
        sums,
        (pair_a, pair_b, pair_c, pair_d),
        (line_a, line_b, line_c, line_d),
        (grad_a, grad_b, grad_c, grad_d),
        {
            "result": (result_a, result_b, result_c, result_d),
            "x_send": x_send,
            "x_recv": x_recv,
            "z_send": z_send,
            "z_recv": z_recv,
            "x_free": x_free,
            "z_free": z_free,
            "out_sem": out_sem,
        },
    )
    triple_back = active

    sources = {
        "wd": (w_d, wd),
        "wu": (w_c, wu),
        "wm": (w_b, wm),
        "wq": (w_a, wq),
        "slope": (slope_in, slope),
        "active": (active_in, active),
        "normed_two": (normed_two_in, feed),
        "normed": (normed_in, feed),
        "output": (output_in, aside),
        "branch": (branch_in, aside),
        "unit_two": (unit_two_in, unit),
        "unit_one": (unit_one_in, unit),
        "inv_two": (inv_two_in, inverse),
        "inv_one": (inv_one_in, inverse),
        "heads": (heads_in, heads),
        "lse": (lse_in, lse),
        "head_mix": (head_mix_in, head_mix),
        "mixed": (mixed_in, mixed),
    }
    names = list(sources)
    loading = {}

    def load(layer, *wanted):
        for name in wanted:
            source, buffer = sources[name]
            copy = pltpu.make_async_copy(
                source.at[layer], buffer, load_sem.at[names.index(name)]
            )
            copy.start()
            loading[name] = copy

    def loaded(*wanted):
        for name in wanted:
            loading.pop(name).wait()

    y_at = [0]

    def y_copy(source, target):
        at = y_at[0]
        y_at[0] += 1
        return remote(source, target, y_send.at[at], y_recv.at[at], place.y_peer)

    c_at = [0]

    def c_copy(source, target):
        at = c_at[0]
        c_at[0] += 1
        return remote(source, target, c_send.at[at], c_recv.at[at], place.c_peer)

    chunk = rows // SPLIT

    def exchange_rows(buffer):
        copies = []
        for at in range(SPLIT):
            copies.append(
                y_copy(
                    buffer.at[pl.ds(at * chunk, chunk), :],
                    buffer.at[pl.ds(rows + at * chunk, chunk), :],
                )
            )
            copies[-1].start()
        return copies

    load(1, "slope", "wd", "output", "wu", "normed_two", "active", "unit_two", "inv_two")
    load(1, "wm", "mixed", "heads", "lse", "head_mix", "wq")
    grad[...] = grad_in[...].astype(f32)
    vec_grads[...] = jnp.zeros_like(vec_grads)
    lane = lax.broadcasted_iota(jnp.int32, (1, 128), 1) < HEAD_DIM
    pick_row = lax.broadcasted_iota(jnp.int32, (8, 128), 0)
    pick_lane = lax.broadcasted_iota(jnp.int32, (8, 128), 1)
    halves = (
        ((pick_row == 0) & (pick_lane < HEAD_DIM)) | ((pick_row == 1) & (pick_lane >= HEAD_DIM))
    ).astype(bf16)
    firsts = (pick_lane == pick_row * HEAD_DIM).astype(bf16)
    size = 32

    def vector(layer, at):
        return vecs[layer : layer + 1, at * D : (at + 1) * D]

    def note(layer, at, value):
        vec_grads[layer : layer + 1, at * D : (at + 1) * D] = value

    def by_rows(count_rows, body, terms):
        def step(at, carry):
            adds = body(pl.ds(aligned(at * size, size), size))
            return tuple(old + fold(new) for old, new in zip(carry, adds, strict=True))

        zeros = tuple(jnp.zeros((8, D), f32) for _ in range(terms))
        sums_ = lax.fori_loop(0, count_rows // size, step, zeros)
        return [total(value) for value in sums_]

    def half_tiles(kind):
        return {0: 3, 1: 1, 2: FF // 2 // half, 3: FF // 2 // half}[kind]

    def weight_grad(kind, owner, at):
        owned = pl.ds(aligned(owner * half), half)
        tile = pl.ds(aligned(at * half), half)
        if kind == 0:
            return tn(feed[:, owned], triple_back[:, tile])
        if kind == 1:
            return tn(mixed[...], back_branch[:, owned])
        if kind == 2:
            return tn(feed[:, owned], slope[:, tile])
        return tn(active[:, tile], back_out[:, owned])

    def spot_of(kind, at):
        tile = pl.ds(aligned(at * half), half)
        return (tile, slice(None)) if kind == 3 else (slice(None), tile)

    half_copies = {}

    def produce_other(layer, kind):
        target = sums[kind]
        buffer = half_tx[kind]

        def step(at, carry):
            buffer[spot_of(kind, at)] = weight_grad(kind, 1 - col, at).astype(bf16)
            return carry

        lax.fori_loop(0, half_tiles(kind), step, 0)
        copy = c_copy(buffer, target)
        copy.start()
        half_copies[kind] = copy

    def produce_own(layer, kind):
        target = sums[kind]
        half_copies.pop(kind).wait()

        def step(at, carry):
            here = spot_of(kind, at)
            value = weight_grad(kind, col, at) + target[here].astype(f32)
            target[here] = value.astype(bf16)
            return carry

        lax.fori_loop(0, half_tiles(kind), step, 0)
        scatter.x_start(layer, kind)

    for layer in reversed(range(LAYERS)):
        last = layer == LAYERS - 1
        loaded("output")

        def out_rows(here):
            value = grad[here, :]
            back = (vector(layer, 13) * value).astype(bf16)
            back_out[here, :] = back
            return (value * aside[here, :], back.astype(f32))

        scale_grad, bias_grad = by_rows(rows, out_rows, 2)
        copies = exchange_rows(back_out)
        note(layer, 13, scale_grad)
        note(layer, 12, bias_grad)
        load(layer, "branch")
        if not last:
            scatter.z_finish(1, 3)
            scatter.z_finish(1, 2)
        loaded("slope", "wd")

        def inner_rows(start, count_rows):
            def step(at, carry):
                lanes = pl.ds(aligned(at * half), half)
                value = nt(back_out[start : start + count_rows, :], wd[lanes, :])
                back = (value * slope[start : start + count_rows, lanes].astype(f32)).astype(bf16)
                slope[start : start + count_rows, lanes] = back
                there = pl.ds(aligned(8 * D + row * (FF // 2) + at * half), half)
                old = vec_grads[layer : layer + 1, there]
                vec_grads[layer : layer + 1, there] = old + total(back.astype(f32))
                return carry

            lax.fori_loop(0, FF // 2 // half, step, 0)

        def two_rows(start, count_rows, target, target_at):
            def step(at, carry):
                lanes = pl.ds(aligned(at * half), half)
                value = nt(slope[start : start + count_rows, :], wu[lanes, :])
                target[pl.ds(target_at, count_rows), lanes] = value.astype(target.dtype)
                return carry

            lax.fori_loop(0, 2, step, 0)

        inner_rows(0, rows)
        loaded("wu")
        if not last:
            scatter.x_finish(1, 1)
        back_copies = []
        for at in range(SPLIT):
            copies[at].wait()
            start = rows + at * chunk
            inner_rows(start, chunk)
            two_rows(start, chunk, tx, at * chunk)
            view = pl.ds(at * chunk, chunk)
            back_copies.append(y_copy(tx.at[view, :], rx.at[view, :]))
            back_copies[-1].start()
        two_rows(0, rows, part, 0)
        if last:
            load(0, "wd")
        else:
            scatter.x_finish(1, 0)
        loaded("active", "normed_two")
        produce_other(layer, 3)
        produce_other(layer, 2)
        produce_own(layer, 3)
        produce_own(layer, 2)
        load(layer, "normed")
        for copy in back_copies:
            copy.wait()
        loaded("unit_two", "inv_two", "branch")

        def middle_rows(here):
            back = part[here, :] + rx[here, :].astype(f32)
            norm = unit[here, :]
            scaled = back * vector(layer, 6)
            first = jnp.sum(scaled, 1, keepdims=True) * (1.0 / D)
            second = jnp.sum(scaled * norm, 1, keepdims=True) * (1.0 / D)
            scale = inverse[here, 0:1]
            value = grad[here, :] + scale * (scaled - first - norm * second)
            grad[here, :] = value
            branch_back = (vector(layer, 5) * value).astype(bf16)
            back_branch[here, :] = branch_back
            return (back * norm, back, value * aside[here, :], branch_back.astype(f32))

        terms = by_rows(rows, middle_rows, 4)
        copies = exchange_rows(back_branch)
        for at, value in zip((6, 7, 5, 4), terms, strict=True):
            note(layer, at, value)
        load(layer, "unit_one", "inv_one")
        loaded("wm")

        def mixed_rows(start, count_rows):
            for owner in range(2):
                lanes = slice(owner * width, owner * width + width)
                value = nt(back_branch[start : start + count_rows, :], wm[lanes, :]).astype(bf16)

                @pl.when(owner == col)
                def _():
                    head_back[pl.ds(aligned(col * group + start, 16), count_rows), :] = value

                @pl.when(owner != col)
                def _():
                    head_tx[start : start + count_rows, :] = value

        core_copies = []

        def send_back(start):
            core_copies.append(
                c_copy(
                    head_tx.at[pl.ds(start, rows), :],
                    head_back.at[pl.ds(aligned(col * group + start, 16), rows), :],
                )
            )
            core_copies[-1].start()

        mixed_rows(0, rows)
        send_back(0)
        for copy in copies:
            copy.wait()
        mixed_rows(rows, rows)
        send_back(rows)
        loaded("heads", "lse", "head_mix", "mixed")
        if last:
            load(0, "wm")
        else:
            scatter.z_finish(1, 1)
            scatter.z_finish(1, 0)
        for copy in core_copies:
            copy.wait()

        piece = 2 * group // 4
        head_copies = []
        for pair in range(pairs):
            lanes = slice(pair * 128, pair * 128 + 128)
            key_lanes = slice(width + pair * 128, width + pair * 128 + 128)
            value_lanes = slice(2 * width + pair * 128, 2 * width + pair * 128 + 128)
            key_sum[...] = jnp.zeros_like(key_sum)
            value_sum[...] = jnp.zeros_like(value_sum)

            def step(at, carry, lanes=lanes, key_lanes=key_lanes, value_lanes=value_lanes):
                here = pl.ds(aligned(at * 128), 128)
                query = heads[here, lanes] * jnp.asarray(HEAD_DIM**-0.5, bf16)
                back = head_back[here, lanes]
                zero = jnp.zeros_like(query)
                queries = jnp.concatenate(
                    [jnp.where(lane, query, zero), jnp.where(lane, zero, query)], 0
                )
                backs = jnp.concatenate(
                    [jnp.where(lane, back, zero), jnp.where(lane, zero, back)], 0
                )
                logs = flip(firsts, lse[here, lanes])
                logs = jnp.concatenate([logs[0:1], logs[1:2]], 1)
                inner = flip(halves, back.astype(f32) * head_mix[here, lanes].astype(f32))
                inner = jnp.concatenate([inner[0:1], inner[1:2]], 1)
                query_grad = jnp.zeros((256, 128), f32)
                for block in range(4):
                    keys = slice(block * piece, block * piece + piece)
                    key = heads[keys, key_lanes]
                    scores = nt(key, queries)
                    probs = jnp.exp(jnp.minimum(scores - logs, 0.0))
                    back_probs = nt(heads[keys, value_lanes], backs)
                    back_scores = (probs * (back_probs - inner)).astype(bf16)
                    value_sum[keys, :] += nn(probs.astype(bf16), backs)
                    key_sum[keys, :] += nn(back_scores, queries)
                    query_grad = query_grad + tn(back_scores, key)
                query_grad = query_grad * HEAD_DIM**-0.5
                head_grad[here, lanes] = jnp.where(
                    lane, query_grad[:128], query_grad[128:]
                ).astype(bf16)
                return carry

            lax.fori_loop(0, 2 * group // 128, step, 0)
            for owner in range(2):
                edge = owner * rows
                valid = lax.broadcasted_iota(jnp.int32, (rows, 1), 0) < tokens - edge
                for part_at in range(2):
                    here = slice(owner * group + part_at * rows, owner * group + part_at * rows + rows)
                    head_grad[here, key_lanes] = jnp.where(valid, key_sum[here, :], 0.0).astype(bf16)
                    head_grad[here, value_lanes] = jnp.where(valid, value_sum[here, :], 0.0).astype(bf16)
            if pair == pairs - 1:
                if last:
                    scatter.x_finish(1, 2)
            else:
                scatter.x_finish(layer, 3)
            there = pl.ds(aligned((1 - col) * group, 16), group)
            mine = pl.ds(aligned(col * group, 16), group)
            for part_at, source in enumerate((lanes, key_lanes, value_lanes)):
                target = pl.ds(aligned(part_at * half + col * width + pair * 128), 128)
                copy = c_copy(head_grad.at[there, source], triple_back.at[:, target])
                copy.start()
                head_copies.append(copy)
                triple_back[:, target] = head_grad[mine, source]
                if part_at != 1:
                    bias_at = pl.ds(
                        aligned((3 * D if part_at else 2 * D) + row * half + col * width + pair * 128), 128
                    )
                    vec_grads[layer : layer + 1, bias_at] = total(head_grad[:, source].astype(f32))
        if not last:
            scatter.x_finish(0, 2)
        for copy in head_copies:
            copy.wait()
        loaded("wq", "normed")
        if not last:
            produce_other(layer, 0)

        def one_rows(start, count_rows, target, target_at):
            def step(at, carry):
                lanes = pl.ds(aligned(at * half), half)
                value = nt(triple_back[start : start + count_rows, : 3 * half], wq[lanes, :])
                target[pl.ds(target_at, count_rows), lanes] = value.astype(target.dtype)
                return carry

            lax.fori_loop(0, 2, step, 0)

        back_copies = []
        for at in range(SPLIT):
            start = rows + at * chunk
            one_rows(start, chunk, tx, at * chunk)
            view = pl.ds(at * chunk, chunk)
            back_copies.append(y_copy(tx.at[view, :], rx.at[view, :]))
            back_copies[-1].start()
        if last:
            produce_other(layer, 1)
            produce_other(layer, 0)
            produce_own(layer, 1)
            produce_own(layer, 0)
        else:
            produce_own(layer, 0)
            produce_other(layer, 1)
            produce_own(layer, 1)
        one_rows(0, rows, part, 0)
        if last:
            load(0, "slope", "wu", "wq", "output", "normed_two", "active")
            load(0, "mixed", "heads", "lse", "head_mix")
        loaded("unit_one", "inv_one")
        for copy in back_copies:
            copy.wait()

        def input_rows(here):
            back = part[here, :] + rx[here, :].astype(f32)
            norm = unit[here, :]
            scaled = back * vector(layer, 0)
            first = jnp.sum(scaled, 1, keepdims=True) * (1.0 / D)
            second = jnp.sum(scaled * norm, 1, keepdims=True) * (1.0 / D)
            scale = inverse[here, 0:1]
            grad[here, :] = grad[here, :] + scale * (scaled - first - norm * second)
            return (back * norm, back)

        terms = by_rows(rows, input_rows, 2)
        for at, value in zip((0, 1), terms, strict=True):
            note(layer, at, value)
        if last:
            load(0, "unit_two", "inv_two")
    grad_out[...] = grad[...]
    scatter.z_finish(0, 3)
    scatter.z_finish(0, 2)
    scatter_vectors(place, vec_grads, packed, spare, spot, vec_out, v_send, v_recv)
    scatter.x_finish(0, 0)
    scatter.x_finish(0, 1)
    scatter.z_finish(0, 0)
    scatter.z_finish(0, 1)
    scatter.finish()


def backward_call(mesh_count, tokens, grad, vecs, weights, saved, spot_shape):
    rows = grad.shape[0]
    group = 2 * rows
    half = D // 2
    width = half // 2
    line = mesh_count // 2
    wide = FF // 2

    def shape(*dims, kind=f32):
        return jax.ShapeDtypeStruct(dims, kind)

    halves = [(half, 3 * half), (half, half), (half, wide), (wide, half)]
    shards = [(dims[0] // mesh_count, dims[1]) for dims in halves]
    outs = [shape(LAYERS, *dims) for dims in shards]
    outs += [shape(rows, D), shape(*spot_shape)]
    dma = pltpu.SemaphoreType.DMA
    scratch = [
        pltpu.VMEM((D, 3 * half), bf16),
        pltpu.VMEM((half, D), bf16),
        pltpu.VMEM((D, wide), bf16),
        pltpu.VMEM((wide, D), bf16),
        pltpu.VMEM((group, wide), bf16),
        pltpu.VMEM((group, wide), bf16),
        pltpu.VMEM((group, D), bf16),
        pltpu.VMEM((2 * group, 3 * width), bf16),
        pltpu.VMEM((2 * group, width), f32),
        pltpu.VMEM((2 * group, width), bf16),
        pltpu.VMEM((group, half), bf16),
        pltpu.VMEM((rows, D), f32),
        pltpu.VMEM((rows, D), f32),
        pltpu.VMEM((rows, 128), f32),
        pltpu.VMEM((rows, D), f32),
        pltpu.VMEM((group, D), bf16),
        pltpu.VMEM((group, D), bf16),
        pltpu.VMEM((rows, D), f32),
        pltpu.VMEM((rows, D), bf16),
        pltpu.VMEM((rows, D), bf16),
        pltpu.VMEM((2 * group, width), bf16),
        pltpu.VMEM((group, width), bf16),
        pltpu.VMEM((2 * group, 3 * width), bf16),
        pltpu.VMEM((2 * group, 128), f32),
        pltpu.VMEM((2 * group, 128), f32),
        [pltpu.VMEM(dims, bf16) for dims in halves],
    ]
    scratch += [pltpu.VMEM(dims, bf16) for dims in halves]
    scratch += [pltpu.VMEM((dims[0] // 2, dims[1]), bf16) for dims in halves]
    scratch += [pltpu.VMEM((line - 1,) + dims, bf16) for dims in shards]
    scratch += [pltpu.VMEM(dims, f32) for dims in shards]
    scratch += [
        pltpu.VMEM((LAYERS, 10 * D + FF), f32),
        pltpu.VMEM((line,) + spot_shape, f32),
        pltpu.VMEM((line + 2,) + spot_shape, f32),
        pltpu.VMEM(spot_shape, f32),
        dma((LAYERS * 4 * SPLIT,)),
        dma((LAYERS * 4 * SPLIT,)),
        dma((LAYERS * 12,)),
        dma((LAYERS * 12,)),
        dma((GROUPS, line)),
        dma((GROUPS, line)),
        dma((GROUPS, line - 1)),
        dma((GROUPS, line - 1)),
        pltpu.SemaphoreType.REGULAR((KINDS,)),
        pltpu.SemaphoreType.REGULAR((KINDS,)),
        dma((KINDS,)),
        dma((line + 2,)),
        dma((line + 2,)),
        dma((18,)),
    ]
    return pl.pallas_call(
        functools.partial(backward_kernel, mesh_count, tokens),
        out_shape=outs,
        in_specs=[WHOLE] * 2 + [ANY] * 18,
        out_specs=[ANY] * 4 + [WHOLE] * 2,
        scratch_shapes=scratch,
        compiler_params=pltpu.CompilerParams(
            collective_id=1, has_side_effects=True, vmem_limit_bytes=63 << 20
        ),
        name="backward",
    )(grad, vecs, *weights, *saved)


def local(
    images,
    cotangent,
    triplet_master,
    triplet_first,
    triplet_second,
    project_master,
    project_first,
    project_second,
    expand_master,
    expand_first,
    expand_second,
    shrink_master,
    shrink_first,
    shrink_second,
    vectors_master,
    vectors_first,
    vectors_second,
):
    count = lax.axis_size("dp")
    row_at = lax.axis_index("row")
    col_at = lax.axis_index("col")
    tokens, features = images.shape
    rows = -(-tokens // (2 * TILE)) * TILE
    group = 2 * rows
    half = D // 2

    def to_tokens(values):
        padded = jnp.pad(values, ((0, 2 * rows - tokens), (0, 0))).reshape(2, rows, features)
        mine = lax.dynamic_index_in_dim(padded, col_at, 0, False)
        other = swap(lax.dynamic_index_in_dim(padded, 1 - col_at, 0, False), "col")
        return ordered(mine, other, col_at, 1)

    def to_features(values):
        split = values.reshape(rows, 2, features).transpose(1, 0, 2)
        mine = lax.dynamic_index_in_dim(split, col_at, 0, False)
        other = swap(lax.dynamic_index_in_dim(split, 1 - col_at, 0, False), "col")
        return ordered(mine, other, col_at, 0)[:tokens]

    shards = [
        triplet_master.astype(bf16).reshape(LAYERS, -1, 3 * half),
        project_master.astype(bf16),
        expand_master.astype(bf16),
        shrink_master.astype(bf16),
    ]
    piece = vectors_master.shape[1]
    line_at = (lax.axis_index("dp") % 2 * 2 + row_at) * 2 + col_at
    spot = lax.dynamic_update_slice_in_dim(
        jnp.zeros((LAYERS, 8 * piece), f32), vectors_master, line_at * piece, 1
    ).reshape(LAYERS, -1, 128)
    used = spot.shape[1]
    spot = jnp.pad(spot, ((0, 0), (0, -used % 8), (0, 0)))
    place = jnp.arange(2 * group) % rows
    late = jnp.arange(2 * group) // group
    bias = jnp.where(place + late * rows < tokens, 0.0, -1e30).astype(f32)[None]

    (w_a, w_b, w_c, w_d, vectors, *saved, block_rows) = forward_call(
        count, tokens, to_tokens(images), spot, bias, shards
    )
    block_out = to_features(block_rows)
    *grads, grad_rows, vector_sums = backward_call(
        count, tokens, to_tokens(cotangent), vectors, (w_a, w_b, w_c, w_d), saved, spot.shape
    )
    grad_out = to_features(grad_rows)
    vector_reduced = lax.dynamic_slice_in_dim(
        vector_sums[:, :used].reshape(LAYERS, -1), line_at * piece, piece, 1
    )

    outs = []
    states = (
        (triplet_master, triplet_first, triplet_second),
        (project_master, project_first, project_second),
        (expand_master, expand_first, expand_second),
        (shrink_master, shrink_first, shrink_second),
    )
    for kind, (master, first, second) in enumerate(states):
        outs += adam_step(
            master, first, second, grads[kind].reshape(master.shape), learn_rate, decay_rate
        )
    outs += adam_step(
        vectors_master, vectors_first, vectors_second, vector_reduced, vector_rate, 0.0
    )
    return (block_out, grad_out, *outs)


def solution(mesh):
    tokens = P(("dp", "row"), "col")
    triplet = P(None, ("col", "dp"), None, "row")
    narrow = P(None, ("row", "dp"), "col")
    wide = P(None, ("col", "dp"), "row")
    vector = P(None, ("dp", "row", "col"))
    states = (triplet,) * 3 + (narrow,) * 3 + (wide,) * 3 + (narrow,) * 3 + (vector,) * 3
    return jax.shard_map(
        local,
        mesh=mesh,
        in_specs=(tokens, tokens) + states,
        out_specs=(tokens, tokens) + states,
        check_vma=False,
    )
```

```python
import functools

import jax
import jax.numpy as jnp
from jax import lax
from jax.experimental import pallas as pl
from jax.experimental.pallas import tpu as pltpu
from jax.sharding import PartitionSpec as P

D = 1024
HEAD_DIM = 64
FF = 4096
LAYERS = 2
STEP = 10
TILE = 16

norm_epsilon = 1e-06
beta_first = 0.9
beta_second = 0.999
adam_epsilon = 1e-08
learn_rate = 0.02
vector_rate = 0.1
decay_rate = 0.05
bf16 = jnp.bfloat16
f32 = jnp.float32


def contract(left, right, left_dims, right_dims):
    return lax.dot_general(
        left, right, ((left_dims, right_dims), ((), ())), preferred_element_type=f32
    )


def adam_step(master, first, second, grad, rate, decay):
    first_new = beta_first * first + (1.0 - beta_first) * grad
    second_new = beta_second * second + (1.0 - beta_second) * grad * grad
    ratio = (
        first_new
        / (1.0 - beta_first**STEP)
        / (jnp.sqrt(second_new / (1.0 - beta_second**STEP)) + adam_epsilon)
    )
    return (first_new, second_new, master - rate * (ratio + decay * master))


MESH = pl.DeviceIdType.MESH
KINDS = 4
GROUPS = LAYERS * KINDS
WINDOW = 2
TRIGGER = 1.0
LEAD = 25.0
SPLIT = 2
ANY = pl.BlockSpec(memory_space=pl.ANY)
WHOLE = pl.BlockSpec(memory_space=pltpu.VMEM)


def nt(left, right):
    return contract(left, right, (1,), (1,))


def nn(left, right):
    return contract(left, right, (1,), (0,))


def tn(left, right):
    return contract(left, right, (0,), (0,))


class Place:
    def __init__(self, count):
        self.count = count
        self.line = count // 2
        self.dp = lax.axis_index("dp")
        self.row = lax.axis_index("row")
        self.col = lax.axis_index("col")
        self.pair = lax.rem(self.dp, 2)
        self.outer = lax.div(self.dp, 2)
        self.x_dp = self.dp + 1 - 2 * self.pair
        self.x_peer = (self.x_dp, self.row, self.col)
        self.y_peer = (self.dp, 1 - self.row, self.col)
        self.c_peer = (self.dp, self.row, 1 - self.col)

    def nearest(self, at):
        inside = (at + 1) // 2 if at % 2 else self.line - at // 2
        return jnp.where(
            self.outer == 0, self.line - at, jnp.where(self.outer == self.line - 1, at, inside)
        )

    def ahead(self, step):
        return lax.rem(self.dp + 2 * step, self.count)

    def behind(self, step):
        return lax.rem(self.dp + self.count - 2 * step, self.count)

    def z_peer(self, step):
        return (self.ahead(step), self.row, self.col)

    def greet(self):
        barrier = pltpu.get_barrier_semaphore()
        peers = [self.z_peer(step) for step in range(1, self.line)]
        peers += [self.x_peer, self.y_peer, self.c_peer]
        for peer in peers:
            pl.semaphore_signal(barrier, inc=1, device_id=peer, device_id_type=MESH)
        pl.semaphore_wait(barrier, len(peers))


def remote(source, target, send, recv, peer):
    return pltpu.make_async_remote_copy(
        source, target, send, recv, device_id=peer, device_id_type=MESH
    )


def aligned(value, by=128):
    return pl.multiple_of(value, by)


def weight_view(kind, ref, layer, place, dp, col):
    if kind in (0, 2):
        size = ref.shape[1] // (2 * place.count)
        return ref.at[layer, pl.ds(aligned((col * place.count + dp) * size, 16), size), :]
    size = ref.shape[1] // place.count
    return ref.at[
        layer,
        pl.ds(aligned(dp * size, 16), size),
        pl.ds(aligned(col * (D // 2)), D // 2),
    ]


def column_view(kind, ref, layer, col):
    if kind in (0, 2):
        return ref.at[layer, pl.ds(aligned(col * (D // 2), 16), D // 2), :]
    return ref.at[layer, :, pl.ds(aligned(col * (D // 2)), D // 2)]


class Gather:
    def __init__(self, place, shards, wholes, far, refs):
        self.place, self.shards, self.wholes, self.far = place, shards, wholes, far
        self.send, self.recv, self.own = refs["send"], refs["recv"], refs["own"]
        self.far_send, self.far_recv = refs["far_send"], refs["far_recv"]

    def view(self, group, dp):
        layer, kind = divmod(group, KINDS)
        return weight_view(kind, self.wholes[kind], layer, self.place, dp, self.place.col)

    def copy(self, group, at, source, target, peer):
        return remote(source, target, self.send.at[group, at], self.recv.at[group, at], peer)

    def shard(self, group):
        layer, kind = divmod(group, KINDS)
        return self.shards[kind].at[layer]

    def line_copy(self, group, step):
        place = self.place
        target = self.view(group, place.dp)
        return self.copy(group, step - 1, self.shard(group), target, place.z_peer(step))

    def pair_copy(self, group, step):
        place = self.place
        view = self.view(group, place.behind(step))
        source = self.shard(group) if isinstance(step, int) else view
        return self.copy(group, place.line - 1 + step, source, view, place.x_peer)

    def core_copy(self, group, step, pair):
        place = self.place
        dp = lax.rem(place.x_dp + place.count - 2 * step, place.count) if pair else place.behind(step)
        view = self.view(group, dp)
        source = view if pair or not isinstance(step, int) else self.shard(group)
        at = 2 * place.line - 1 + pair * place.line + step
        return self.copy(group, at, source, view, place.c_peer)

    def own_copy(self, group):
        return pltpu.make_async_copy(
            self.shard(group), self.view(group, self.place.dp), self.own.at[group]
        )

    def line_out(self, group):
        for at in range(1, self.place.line):
            self.line_copy(group, at).start()

    def own_out(self, group):
        self.pair_copy(group, 0).start()
        self.core_copy(group, 0, 0).start()
        self.own_copy(group).start()

    def line_in(self, group, at):
        step = self.place.nearest(at)
        self.line_copy(group, step).wait_recv()
        self.pair_copy(group, step).start()
        self.core_copy(group, step, 0).start()

    def pair_in(self, group, at):
        step = self.place.nearest(at) if at else 0
        self.pair_copy(group, step).wait_recv()
        self.core_copy(group, step, 1).start()

    def arrive(self, group):
        self.own_copy(group).wait()
        for pair in range(2):
            for step in range(self.place.line):
                self.core_copy(group, step, pair).wait_recv()

    def far_copy(self, layer):
        place = self.place
        return remote(
            column_view(1, self.wholes[1], layer, place.col),
            column_view(1, self.far, layer, place.col),
            self.far_send.at[layer, 0],
            self.far_recv.at[layer, 0],
            place.y_peer,
        )

    def far_core_copy(self, layer):
        view = column_view(1, self.far, layer, self.place.col)
        return remote(
            view, view, self.far_send.at[layer, 1], self.far_recv.at[layer, 1], self.place.c_peer
        )

    def far_start(self, layer):
        self.own_copy(layer * KINDS + 1).wait()
        self.far_copy(layer).start()

    def far_in(self, layer):
        self.far_copy(layer).wait_recv()
        self.far_core_copy(layer).start()

    def far_arrive(self, layer):
        self.far_core_copy(layer).wait_recv()

    def finish(self):
        for group in range(GROUPS):
            for step in range(self.place.line):
                if step:
                    self.line_copy(group, step).wait_send()
                self.pair_copy(group, step).wait_send()
                self.core_copy(group, step, 0).wait_send()
                self.core_copy(group, step, 1).wait_send()
        for layer in range(LAYERS):
            self.far_copy(layer).wait_send()
            self.far_core_copy(layer).wait_send()


class Vectors:
    def __init__(self, place, spot, raw, spare, send, recv):
        self.place, self.spot, self.raw, self.spare = place, spot, raw, spare
        self.send, self.recv = send, recv

    def line_copy(self, step):
        place = self.place
        return remote(
            self.spot,
            self.raw.at[place.outer],
            self.send.at[2 + step],
            self.recv.at[2 + step],
            place.z_peer(step),
        )

    def start(self):
        for step in range(1, self.place.line):
            self.line_copy(step).start()
        self.raw[self.place.outer] = self.spot[...]

    def line_in(self):
        for step in range(1, self.place.line):
            self.line_copy(step).wait()

    def add(self, at, peer):
        copy = remote(self.raw, self.spare.at[at], self.send.at[at], self.recv.at[at], peer)
        copy.start()
        copy.wait()
        self.raw[...] = self.raw[...] + self.spare[at]

    def spread(self, vecs):
        size = self.spot.shape[1]
        for outer in range(self.place.line):
            vecs[:, outer * size : (outer + 1) * size] = self.raw[outer]


def to_tokens(place, values, padded, arrived, target, send, recv):
    rows = arrived.shape[0]
    tokens, half = values.shape
    padded[rows:, :] = jnp.zeros_like(padded[rows:, :])
    padded[:tokens, :] = values[...]
    copy = remote(
        padded.at[pl.ds(aligned((1 - place.col) * rows, 16), rows), :],
        arrived,
        send,
        recv,
        place.c_peer,
    )
    copy.start()
    own = padded[pl.ds(aligned(place.col * rows, 16), rows), :]
    target[:, pl.ds(aligned(place.col * half), half)] = own.astype(target.dtype)
    copy.wait()
    other = pl.ds(aligned((1 - place.col) * half), half)
    target[:, other] = arrived[...].astype(target.dtype)


def to_features(place, values, arrived, target, send, recv):
    rows = values.shape[0]
    tokens, half = target.shape
    copy = remote(
        values.at[:, pl.ds(aligned((1 - place.col) * half), half)], arrived, send, recv, place.c_peer
    )
    copy.start()
    own = values[:, pl.ds(aligned(place.col * half), half)]
    copy.wait()
    other = arrived[...]

    @pl.when(place.col == 0)
    def _():
        target[:rows, :] = own
        target[rows:, :] = other[: tokens - rows]

    @pl.when(place.col == 1)
    def _():
        target[:rows, :] = other
        target[rows:, :] = own[: tokens - rows]


def norm_rows(source, gain, shift, unit, inverse, target, start, rows):
    size = 16

    def step(at, carry):
        place = pl.ds(aligned(start + at * size, size), size)
        values = source[place, :].astype(f32)
        centre = jnp.sum(values, 1, keepdims=True) * (1.0 / D)
        spread = jnp.sum(values * values, 1, keepdims=True) * (1.0 / D) - centre * centre
        scale = lax.rsqrt(spread + norm_epsilon)
        norm = (values - centre) * scale
        unit[place, :] = norm
        inverse[place, :] = jnp.broadcast_to(scale, (size, 128))
        target[place, :] = (norm * gain + shift).astype(bf16)
        return carry

    lax.fori_loop(0, rows // size, step, 0)


def gelu_both(values):
    normal = 0.5 + 0.5 * lax.erf(values * (0.5**0.5))
    density = jnp.exp(-0.5 * values * values) * 0.3989422804014327
    return values * normal, normal + values * density


def forward_kernel(count, *refs):
    (
        images,
        cotangent,
        spot_in,
        bias_in,
        shard_a,
        shard_b,
        shard_c,
        shard_d,
        w_a,
        w_b,
        w_c,
        w_d,
        w_far,
        vecs_out,
        unit_one_out,
        inv_one_out,
        normed_out,
        heads_out,
        lse_out,
        mixed_out,
        branch_out,
        unit_two_out,
        inv_two_out,
        normed_two_out,
        active_out,
        slope_out,
        output_out,
        head_mix_out,
        back_out_out,
        cotangent_out,
        block_out,
        state,
        padded,
        arrived,
        spot,
        spare,
        raw,
        vecs,
        wq,
        wm,
        wu,
        wd,
        wf,
        unit,
        inverse,
        unit_two,
        inverse_two,
        normed,
        normed_two,
        heads_all,
        head_tx,
        head_mix,
        lse,
        mixed_all,
        mixed_far,
        back_out,
        branch,
        output,
        active,
        slope,
        tx,
        rx,
        part,
        g_send,
        g_recv,
        g_own,
        far_send,
        far_recv,
        v_send,
        v_recv,
        y_send,
        y_recv,
        c_send,
        c_recv,
        stage_sem,
        save_sem,
    ) = refs
    tokens = images.shape[0]
    rows = state.shape[0]
    group = 2 * rows
    half = D // 2
    width = half // 2
    place = Place(count)
    row, col = place.row, place.col
    wholes = (w_a, w_b, w_c, w_d)
    gather = Gather(
        place,
        (shard_a, shard_b, shard_c, shard_d),
        wholes,
        w_far,
        {
            "send": g_send,
            "recv": g_recv,
            "own": g_own,
            "far_send": far_send,
            "far_recv": far_recv,
        },
    )
    place.greet()
    spot[...] = spot_in[...]
    vectors = Vectors(place, spot, raw, spare, v_send, v_recv)
    vectors.start()
    for at in range(WINDOW):
        gather.line_out(at)

    plan = []
    due = [4.0]
    for at in range(GROUPS):
        dims = wholes[at % KINDS].shape
        due.append(due[-1] + 1.1 * (dims[1] * dims[2] / 92e3))
    for at in range(GROUPS):
        begin, span = due[at], due[at + 1] - due[at]
        for step in range(1, place.line):
            line_due = begin + span * (0.3 + 0.7 * step / (place.line - 1))
            plan.append((line_due, 1, gather.line_in, (at, step)))
            if 0 < at < GROUPS - 1 and step == 1:
                plan.append((line_due, 0.5, gather.own_out, (at + 1,)))
            if at + WINDOW < GROUPS and step == max(1, round(TRIGGER * (place.line - 1))):
                plan.append((line_due, 1.5, gather.line_out, (at + WINDOW,)))
        for step in range(place.line):
            pair_due = begin + span * (0.6 + 0.7 * step / (place.line - 1)) + 2.0
            plan.append((pair_due, 2, gather.pair_in, (at, step)))
    plan.sort(key=lambda item: item[:2])
    last_of = [
        max(
            spot
            for spot, item in enumerate(plan)
            if item[2] == gather.pair_in and item[3] == (at, place.line - 1)
        )
        for at in range(GROUPS)
    ]
    plan_at = [0]

    def advance(until):
        for item in plan[plan_at[0] : until]:
            item[2](*item[3])
        plan_at[0] = max(until, plan_at[0])

    def pump(time):
        advance(sum(1 for item in plan if item[0] <= time + LEAD))

    def ensure(at):
        advance(last_of[at] + 1)

    def pump_step(at, count_steps, begin, step_time):
        for step in range(count_steps):
            until = sum(1 for item in plan if item[0] <= begin + (step + 1) * step_time + LEAD)
            if until > plan_at[0]:
                pl.when(at == step)(functools.partial(advance, until))

    pending = {}

    def settle(*names):
        for name in names:
            if name in pending:
                pending.pop(name).wait()

    def save(name, at, source, target):
        settle(name)
        copy = pltpu.make_async_copy(source, target, save_sem.at[at])
        copy.start()
        pending[name] = copy

    staged = {}
    buffers = (wq, wm, wu, wd)

    def stage(kind, layer):
        at = layer * KINDS + kind
        if kind == 1:
            for pair in range(2):
                for step in range(place.line):
                    gather.core_copy(at, step, pair).wait_recv()
        else:
            gather.arrive(at)
        copy = pltpu.make_async_copy(wholes[kind].at[layer], buffers[kind], stage_sem.at[kind])
        copy.start()
        staged[kind] = copy

    def stage_far(layer):
        gather.far_arrive(layer)
        copy = pltpu.make_async_copy(w_far.at[layer], wf, stage_sem.at[KINDS])
        copy.start()
        staged[KINDS] = copy

    def ready(kind):
        staged.pop(kind).wait()

    y_at = [0]

    def y_copy(source, target):
        at = y_at[0]
        y_at[0] += 1
        copy = remote(source, target, y_send.at[at], y_recv.at[at], place.y_peer)
        copy.start()
        return copy

    c_at = [0]

    def c_copy(source, target):
        at = c_at[0]
        c_at[0] += 1
        copy = remote(source, target, c_send.at[at], c_recv.at[at], place.c_peer)
        copy.start()
        return copy

    chunk = rows // SPLIT

    def send_rows(buffer, at):
        return y_copy(
            buffer.at[pl.ds(at * chunk, chunk), :],
            buffer.at[pl.ds(rows + at * chunk, chunk), :],
        )

    to_tokens(place, images, padded, arrived, state, c_send.at[0], c_recv.at[0])
    c_at[0] = 2
    vectors.line_in()
    vectors.add(0, place.x_peer)
    gather.own_out(0)
    gather.own_out(1)
    vectors.add(1, place.y_peer)
    vectors.add(2, place.c_peer)
    vectors.spread(vecs)
    save("vecs", 11, vecs, vecs_out)

    lane = lax.broadcasted_iota(jnp.int32, (1, 128), 1) < HEAD_DIM
    valid = lax.broadcasted_iota(jnp.int32, (rows, 1), 0) < tokens - col * rows

    def vector(layer, at):
        return vecs[layer : layer + 1, at * D : (at + 1) * D]

    def norm_one(layer, at):
        norm_rows(
            state, vector(layer, 0), vector(layer, 1), unit, inverse, normed, at * chunk, chunk
        )
        return send_rows(normed, at)

    copies = [norm_one(0, at) for at in range(SPLIT)]
    to_tokens(place, cotangent, padded, arrived, branch, c_send.at[1], c_recv.at[1])
    cotangent_out[...] = branch[...].astype(bf16)
    back_out[:rows, :] = (vector(LAYERS - 1, 13) * branch[...]).astype(bf16)
    out_copies = [send_rows(back_out, at) for at in range(SPLIT)]
    for layer in range(LAYERS):
        first = layer == 0
        heads, mixed = heads_all.at[layer], mixed_all.at[layer]
        save("unit", 0, unit, unit_one_out.at[layer])
        save("inverse", 1, inverse, inv_one_out.at[layer])
        if first:
            ensure(0)
            stage(0, 0)
        ready(0)

        def triple(start, size):
            def step(at, carry):
                part_at = lax.rem(at, 3)
                mine = lax.div(at, 3)
                owner = jnp.where(mine == 1, col, 1 - col)
                column = aligned(part_at * half + owner * width)
                value = nn(normed[start : start + size, :], wq[:, pl.ds(column, width)])
                bias_at = aligned(
                    jnp.where(part_at == 2, 3 * D, 2 * D) + row * half + owner * width
                )
                bias = vecs[layer : layer + 1, pl.ds(bias_at, width)]
                bias = bias * jnp.where(part_at == 1, 0.0, 1.0)
                inside = valid[start % rows : start % rows + size]
                value = jnp.where(inside, value + bias, 0.0).astype(bf16)
                lanes = pl.ds(aligned(part_at * width), width)

                @pl.when(mine == 0)
                def _():
                    head_tx[start : start + size, lanes] = value

                @pl.when(mine == 1)
                def _():
                    heads[pl.ds(aligned(col * group + start, 16), size), lanes] = value

                return carry

            lax.fori_loop(0, 6, step, 0)
            return c_copy(
                head_tx.at[pl.ds(start, size), :],
                heads.at[pl.ds(aligned(col * group + start, 16), size), :],
            )

        core_copies = [triple(0, rows)]
        if first:
            ensure(1)
            gather.far_start(0)
            for copy in copies:
                copy.wait()
            core_copies.append(triple(rows, rows))
            pump(33)
        else:
            ensure(5)
            gather.far_start(1)
            stage(1, 1)
            pump(106)
            copies[0].wait()
            core_copies.append(triple(rows, chunk))
            pump(111)
            copies[1].wait()
            core_copies.append(triple(rows + chunk, chunk))
            pump(119)
        save("normed", 2, normed, normed_out.at[layer])
        for copy in core_copies:
            copy.wait()
        save("heads", 3, heads, heads_out.at[layer])
        settle("lse", "head_mix")

        attend_at = [35.0 if first else 121.0]

        def attend(owner, side):
            begin_time = attend_at[0]
            attend_at[0] += 3.4
            tile = rows // 2
            begin = owner * group + side * rows

            def step(at, carry):
                place_rows = pl.ds(aligned(begin + at * tile, 16), tile)
                for pair in range(width // 128):
                    lanes = slice(pair * 128, pair * 128 + 128)
                    query = heads[place_rows, lanes] * jnp.asarray(HEAD_DIM**-0.5, bf16)
                    zero = jnp.zeros_like(query)
                    both = jnp.concatenate(
                        [jnp.where(lane, query, zero), jnp.where(lane, zero, query)], 0
                    )
                    key = heads[:, width + pair * 128 : width + pair * 128 + 128]
                    value = heads[:, 2 * width + pair * 128 : 2 * width + pair * 128 + 128]
                    scores = nt(both, key) + bias_in[...]
                    peak = jnp.max(scores, 1, keepdims=True)
                    weights = jnp.exp(scores - peak)
                    total = jnp.sum(weights, 1, keepdims=True)
                    result = nn(weights.astype(bf16), value) / total
                    logsum = peak + jnp.log(total)
                    head_mix[place_rows, lanes] = jnp.where(
                        lane, result[:tile], result[tile:]
                    ).astype(bf16)
                    lse[place_rows, lanes] = jnp.where(lane, logsum[:tile], logsum[tile:])
                pump_step(at, rows // tile, begin_time, 1.7)
                return carry

            lax.fori_loop(0, rows // tile, step, 0)
            plan_at[0] = max(plan_at[0], sum(1 for item in plan if item[0] <= attend_at[0] + LEAD))

        my_lanes = pl.ds(aligned(col * width), width)

        def send_mixed(side):
            return c_copy(
                head_mix.at[pl.ds(aligned((1 - col) * group + side * rows, 16), rows), :],
                mixed.at[pl.ds(side * rows, rows), my_lanes],
            )

        def keep_mixed(side):
            mixed[side * rows : side * rows + rows, my_lanes] = head_mix[
                pl.ds(aligned(col * group + side * rows, 16), rows), :
            ]

        attend(1 - col, 1)
        copy = send_mixed(1)
        attend(col, 1)
        keep_mixed(1)
        copy.wait()
        settle("normed_two")
        far_copy = y_copy(mixed.at[pl.ds(rows, rows), :], mixed_far)
        if first:
            stage(1, 0)
        attend(1 - col, 0)
        copy = send_mixed(0)
        gather.far_in(layer)
        attend(col, 0)
        keep_mixed(0)
        copy.wait()
        save("lse", 4, lse, lse_out.at[layer])
        save("head_mix", 14, head_mix, head_mix_out.at[layer])
        save("mixed", 5, mixed, mixed_out.at[layer])
        stage_far(layer)
        ready(1)
        settle("branch", "unit_two", "inverse_two")

        def project(start):
            def step(at, carry):
                lanes = pl.ds(aligned(at * half), half)
                value = nn(mixed[start : start + chunk, :], wm[:, lanes])
                value = value + nn(mixed_far[start : start + chunk, :], wf[:, lanes])
                bias_at = aligned(4 * D + at * half)
                value = value + vecs[layer : layer + 1, pl.ds(bias_at, half)]
                scale = vecs[layer : layer + 1, pl.ds(aligned(5 * D + at * half), half)]
                branch[start : start + chunk, lanes] = value
                state[start : start + chunk, lanes] += scale * value
                return carry

            lax.fori_loop(0, 2, step, 0)

        far_copy.wait()
        ready(KINDS)
        copies = []
        for at in range(SPLIT):
            project(at * chunk)
            norm_rows(
                state,
                vector(layer, 6),
                vector(layer, 7),
                unit_two,
                inverse_two,
                normed_two,
                at * chunk,
                chunk,
            )
            copies.append(send_rows(normed_two, at))
            pump((50 if first else 137) + at * 1.5)
        ensure(2 if first else 6)
        stage(2, layer)
        save("branch", 6, branch, branch_out.at[layer])
        save("unit_two", 7, unit_two, unit_two_out.at[layer])
        save("inverse_two", 8, inverse_two, inv_two_out.at[layer])
        ready(2)
        settle("active", "slope", "normed")

        def expand(start, size, begin_time):
            def step(at, carry):
                lanes = pl.ds(aligned(at * half), half)
                bias_at = aligned(8 * D + row * (FF // 2) + at * half)
                value = nn(normed_two[start : start + size, :], wu[:, lanes])
                value = value + vecs[layer : layer + 1, pl.ds(bias_at, half)]
                act, grad = gelu_both(value)
                active[start : start + size, lanes] = act.astype(bf16)
                slope[start : start + size, lanes] = grad.astype(bf16)
                pump_step(at, FF // 2 // half, begin_time, 0.8)
                return carry

            lax.fori_loop(0, FF // 2 // half, step, 0)
            end = begin_time + FF // 2 // half * 0.8 + LEAD
            plan_at[0] = max(plan_at[0], sum(1 for item in plan if item[0] <= end))

        def shrink(start, size, target, target_at):
            def step(at, carry):
                lanes = pl.ds(aligned(at * half), half)
                value = nn(active[start : start + size, :], wd[:, lanes])
                target[pl.ds(target_at, size), lanes] = value.astype(target.dtype)
                return carry

            lax.fori_loop(0, 2, step, 0)

        def shrink_send(at):
            shrink(rows + at * chunk, chunk, tx, at * chunk)
            view = pl.ds(at * chunk, chunk)
            return y_copy(tx.at[view, :], rx.at[view, :])

        back_copies = []
        if first:
            expand(0, rows, 56.0)
            copies[0].wait()
            expand(rows, chunk, 63.0)
            copies[1].wait()
            expand(rows + chunk, chunk, 71.0)
            ensure(3)
            stage(3, 0)
            ready(3)
            back_copies.append(shrink_send(0))
            back_copies.append(shrink_send(1))
        else:
            expand(0, rows, 139.0)
            copies[0].wait()
            expand(rows, chunk, 146.0)
            ensure(7)
            stage(3, 1)
            ready(3)
            back_copies.append(shrink_send(0))
            copies[1].wait()
            expand(rows + chunk, chunk, 160.0)
            back_copies.append(shrink_send(1))
        shrink(0, rows, part, 0)
        save("normed_two", 9, normed_two, normed_two_out.at[layer])
        save("active", 10, active, active_out.at[layer])
        save("slope", 12, slope, slope_out.at[layer])
        if first:
            pump(87)
        else:
            for copy in out_copies:
                copy.wait()
            save("back_out", 15, back_out, back_out_out)
        settle("output", "unit", "inverse")
        next_copies = []
        for at in range(SPLIT):
            back_copies[at].wait()
            here = slice(at * chunk, at * chunk + chunk)
            output[here, :] = part[here, :] + rx[here, :].astype(f32) + vector(layer, 12)
            state[here, :] = state[here, :] + vector(layer, 13) * output[here, :]
            if first:
                next_copies.append(norm_one(1, at))
                if at == 0:
                    pump(94)
        save("output", 13, output, output_out.at[layer])
        if first:
            ensure(4)
            stage(0, 1)
        copies = next_copies
    tx[...] = state[...].astype(bf16)
    to_features(place, tx, arrived, block_out, c_send.at[15], c_recv.at[15])
    gather.finish()
    settle(*list(pending))


def padded_rows(tokens):
    return -(-tokens // (2 * TILE)) * TILE


def forward_call(mesh_count, images, cotangent, spot, bias, shards):
    tokens = images.shape[0]
    rows = padded_rows(tokens)
    group = 2 * rows
    half = D // 2
    width = half // 2
    line = mesh_count // 2

    def shape(*dims, kind=f32):
        return jax.ShapeDtypeStruct(dims, kind)

    outs = [
        shape(LAYERS, D, 3 * half, kind=bf16),
        shape(LAYERS, half, D, kind=bf16),
        shape(LAYERS, D, FF // 2, kind=bf16),
        shape(LAYERS, FF // 2, D, kind=bf16),
        shape(LAYERS, half, D, kind=bf16),
        shape(LAYERS, 10 * D + FF),
        shape(LAYERS, rows, D),
        shape(LAYERS, rows, 128),
        shape(LAYERS, group, D, kind=bf16),
        shape(LAYERS, 2 * group, 3 * width, kind=bf16),
        shape(LAYERS, 2 * group, width),
        shape(LAYERS, group, half, kind=bf16),
        shape(LAYERS, rows, D),
        shape(LAYERS, rows, D),
        shape(LAYERS, rows, 128),
        shape(LAYERS, group, D, kind=bf16),
        shape(LAYERS, group, FF // 2, kind=bf16),
        shape(LAYERS, group, FF // 2, kind=bf16),
        shape(LAYERS, rows, D),
        shape(LAYERS, 2 * group, width, kind=bf16),
        shape(group, D, kind=bf16),
        shape(rows, D, kind=bf16),
        shape(tokens, half, kind=bf16),
    ]
    dma = pltpu.SemaphoreType.DMA
    scratch = [
        pltpu.VMEM((rows, D), f32),
        pltpu.VMEM((group, half), bf16),
        pltpu.VMEM((rows, half), bf16),
        pltpu.VMEM(spot.shape, f32),
        pltpu.VMEM((3, line) + spot.shape, f32),
        pltpu.VMEM((line,) + spot.shape, f32),
        pltpu.VMEM((LAYERS, 10 * D + FF), f32),
        pltpu.VMEM((D, 3 * half), bf16),
        pltpu.VMEM((half, D), bf16),
        pltpu.VMEM((D, FF // 2), bf16),
        pltpu.VMEM((FF // 2, D), bf16),
        pltpu.VMEM((half, D), bf16),
        pltpu.VMEM((rows, D), f32),
        pltpu.VMEM((rows, 128), f32),
        pltpu.VMEM((rows, D), f32),
        pltpu.VMEM((rows, 128), f32),
        pltpu.VMEM((group, D), bf16),
        pltpu.VMEM((group, D), bf16),
        pltpu.VMEM((LAYERS, 2 * group, 3 * width), bf16),
        pltpu.VMEM((group, 3 * width), bf16),
        pltpu.VMEM((2 * group, width), bf16),
        pltpu.VMEM((2 * group, width), f32),
        pltpu.VMEM((LAYERS, group, half), bf16),
        pltpu.VMEM((rows, half), bf16),
        pltpu.VMEM((group, D), bf16),
        pltpu.VMEM((rows, D), f32),
        pltpu.VMEM((rows, D), f32),
        pltpu.VMEM((group, FF // 2), bf16),
        pltpu.VMEM((group, FF // 2), bf16),
        pltpu.VMEM((rows, D), bf16),
        pltpu.VMEM((rows, D), bf16),
        pltpu.VMEM((rows, D), f32),
        dma((GROUPS, 4 * line - 1)),
        dma((GROUPS, 4 * line - 1)),
        dma((GROUPS,)),
        dma((LAYERS, 2)),
        dma((LAYERS, 2)),
        dma((line + 2,)),
        dma((line + 2,)),
        dma((16,)),
        dma((16,)),
        dma((16,)),
        dma((16,)),
        dma((KINDS + 1,)),
        dma((16,)),
    ]
    return pl.pallas_call(
        functools.partial(forward_kernel, mesh_count),
        out_shape=outs,
        in_specs=[WHOLE] * 8,
        out_specs=[ANY] * 21 + [WHOLE] * 2,
        scratch_shapes=scratch,
        compiler_params=pltpu.CompilerParams(
            collective_id=0, has_side_effects=True, vmem_limit_bytes=60 << 20
        ),
        name="forward",
    )(images, cotangent, spot, bias, *shards)


def fold(values):
    return jnp.sum(values.reshape(-1, 8, values.shape[-1]), 0)


def total(values):
    return jnp.sum(values, 0, keepdims=True)


def flip(picks, values):
    high = values.astype(bf16)
    rest = values - high.astype(f32)
    middle = rest.astype(bf16)
    low = (rest - middle.astype(f32)).astype(bf16)
    return nt(picks, high) + nt(picks, middle) + nt(picks, low)


class Scatter:
    def __init__(self, place, sums, pair_rx, line_rx, outs, refs):
        self.place, self.sums, self.pair_rx, self.line_rx = place, sums, pair_rx, line_rx
        self.outs, self.result = outs, refs["result"]
        self.x_send, self.x_recv = refs["x_send"], refs["x_recv"]
        self.z_send, self.z_recv = refs["z_send"], refs["z_recv"]
        self.x_free, self.z_free, self.out_sem = refs["x_free"], refs["z_free"], refs["out_sem"]
        self.writing = {}

    def size(self, kind):
        return self.sums[kind].shape[0] // self.place.count

    def block(self, kind, dp):
        size = self.size(kind)
        return pl.ds(aligned(dp * size, 16), size)

    def x_copy(self, layer, kind, outer):
        place = self.place
        size = self.size(kind)
        at = layer * KINDS + kind
        return remote(
            self.sums[kind].at[self.block(kind, 2 * outer + 1 - place.pair), :],
            self.pair_rx[kind].at[pl.ds(outer * size, size), :],
            self.x_send.at[at, outer],
            self.x_recv.at[at, outer],
            place.x_peer,
        )

    def z_copy(self, layer, kind, outer):
        place = self.place
        size = self.size(kind)
        at = layer * KINDS + kind
        step = lax.rem(outer - place.outer + place.line, place.line)
        return remote(
            self.pair_rx[kind].at[pl.ds(aligned(outer * size, 16), size), :],
            self.line_rx[kind].at[step - 1],
            self.z_send.at[at, step - 1],
            self.z_recv.at[at, step - 1],
            (2 * outer + place.pair, place.row, place.col),
        )

    def x_start(self, layer, kind):
        if layer < LAYERS - 1:
            pl.semaphore_wait(self.x_free.at[kind], 1)
        for outer in range(self.place.line):
            self.x_copy(layer, kind, outer).start()

    def x_finish(self, layer, kind):
        place = self.place
        size = self.size(kind)
        rows = min(size, 64)
        if layer < LAYERS - 1:
            pl.semaphore_wait(self.z_free.at[kind], place.line - 1)
        for outer in range(place.line):
            self.x_copy(layer, kind, outer).wait()

            def step(at, carry, outer=outer):
                here = pl.ds(aligned(outer * size + at * rows, 16), rows)
                own = pl.ds(aligned((2 * outer + place.pair) * size + at * rows, 16), rows)
                pair_rx = self.pair_rx[kind]
                value = pair_rx[here, :].astype(f32) + self.sums[kind][own, :].astype(f32)
                pair_rx[here, :] = value.astype(bf16)
                return carry

            lax.fori_loop(0, size // rows, step, 0)

            @pl.when(place.outer != outer)
            def _(outer=outer):
                self.z_copy(layer, kind, outer).start()

    def z_finish(self, layer, kind):
        place = self.place
        size = self.size(kind)
        for step_at in range(1, place.line):
            self.z_copy(layer, kind, lax.rem(place.outer + step_at, place.line)).wait()
        if kind in self.writing:
            self.writing.pop(kind).wait()
        rows = min(size, 64)

        def step(at, carry):
            here = pl.ds(aligned(at * rows, 16), rows)
            own = pl.ds(aligned(place.outer * size + at * rows, 16), rows)
            value = self.pair_rx[kind][own, :].astype(f32)
            for step_at in range(place.line - 1):
                value = value + self.line_rx[kind][step_at, here, :].astype(f32)
            if kind == 0:
                third = value.shape[1] // 3
                for part_at in range(3):
                    self.result[kind][part_at, here, :] = value[:, part_at * third : (part_at + 1) * third]
            else:
                self.result[kind][here, :] = value
            return carry

        lax.fori_loop(0, size // rows, step, 0)
        copy = pltpu.make_async_copy(
            self.result[kind], self.outs[kind].at[layer], self.out_sem.at[kind]
        )
        copy.start()
        self.writing[kind] = copy
        if layer == LAYERS - 1:
            pl.semaphore_signal(
                self.x_free.at[kind], inc=1, device_id=place.x_peer, device_id_type=MESH
            )
            for step_at in range(1, place.line):
                pl.semaphore_signal(
                    self.z_free.at[kind],
                    inc=1,
                    device_id=place.z_peer(step_at),
                    device_id_type=MESH,
                )

    def finish(self):
        for copy in self.writing.values():
            copy.wait()


def scatter_vectors(place, grads, packed, spare, spot, target, send, recv):
    size = spot.shape[1]
    for outer in range(place.line):
        packed[outer] = grads[:, outer * size : (outer + 1) * size]
    copies = []
    for step in range(1, place.line):
        outer = lax.rem(place.outer + step, place.line)
        copy = remote(
            packed.at[outer], spare.at[2 + step], send.at[2 + step], recv.at[2 + step], place.z_peer(step)
        )
        copy.start()
        copies.append(copy)
    for copy in copies:
        copy.wait()
    value = packed[place.outer]
    for step in range(1, place.line):
        value = value + spare[2 + step]
    spot[...] = value
    for at, peer in enumerate((place.x_peer, place.y_peer, place.c_peer)):
        copy = remote(spot, spare.at[at], send.at[at], recv.at[at], peer)
        copy.start()
        copy.wait()
        spot[...] = spot[...] + spare[at]
    target[...] = spot[...]


def backward_kernel(count, *refs):
    (
        grad_in,
        vecs,
        w_a,
        w_b,
        w_c,
        w_d,
        unit_one_in,
        inv_one_in,
        normed_in,
        heads_in,
        lse_in,
        mixed_in,
        branch_in,
        unit_two_in,
        inv_two_in,
        normed_two_in,
        active_in,
        slope_in,
        output_in,
        head_mix_in,
        back_out_in,
        grad_a,
        grad_b,
        grad_c,
        grad_d,
        grad_out,
        vec_out,
        wq,
        wm,
        wu,
        wd,
        active,
        slope,
        feed,
        heads,
        lse,
        head_mix,
        mixed,
        aside,
        unit,
        inverse,
        grad,
        back_out,
        back_branch,
        part,
        tx,
        rx,
        head_back,
        head_tx,
        head_grad,
        key_sum,
        value_sum,
        half_tx,
        sum_a,
        sum_b,
        sum_c,
        sum_d,
        pair_a,
        pair_b,
        pair_c,
        pair_d,
        line_a,
        line_b,
        line_c,
        line_d,
        result_a,
        result_b,
        result_c,
        result_d,
        vec_grads,
        packed,
        spare,
        spot,
        y_send,
        y_recv,
        c_send,
        c_recv,
        x_send,
        x_recv,
        z_send,
        z_recv,
        x_free,
        z_free,
        out_sem,
        v_send,
        v_recv,
        load_sem,
    ) = refs
    tokens = grad_out.shape[0]
    rows = grad_in.shape[0]
    group = 2 * rows
    half = D // 2
    width = half // 2
    pairs = width // 128
    place = Place(count)
    row, col = place.row, place.col
    sums = (sum_a, sum_b, sum_c, sum_d)
    place.greet()
    scatter = Scatter(
        place,
        sums,
        (pair_a, pair_b, pair_c, pair_d),
        (line_a, line_b, line_c, line_d),
        (grad_a, grad_b, grad_c, grad_d),
        {
            "result": (result_a, result_b, result_c, result_d),
            "x_send": x_send,
            "x_recv": x_recv,
            "z_send": z_send,
            "z_recv": z_recv,
            "x_free": x_free,
            "z_free": z_free,
            "out_sem": out_sem,
        },
    )
    triple_back = active

    sources = {
        "wd": (w_d, wd),
        "wu": (w_c, wu),
        "wm": (w_b, wm),
        "wq": (w_a, wq),
        "slope": (slope_in, slope),
        "active": (active_in, active),
        "normed_two": (normed_two_in, feed),
        "normed": (normed_in, feed),
        "output": (output_in, aside),
        "branch": (branch_in, aside),
        "unit_two": (unit_two_in, unit),
        "unit_one": (unit_one_in, unit),
        "inv_two": (inv_two_in, inverse),
        "inv_one": (inv_one_in, inverse),
        "heads": (heads_in, heads),
        "lse": (lse_in, lse),
        "head_mix": (head_mix_in, head_mix),
        "mixed": (mixed_in, mixed),
        "back_out": (back_out_in, back_out),
    }
    names = list(sources)
    loading = {}

    def load(layer, *wanted):
        for name in wanted:
            source, buffer = sources[name]
            if name != "back_out":
                source = source.at[layer]
            copy = pltpu.make_async_copy(source, buffer, load_sem.at[names.index(name)])
            copy.start()
            loading[name] = copy

    def loaded(*wanted):
        for name in wanted:
            loading.pop(name).wait()

    y_at = [0]

    def y_copy(source, target):
        at = y_at[0]
        y_at[0] += 1
        copy = remote(source, target, y_send.at[at], y_recv.at[at], place.y_peer)
        copy.start()
        return copy

    c_at = [0]

    def c_copy(source, target):
        at = c_at[0]
        c_at[0] += 1
        return remote(source, target, c_send.at[at], c_recv.at[at], place.c_peer)

    chunk = rows // SPLIT

    def send_rows(buffer, at):
        return y_copy(
            buffer.at[pl.ds(at * chunk, chunk), :],
            buffer.at[pl.ds(rows + at * chunk, chunk), :],
        )

    def send_part(at):
        view = pl.ds(at * chunk, chunk)
        return y_copy(tx.at[view, :], rx.at[view, :])

    load(1, "back_out", "wd", "slope", "wu", "output", "active", "normed_two", "unit_two", "inv_two")
    load(1, "wm", "mixed", "heads", "lse", "head_mix", "wq")
    grad[...] = grad_in[...].astype(f32)
    vec_grads[...] = jnp.zeros_like(vec_grads)
    lane = lax.broadcasted_iota(jnp.int32, (1, 128), 1) < HEAD_DIM
    pick_row = lax.broadcasted_iota(jnp.int32, (8, 128), 0)
    pick_lane = lax.broadcasted_iota(jnp.int32, (8, 128), 1)
    halves = (
        ((pick_row == 0) & (pick_lane < HEAD_DIM)) | ((pick_row == 1) & (pick_lane >= HEAD_DIM))
    ).astype(bf16)
    firsts = (pick_lane == pick_row * HEAD_DIM).astype(bf16)
    size = 16

    def vector(layer, at):
        return vecs[layer : layer + 1, at * D : (at + 1) * D]

    def note(layer, at, value):
        vec_grads[layer : layer + 1, at * D : (at + 1) * D] += value

    def by_rows(start, count_rows, body, terms):
        def step(at, carry):
            adds = body(pl.ds(aligned(start + at * size, size), size))
            return tuple(old + fold(new) for old, new in zip(carry, adds, strict=True))

        zeros = tuple(jnp.zeros((8, D), f32) for _ in range(terms))
        sums_ = lax.fori_loop(0, count_rows // size, step, zeros)
        return [total(value) for value in sums_]

    def half_tiles(kind):
        return {0: 3, 1: 1, 2: FF // 2 // half, 3: FF // 2 // half}[kind]

    def weight_grad(kind, owner, at):
        owned = pl.ds(aligned(owner * half), half)
        tile = pl.ds(aligned(at * half), half)
        if kind == 0:
            return tn(feed[:, owned], triple_back[:, tile])
        if kind == 1:
            return tn(mixed[...], back_branch[:, owned])
        if kind == 2:
            return tn(feed[:, owned], slope[:, tile])
        return tn(active[:, tile], back_out[:, owned])

    def spot_of(kind, at):
        tile = pl.ds(aligned(at * half), half)
        return (tile, slice(None)) if kind == 3 else (slice(None), tile)

    half_copies = {}

    def produce_other(layer, kind):
        target = sums[kind]
        buffer = half_tx[kind]

        def step(at, carry):
            buffer[spot_of(kind, at)] = weight_grad(kind, 1 - col, at).astype(bf16)
            return carry

        lax.fori_loop(0, half_tiles(kind), step, 0)
        copy = c_copy(buffer, target)
        copy.start()
        half_copies[kind] = copy

    def produce_own(layer, kind):
        target = sums[kind]
        half_copies.pop(kind).wait()

        def step(at, carry):
            here = spot_of(kind, at)
            value = weight_grad(kind, col, at) + target[here].astype(f32)
            target[here] = value.astype(bf16)
            return carry

        lax.fori_loop(0, half_tiles(kind), step, 0)
        scatter.x_start(layer, kind)

    def out_rows(layer, start, count_rows):
        def body(here):
            value = grad[here, :]
            back = (vector(layer, 13) * value).astype(bf16)
            if layer < LAYERS - 1:
                back_out[here, :] = back
            return (value * aside[here, :], back.astype(f32))

        for at, value in zip((13, 12), by_rows(start, count_rows, body, 2), strict=True):
            note(layer, at, value)

    for layer in reversed(range(LAYERS)):
        last = layer == LAYERS - 1
        if last:
            loaded("back_out")
        else:
            load(0, "branch")
            scatter.z_finish(1, 3)
            scatter.z_finish(1, 2)
        loaded("slope", "wd")

        def inner_rows(start, count_rows):
            def step(at, carry):
                lanes = pl.ds(aligned(at * half), half)
                value = nt(back_out[start : start + count_rows, :], wd[lanes, :])
                back = (value * slope[start : start + count_rows, lanes].astype(f32)).astype(bf16)
                slope[start : start + count_rows, lanes] = back
                there = pl.ds(aligned(8 * D + row * (FF // 2) + at * half), half)
                old = vec_grads[layer : layer + 1, there]
                vec_grads[layer : layer + 1, there] = old + total(back.astype(f32))
                return carry

            lax.fori_loop(0, FF // 2 // half, step, 0)

        def two_rows(start, count_rows, target, target_at):
            def step(at, carry):
                lanes = pl.ds(aligned(at * half), half)
                value = nt(slope[start : start + count_rows, :], wu[lanes, :])
                target[pl.ds(target_at, count_rows), lanes] = value.astype(target.dtype)
                return carry

            lax.fori_loop(0, 2, step, 0)

        def back_chunk(at):
            start = rows + at * chunk
            inner_rows(start, chunk)
            two_rows(start, chunk, tx, at * chunk)
            return send_part(at)

        if last:
            loaded("wu")
            back_copies = [back_chunk(at) for at in range(SPLIT)]
            inner_rows(0, rows)
        else:
            inner_rows(0, rows)
            loaded("wu")
            scatter.x_finish(1, 1)
            back_copies = []
            for at in range(SPLIT):
                out_copies[at].wait()
                back_copies.append(back_chunk(at))
        two_rows(0, rows, part, 0)
        if last:
            load(0, "wd")
        else:
            scatter.x_finish(1, 0)
        loaded("active", "normed_two")
        produce_other(layer, 3)
        produce_other(layer, 2)
        produce_own(layer, 3)
        produce_own(layer, 2)
        load(layer, "normed")
        if last:
            loaded("output")
            out_rows(layer, 0, rows)
            load(1, "branch")
        loaded("unit_two", "inv_two", "branch")

        def middle_rows(here):
            back = part[here, :] + rx[here, :].astype(f32)
            norm = unit[here, :]
            scaled = back * vector(layer, 6)
            first = jnp.sum(scaled, 1, keepdims=True) * (1.0 / D)
            second = jnp.sum(scaled * norm, 1, keepdims=True) * (1.0 / D)
            scale = inverse[here, 0:1]
            value = grad[here, :] + scale * (scaled - first - norm * second)
            grad[here, :] = value
            branch_back = (vector(layer, 5) * value).astype(bf16)
            back_branch[here, :] = branch_back
            return (back * norm, back, value * aside[here, :], branch_back.astype(f32))

        copies = []
        for at in range(SPLIT):
            back_copies[at].wait()
            terms = by_rows(at * chunk, chunk, middle_rows, 4)
            copies.append(send_rows(back_branch, at))
            for spot_at, value in zip((6, 7, 5, 4), terms, strict=True):
                note(layer, spot_at, value)
        load(layer, "unit_one", "inv_one")
        loaded("wm")

        def mixed_rows(start, count_rows):
            for owner in range(2):
                lanes = slice(owner * width, owner * width + width)
                value = nt(back_branch[start : start + count_rows, :], wm[lanes, :]).astype(bf16)

                @pl.when(owner == col)
                def _():
                    head_back[pl.ds(aligned(col * group + start, 16), count_rows), :] = value

                @pl.when(owner != col)
                def _():
                    head_tx[start : start + count_rows, :] = value

        core_copies = []

        def send_back(start, count_rows):
            core_copies.append(
                c_copy(
                    head_tx.at[pl.ds(start, count_rows), :],
                    head_back.at[pl.ds(aligned(col * group + start, 16), count_rows), :],
                )
            )
            core_copies[-1].start()

        mixed_rows(0, rows)
        send_back(0, rows)
        for at in range(SPLIT):
            copies[at].wait()
            mixed_rows(rows + at * chunk, chunk)
            send_back(rows + at * chunk, chunk)
        loaded("heads", "lse", "head_mix", "mixed")
        if last:
            load(0, "wm")
        else:
            scatter.z_finish(1, 1)
            scatter.z_finish(1, 0)
        for copy in core_copies:
            copy.wait()

        piece = 2 * group // 4
        head_copies = []
        for pair in range(pairs):
            lanes = slice(pair * 128, pair * 128 + 128)
            key_lanes = slice(width + pair * 128, width + pair * 128 + 128)
            value_lanes = slice(2 * width + pair * 128, 2 * width + pair * 128 + 128)
            key_sum[...] = jnp.zeros_like(key_sum)
            value_sum[...] = jnp.zeros_like(value_sum)

            def step(at, carry, lanes=lanes, key_lanes=key_lanes, value_lanes=value_lanes):
                here = pl.ds(aligned(at * 128), 128)
                query = heads[here, lanes] * jnp.asarray(HEAD_DIM**-0.5, bf16)
                back = head_back[here, lanes]
                zero = jnp.zeros_like(query)
                queries = jnp.concatenate(
                    [jnp.where(lane, query, zero), jnp.where(lane, zero, query)], 0
                )
                backs = jnp.concatenate(
                    [jnp.where(lane, back, zero), jnp.where(lane, zero, back)], 0
                )
                logs = flip(firsts, lse[here, lanes])
                logs = jnp.concatenate([logs[0:1], logs[1:2]], 1)
                inner = flip(halves, back.astype(f32) * head_mix[here, lanes].astype(f32))
                inner = jnp.concatenate([inner[0:1], inner[1:2]], 1)
                query_grad = jnp.zeros((256, 128), f32)
                for block in range(4):
                    keys = slice(block * piece, block * piece + piece)
                    key = heads[keys, key_lanes]
                    scores = nt(key, queries)
                    probs = jnp.exp(jnp.minimum(scores - logs, 0.0))
                    back_probs = nt(heads[keys, value_lanes], backs)
                    back_scores = (probs * (back_probs - inner)).astype(bf16)
                    value_sum[keys, :] += nn(probs.astype(bf16), backs)
                    key_sum[keys, :] += nn(back_scores, queries)
                    query_grad = query_grad + tn(back_scores, key)
                query_grad = query_grad * HEAD_DIM**-0.5
                head_grad[here, lanes] = jnp.where(
                    lane, query_grad[:128], query_grad[128:]
                ).astype(bf16)
                return carry

            lax.fori_loop(0, 2 * group // 128, step, 0)
            for owner in range(2):
                edge = owner * rows
                valid = lax.broadcasted_iota(jnp.int32, (rows, 1), 0) < tokens - edge
                for part_at in range(2):
                    here = slice(owner * group + part_at * rows, owner * group + part_at * rows + rows)
                    head_grad[here, key_lanes] = jnp.where(valid, key_sum[here, :], 0.0).astype(bf16)
                    head_grad[here, value_lanes] = jnp.where(valid, value_sum[here, :], 0.0).astype(bf16)
            if pair == pairs - 1:
                if last:
                    scatter.x_finish(1, 2)
            else:
                scatter.x_finish(layer, 3)
            there = pl.ds(aligned((1 - col) * group, 16), group)
            mine = pl.ds(aligned(col * group, 16), group)
            for part_at, source in enumerate((lanes, key_lanes, value_lanes)):
                target = pl.ds(aligned(part_at * half + col * width + pair * 128), 128)
                copy = c_copy(head_grad.at[there, source], triple_back.at[:, target])
                copy.start()
                head_copies.append(copy)
                triple_back[:, target] = head_grad[mine, source]
                if part_at != 1:
                    bias_at = pl.ds(
                        aligned((3 * D if part_at else 2 * D) + row * half + col * width + pair * 128), 128
                    )
                    vec_grads[layer : layer + 1, bias_at] = total(head_grad[:, source].astype(f32))
        if not last:
            scatter.x_finish(0, 2)
        for copy in head_copies:
            copy.wait()
        loaded("wq", "normed")
        if not last:
            produce_other(layer, 0)

        def one_rows(start, count_rows, target, target_at):
            def step(at, carry):
                lanes = pl.ds(aligned(at * half), half)
                value = nt(triple_back[start : start + count_rows, : 3 * half], wq[lanes, :])
                target[pl.ds(target_at, count_rows), lanes] = value.astype(target.dtype)
                return carry

            lax.fori_loop(0, 2, step, 0)

        back_copies = []
        for at in range(SPLIT):
            one_rows(rows + at * chunk, chunk, tx, at * chunk)
            back_copies.append(send_part(at))
        if last:
            produce_other(layer, 1)
            produce_other(layer, 0)
            produce_own(layer, 1)
            produce_own(layer, 0)
        else:
            produce_own(layer, 0)
            produce_other(layer, 1)
            produce_own(layer, 1)
        one_rows(0, rows, part, 0)
        if last:
            load(0, "slope", "wu", "wq", "output", "normed_two", "active")
            load(0, "mixed", "heads", "lse", "head_mix")
        loaded("unit_one", "inv_one")

        def input_rows(here):
            back = part[here, :] + rx[here, :].astype(f32)
            norm = unit[here, :]
            scaled = back * vector(layer, 0)
            first = jnp.sum(scaled, 1, keepdims=True) * (1.0 / D)
            second = jnp.sum(scaled * norm, 1, keepdims=True) * (1.0 / D)
            scale = inverse[here, 0:1]
            grad[here, :] = grad[here, :] + scale * (scaled - first - norm * second)
            return (back * norm, back)

        if last:
            loaded("output")
        out_copies = []
        for at in range(SPLIT):
            back_copies[at].wait()
            terms = by_rows(at * chunk, chunk, input_rows, 2)
            if last:
                out_rows(0, at * chunk, chunk)
                out_copies.append(send_rows(back_out, at))
            for spot_at, value in zip((0, 1), terms, strict=True):
                note(layer, spot_at, value)
        if last:
            load(0, "unit_two", "inv_two")
    scatter.z_finish(0, 3)
    scatter.z_finish(0, 2)
    to_features(place, grad, aside.at[:, pl.ds(0, half)], grad_out, c_send.at[26], c_recv.at[26])
    scatter.x_finish(0, 0)
    scatter.x_finish(0, 1)
    scatter_vectors(place, vec_grads, packed, spare, spot, vec_out, v_send, v_recv)
    scatter.z_finish(0, 0)
    scatter.z_finish(0, 1)
    scatter.finish()


def backward_call(mesh_count, tokens, grad, vecs, weights, saved, spot_shape):
    rows = padded_rows(tokens)
    group = 2 * rows
    half = D // 2
    width = half // 2
    line = mesh_count // 2
    wide = FF // 2

    def shape(*dims, kind=f32):
        return jax.ShapeDtypeStruct(dims, kind)

    halves = [(half, 3 * half), (half, half), (half, wide), (wide, half)]
    shards = [(dims[0] // mesh_count, dims[1]) for dims in halves]
    results = [(3, shards[0][0], half)] + shards[1:]
    outs = [shape(LAYERS, *dims) for dims in results]
    outs += [shape(tokens, half), shape(*spot_shape)]
    dma = pltpu.SemaphoreType.DMA
    scratch = [
        pltpu.VMEM((D, 3 * half), bf16),
        pltpu.VMEM((half, D), bf16),
        pltpu.VMEM((D, wide), bf16),
        pltpu.VMEM((wide, D), bf16),
        pltpu.VMEM((group, wide), bf16),
        pltpu.VMEM((group, wide), bf16),
        pltpu.VMEM((group, D), bf16),
        pltpu.VMEM((2 * group, 3 * width), bf16),
        pltpu.VMEM((2 * group, width), f32),
        pltpu.VMEM((2 * group, width), bf16),
        pltpu.VMEM((group, half), bf16),
        pltpu.VMEM((rows, D), f32),
        pltpu.VMEM((rows, D), f32),
        pltpu.VMEM((rows, 128), f32),
        pltpu.VMEM((rows, D), f32),
        pltpu.VMEM((group, D), bf16),
        pltpu.VMEM((group, D), bf16),
        pltpu.VMEM((rows, D), f32),
        pltpu.VMEM((rows, D), bf16),
        pltpu.VMEM((rows, D), bf16),
        pltpu.VMEM((2 * group, width), bf16),
        pltpu.VMEM((group, width), bf16),
        pltpu.VMEM((2 * group, 3 * width), bf16),
        pltpu.VMEM((2 * group, 128), f32),
        pltpu.VMEM((2 * group, 128), f32),
        [pltpu.VMEM(dims, bf16) for dims in halves],
    ]
    scratch += [pltpu.VMEM(dims, bf16) for dims in halves]
    scratch += [pltpu.VMEM((dims[0] // 2, dims[1]), bf16) for dims in halves]
    scratch += [pltpu.VMEM((line - 1,) + dims, bf16) for dims in shards]
    scratch += [pltpu.VMEM(dims, f32) for dims in results]
    scratch += [
        pltpu.VMEM((LAYERS, 10 * D + FF), f32),
        pltpu.VMEM((line,) + spot_shape, f32),
        pltpu.VMEM((line + 2,) + spot_shape, f32),
        pltpu.VMEM(spot_shape, f32),
        dma((LAYERS * 4 * SPLIT,)),
        dma((LAYERS * 4 * SPLIT,)),
        dma((LAYERS * 13 + 1,)),
        dma((LAYERS * 13 + 1,)),
        dma((GROUPS, line)),
        dma((GROUPS, line)),
        dma((GROUPS, line - 1)),
        dma((GROUPS, line - 1)),
        pltpu.SemaphoreType.REGULAR((KINDS,)),
        pltpu.SemaphoreType.REGULAR((KINDS,)),
        dma((KINDS,)),
        dma((line + 2,)),
        dma((line + 2,)),
        dma((19,)),
    ]
    return pl.pallas_call(
        functools.partial(backward_kernel, mesh_count),
        out_shape=outs,
        in_specs=[WHOLE] * 2 + [ANY] * 19,
        out_specs=[ANY] * 4 + [WHOLE] * 2,
        scratch_shapes=scratch,
        compiler_params=pltpu.CompilerParams(
            collective_id=1, has_side_effects=True, vmem_limit_bytes=63 << 20
        ),
        name="backward",
    )(grad, vecs, *weights, *saved)


def local(
    images,
    cotangent,
    triplet_master,
    triplet_first,
    triplet_second,
    project_master,
    project_first,
    project_second,
    expand_master,
    expand_first,
    expand_second,
    shrink_master,
    shrink_first,
    shrink_second,
    vectors_master,
    vectors_first,
    vectors_second,
):
    count = lax.axis_size("dp")
    row_at = lax.axis_index("row")
    col_at = lax.axis_index("col")
    tokens, features = images.shape
    rows = -(-tokens // (2 * TILE)) * TILE
    group = 2 * rows
    half = D // 2

    shards = [
        triplet_master.astype(bf16).reshape(LAYERS, -1, 3 * half),
        project_master.astype(bf16),
        expand_master.astype(bf16),
        shrink_master.astype(bf16),
    ]
    piece = vectors_master.shape[1]
    line_at = (lax.axis_index("dp") % 2 * 2 + row_at) * 2 + col_at
    spot = jnp.where(
        jnp.arange(8 * piece) // piece == line_at, jnp.tile(vectors_master, (1, 8)), 0.0
    )
    place = jnp.arange(2 * group) % rows
    late = jnp.arange(2 * group) // group
    bias = jnp.where(place + late * rows < tokens, 0.0, -1e30).astype(f32)[None]

    (w_a, w_b, w_c, w_d, _, vectors, *saved, grad_rows, block_out) = forward_call(
        count, images, cotangent, spot, bias, shards
    )
    *grads, grad_out, vector_sums = backward_call(
        count, tokens, grad_rows, vectors, (w_a, w_b, w_c, w_d), saved, spot.shape
    )
    vector_reduced = lax.dynamic_slice_in_dim(vector_sums, line_at * piece, piece, 1)

    outs = []
    states = (
        (triplet_master, triplet_first, triplet_second),
        (project_master, project_first, project_second),
        (expand_master, expand_first, expand_second),
        (shrink_master, shrink_first, shrink_second),
    )
    grads[0] = grads[0].transpose(0, 2, 1, 3)
    for kind, (master, first, second) in enumerate(states):
        outs += adam_step(master, first, second, grads[kind], learn_rate, decay_rate)
    outs += adam_step(
        vectors_master, vectors_first, vectors_second, vector_reduced, vector_rate, 0.0
    )
    return (block_out, grad_out, *outs)


def solution(mesh):
    tokens = P(("dp", "row"), "col")
    triplet = P(None, ("col", "dp"), None, "row")
    narrow = P(None, ("row", "dp"), "col")
    wide = P(None, ("col", "dp"), "row")
    vector = P(None, ("dp", "row", "col"))
    states = (triplet,) * 3 + (narrow,) * 3 + (wide,) * 3 + (narrow,) * 3 + (vector,) * 3
    return jax.shard_map(
        local,
        mesh=mesh,
        in_specs=(tokens, tokens) + states,
        out_specs=(tokens, tokens) + states,
        check_vma=False,
    )
```

```python
import functools

import jax
import jax.numpy as jnp
from jax import lax
from jax.experimental import pallas as pl
from jax.experimental.pallas import tpu as pltpu
from jax.sharding import PartitionSpec as P

D = 1024
HEAD_DIM = 64
FF = 4096
LAYERS = 2
STEP = 10
TILE = 16

norm_epsilon = 1e-06
beta_first = 0.9
beta_second = 0.999
adam_epsilon = 1e-08
learn_rate = 0.02
vector_rate = 0.1
decay_rate = 0.05
bf16 = jnp.bfloat16
f32 = jnp.float32


def contract(left, right, left_dims, right_dims):
    return lax.dot_general(
        left, right, ((left_dims, right_dims), ((), ())), preferred_element_type=f32
    )


def adam_step(master, first, second, grad, rate, decay):
    first_new = beta_first * first + (1.0 - beta_first) * grad
    second_new = beta_second * second + (1.0 - beta_second) * grad * grad
    ratio = (
        first_new
        / (1.0 - beta_first**STEP)
        / (jnp.sqrt(second_new / (1.0 - beta_second**STEP)) + adam_epsilon)
    )
    return (first_new, second_new, master - rate * (ratio + decay * master))


MESH = pl.DeviceIdType.MESH
KINDS = 4
GROUPS = LAYERS * KINDS
WINDOW = 3
TRIGGER = 1.0
LEAD = 25.0
EARLY = 4
SPLIT = 2
ANY = pl.BlockSpec(memory_space=pl.ANY)
WHOLE = pl.BlockSpec(memory_space=pltpu.VMEM)


def nt(left, right):
    return contract(left, right, (1,), (1,))


def nn(left, right):
    return contract(left, right, (1,), (0,))


def tn(left, right):
    return contract(left, right, (0,), (0,))


class Place:
    def __init__(self, count):
        self.count = count
        self.line = count // 2
        self.dp = lax.axis_index("dp")
        self.row = lax.axis_index("row")
        self.col = lax.axis_index("col")
        self.pair = lax.rem(self.dp, 2)
        self.outer = lax.div(self.dp, 2)
        self.x_dp = self.dp + 1 - 2 * self.pair
        self.x_peer = (self.x_dp, self.row, self.col)
        self.y_peer = (self.dp, 1 - self.row, self.col)
        self.c_peer = (self.dp, self.row, 1 - self.col)

    def nearest(self, at):
        inside = (at + 1) // 2 if at % 2 else self.line - at // 2
        return jnp.where(
            self.outer == 0, self.line - at, jnp.where(self.outer == self.line - 1, at, inside)
        )

    def ahead(self, step):
        return lax.rem(self.dp + 2 * step, self.count)

    def behind(self, step):
        return lax.rem(self.dp + self.count - 2 * step, self.count)

    def z_peer(self, step):
        return (self.ahead(step), self.row, self.col)

    def greet(self):
        barrier = pltpu.get_barrier_semaphore()
        peers = [self.z_peer(step) for step in range(1, self.line)]
        peers += [self.x_peer, self.y_peer, self.c_peer]
        for peer in peers:
            pl.semaphore_signal(barrier, inc=1, device_id=peer, device_id_type=MESH)
        pl.semaphore_wait(barrier, len(peers))


def remote(source, target, send, recv, peer):
    return pltpu.make_async_remote_copy(
        source, target, send, recv, device_id=peer, device_id_type=MESH
    )


def aligned(value, by=128):
    return pl.multiple_of(value, by)


def weight_view(kind, ref, layer, place, dp, col):
    if kind in (0, 2):
        size = ref.shape[1] // (2 * place.count)
        return ref.at[layer, pl.ds(aligned((col * place.count + dp) * size, 16), size), :]
    size = ref.shape[1] // place.count
    return ref.at[
        layer,
        pl.ds(aligned(dp * size, 16), size),
        pl.ds(aligned(col * (D // 2)), D // 2),
    ]


def column_view(kind, ref, layer, col):
    if kind in (0, 2):
        return ref.at[layer, pl.ds(aligned(col * (D // 2), 16), D // 2), :]
    return ref.at[layer, :, pl.ds(aligned(col * (D // 2)), D // 2)]


class Gather:
    def __init__(self, place, shards, wholes, far, refs):
        self.place, self.shards, self.wholes, self.far = place, shards, wholes, far
        self.send, self.recv, self.own = refs["send"], refs["recv"], refs["own"]
        self.far_send, self.far_recv = refs["far_send"], refs["far_recv"]

    def view(self, group, dp):
        layer, kind = divmod(group, KINDS)
        return weight_view(kind, self.wholes[kind], layer, self.place, dp, self.place.col)

    def copy(self, group, at, source, target, peer):
        return remote(source, target, self.send.at[group, at], self.recv.at[group, at], peer)

    def shard(self, group):
        layer, kind = divmod(group, KINDS)
        return self.shards[kind].at[layer]

    def line_copy(self, group, step):
        place = self.place
        target = self.view(group, place.dp)
        return self.copy(group, step - 1, self.shard(group), target, place.z_peer(step))

    def pair_copy(self, group, step):
        place = self.place
        view = self.view(group, place.behind(step))
        source = self.shard(group) if isinstance(step, int) else view
        return self.copy(group, place.line - 1 + step, source, view, place.x_peer)

    def core_copy(self, group, step, pair):
        place = self.place
        dp = lax.rem(place.x_dp + place.count - 2 * step, place.count) if pair else place.behind(step)
        view = self.view(group, dp)
        source = view if pair or not isinstance(step, int) else self.shard(group)
        at = 2 * place.line - 1 + pair * place.line + step
        return self.copy(group, at, source, view, place.c_peer)

    def own_copy(self, group):
        return pltpu.make_async_copy(
            self.shard(group), self.view(group, self.place.dp), self.own.at[group]
        )

    def line_out(self, group):
        for at in range(1, self.place.line):
            self.line_copy(group, at).start()

    def own_out(self, group):
        self.pair_copy(group, 0).start()
        self.core_copy(group, 0, 0).start()
        self.own_copy(group).start()

    def line_in(self, group, at):
        step = self.place.nearest(at)
        self.line_copy(group, step).wait_recv()
        self.pair_copy(group, step).start()
        self.core_copy(group, step, 0).start()

    def pair_in(self, group, at):
        step = self.place.nearest(at) if at else 0
        self.pair_copy(group, step).wait_recv()
        self.core_copy(group, step, 1).start()

    def arrive(self, group):
        self.own_copy(group).wait()
        for pair in range(2):
            for step in range(self.place.line):
                self.core_copy(group, step, pair).wait_recv()

    def far_copy(self, layer):
        place = self.place
        return remote(
            column_view(1, self.wholes[1], layer, place.col),
            column_view(1, self.far, layer, place.col),
            self.far_send.at[layer, 0],
            self.far_recv.at[layer, 0],
            place.y_peer,
        )

    def far_core_copy(self, layer):
        view = column_view(1, self.far, layer, self.place.col)
        return remote(
            view, view, self.far_send.at[layer, 1], self.far_recv.at[layer, 1], self.place.c_peer
        )

    def far_start(self, layer):
        self.own_copy(layer * KINDS + 1).wait()
        self.far_copy(layer).start()

    def far_in(self, layer):
        self.far_copy(layer).wait_recv()
        self.far_core_copy(layer).start()

    def far_arrive(self, layer):
        self.far_core_copy(layer).wait_recv()

    def finish(self):
        for group in range(GROUPS):
            for step in range(self.place.line):
                if step:
                    self.line_copy(group, step).wait_send()
                self.pair_copy(group, step).wait_send()
                self.core_copy(group, step, 0).wait_send()
                self.core_copy(group, step, 1).wait_send()
        for layer in range(LAYERS):
            self.far_copy(layer).wait_send()
            self.far_core_copy(layer).wait_send()


class Vectors:
    def __init__(self, place, spot, raw, spare, send, recv):
        self.place, self.spot, self.raw, self.spare = place, spot, raw, spare
        self.send, self.recv = send, recv

    def line_copy(self, step):
        place = self.place
        return remote(
            self.spot,
            self.raw.at[place.outer],
            self.send.at[2 + step],
            self.recv.at[2 + step],
            place.z_peer(step),
        )

    def start(self):
        for step in range(1, self.place.line):
            self.line_copy(step).start()
        self.raw[self.place.outer] = self.spot[...]

    def line_in(self):
        for step in range(1, self.place.line):
            self.line_copy(step).wait()

    def add(self, at, peer):
        copy = remote(self.raw, self.spare.at[at], self.send.at[at], self.recv.at[at], peer)
        copy.start()
        copy.wait()
        self.raw[...] = self.raw[...] + self.spare[at]

    def spread(self, vecs):
        size = self.spot.shape[1]
        for outer in range(self.place.line):
            vecs[:, outer * size : (outer + 1) * size] = self.raw[outer]


def to_tokens(place, values, padded, arrived, target, send, recv):
    rows = arrived.shape[0]
    tokens, half = values.shape
    padded[rows:, :] = jnp.zeros_like(padded[rows:, :])
    padded[:tokens, :] = values[...]
    copy = remote(
        padded.at[pl.ds(aligned((1 - place.col) * rows, 16), rows), :],
        arrived,
        send,
        recv,
        place.c_peer,
    )
    copy.start()
    own = padded[pl.ds(aligned(place.col * rows, 16), rows), :]
    target[:, pl.ds(aligned(place.col * half), half)] = own.astype(target.dtype)
    copy.wait()
    other = pl.ds(aligned((1 - place.col) * half), half)
    target[:, other] = arrived[...].astype(target.dtype)


def to_features(place, values, arrived, target, send, recv):
    rows = values.shape[0]
    tokens, half = target.shape
    copy = remote(
        values.at[:, pl.ds(aligned((1 - place.col) * half), half)], arrived, send, recv, place.c_peer
    )
    copy.start()
    own = values[:, pl.ds(aligned(place.col * half), half)]
    copy.wait()
    other = arrived[...]

    @pl.when(place.col == 0)
    def _():
        target[:rows, :] = own
        target[rows:, :] = other[: tokens - rows]

    @pl.when(place.col == 1)
    def _():
        target[:rows, :] = other
        target[rows:, :] = own[: tokens - rows]


def norm_rows(source, gain, shift, unit, inverse, target, start, rows):
    size = 16

    def step(at, carry):
        place = pl.ds(aligned(start + at * size, size), size)
        values = source[place, :].astype(f32)
        centre = jnp.sum(values, 1, keepdims=True) * (1.0 / D)
        spread = jnp.sum(values * values, 1, keepdims=True) * (1.0 / D) - centre * centre
        scale = lax.rsqrt(spread + norm_epsilon)
        norm = (values - centre) * scale
        unit[place, :] = norm
        inverse[place, :] = jnp.broadcast_to(scale, (size, 128))
        target[place, :] = (norm * gain + shift).astype(bf16)
        return carry

    lax.fori_loop(0, rows // size, step, 0)


def gelu_both(values):
    normal = 0.5 + 0.5 * lax.erf(values * (0.5**0.5))
    density = jnp.exp(-0.5 * values * values) * 0.3989422804014327
    return values * normal, normal + values * density


def forward_kernel(count, *refs):
    (
        images,
        cotangent,
        spot_in,
        master_a,
        master_b,
        master_c,
        master_d,
        w_a,
        w_b,
        w_c,
        w_d,
        w_far,
        vecs_out,
        unit_one_out,
        inv_one_out,
        normed_out,
        heads_out,
        lse_out,
        mixed_out,
        branch_out,
        unit_two_out,
        inv_two_out,
        normed_two_out,
        active_out,
        slope_out,
        output_out,
        head_mix_out,
        back_out_out,
        cotangent_out,
        middle_out,
        shard_a,
        shard_b,
        shard_c,
        shard_d,
        state,
        padded,
        arrived,
        spot,
        spare,
        raw,
        vecs,
        wq,
        wm,
        wu,
        wd,
        wf,
        unit,
        inverse,
        unit_two,
        inverse_two,
        normed,
        normed_two,
        heads_all,
        head_tx,
        head_mix,
        lse,
        mixed_all,
        mixed_far,
        back_out,
        branch,
        output,
        active,
        slope,
        tx,
        rx,
        part,
        g_send,
        g_recv,
        g_own,
        far_send,
        far_recv,
        v_send,
        v_recv,
        y_send,
        y_recv,
        c_send,
        c_recv,
        stage_sem,
        save_sem,
    ) = refs
    tokens = images.shape[0]
    rows = state.shape[0]
    group = 2 * rows
    half = D // 2
    width = half // 2
    place = Place(count)
    row, col = place.row, place.col
    wholes = (w_a, w_b, w_c, w_d)
    gather = Gather(
        place,
        (shard_a, shard_b, shard_c, shard_d),
        wholes,
        w_far,
        {
            "send": g_send,
            "recv": g_recv,
            "own": g_own,
            "far_send": far_send,
            "far_recv": far_recv,
        },
    )
    place.greet()
    spot[...] = spot_in[...]
    vectors = Vectors(place, spot, raw, spare, v_send, v_recv)
    vectors.start()
    cast_done = set()

    def cast(at):
        if at in cast_done or at >= GROUPS:
            return
        cast_done.add(at)
        layer, kind = divmod(at, KINDS)
        if kind == 0:
            for part_at in range(3):
                shard_a[layer, :, part_at * half : (part_at + 1) * half] = master_a[
                    layer, part_at
                ].astype(bf16)
        else:
            source = (master_a, master_b, master_c, master_d)[kind]
            (shard_a, shard_b, shard_c, shard_d)[kind][layer] = source[layer].astype(bf16)

    for at in range(WINDOW):
        cast(at)
        gather.line_out(at)

    plan = []
    due = [4.0]
    for at in range(GROUPS):
        dims = wholes[at % KINDS].shape
        due.append(due[-1] + 1.1 * (dims[1] * dims[2] / 92e3))
    for at in range(GROUPS):
        begin, span = due[at], due[at + 1] - due[at]
        for step in range(1, place.line):
            line_due = begin + span * (0.3 + 0.7 * step / (place.line - 1))
            plan.append((line_due, 1, gather.line_in, (at, step)))
            if at >= EARLY and step == 1:
                plan.append((begin - 5.0, 0.5, gather.own_out, (at,)))
            if at + WINDOW < GROUPS and step == max(1, round(TRIGGER * (place.line - 1))):
                plan.append((line_due, 1.5, gather.line_out, (at + WINDOW,)))
        for step in range(place.line):
            pair_due = begin + span * (0.6 + 0.7 * step / (place.line - 1)) + 2.0
            plan.append((pair_due, 2, gather.pair_in, (at, step)))
    plan.sort(key=lambda item: item[:2])
    last_of = [
        max(
            spot
            for spot, item in enumerate(plan)
            if item[2] == gather.pair_in and item[3] == (at, place.line - 1)
        )
        for at in range(GROUPS)
    ]
    plan_at = [0]

    def advance(until):
        for item in plan[plan_at[0] : until]:
            item[2](*item[3])
        plan_at[0] = max(until, plan_at[0])

    def pump(time):
        advance(sum(1 for item in plan if item[0] <= time + LEAD))

    def ensure(at):
        advance(last_of[at] + 1)

    def pump_step(at, count_steps, begin, step_time):
        for step in range(count_steps):
            until = sum(1 for item in plan if item[0] <= begin + (step + 1) * step_time + LEAD)
            if until > plan_at[0]:
                pl.when(at == step)(functools.partial(advance, until))

    pending = {}

    def settle(*names):
        for name in names:
            if name in pending:
                pending.pop(name).wait()

    def save(name, at, source, target):
        settle(name)
        copy = pltpu.make_async_copy(source, target, save_sem.at[at])
        copy.start()
        pending[name] = copy

    staged = {}
    buffers = (wq, wm, wu, wd)

    def stage(kind, layer):
        at = layer * KINDS + kind
        if kind == 1:
            for pair in range(2):
                for step in range(place.line):
                    gather.core_copy(at, step, pair).wait_recv()
        else:
            gather.arrive(at)
        copy = pltpu.make_async_copy(wholes[kind].at[layer], buffers[kind], stage_sem.at[kind])
        copy.start()
        staged[kind] = copy

    def stage_far(layer):
        gather.far_arrive(layer)
        copy = pltpu.make_async_copy(w_far.at[layer], wf, stage_sem.at[KINDS])
        copy.start()
        staged[KINDS] = copy

    def ready(kind):
        staged.pop(kind).wait()

    y_at = [0]

    def y_copy(source, target):
        at = y_at[0]
        y_at[0] += 1
        copy = remote(source, target, y_send.at[at], y_recv.at[at], place.y_peer)
        copy.start()
        return copy

    c_at = [0]

    def c_copy(source, target):
        at = c_at[0]
        c_at[0] += 1
        copy = remote(source, target, c_send.at[at], c_recv.at[at], place.c_peer)
        copy.start()
        return copy

    chunk = rows // SPLIT

    def send_rows(buffer, at):
        return y_copy(
            buffer.at[pl.ds(at * chunk, chunk), :],
            buffer.at[pl.ds(rows + at * chunk, chunk), :],
        )

    to_tokens(place, images, padded, arrived, state, c_send.at[0], c_recv.at[0])
    c_at[0] = 2
    vectors.line_in()
    vectors.add(0, place.x_peer)
    for at in range(GROUPS):
        cast(at)
    for at in range(EARLY):
        gather.own_out(at)
    vectors.add(1, place.y_peer)
    vectors.add(2, place.c_peer)
    vectors.spread(vecs)
    save("vecs", 11, vecs, vecs_out)

    lane = lax.broadcasted_iota(jnp.int32, (1, 128), 1) < HEAD_DIM
    key_at = lax.broadcasted_iota(jnp.int32, (1, 2 * group), 1)
    late = key_at >= group
    spare_row = tokens - rows
    padding = late & (
        (key_at >= group + spare_row) & (key_at < group + rows) | (key_at >= group + rows + spare_row)
    )
    mask = jnp.where(padding, -1e30, 0.0)
    valid = lax.broadcasted_iota(jnp.int32, (rows, 1), 0) < tokens - col * rows

    def vector(layer, at):
        return vecs[layer : layer + 1, at * D : (at + 1) * D]

    def norm_one(layer, at):
        norm_rows(
            state, vector(layer, 0), vector(layer, 1), unit, inverse, normed, at * chunk, chunk
        )
        return send_rows(normed, at)

    copies = [norm_one(0, at) for at in range(SPLIT)]
    to_tokens(place, cotangent, padded, arrived, branch, c_send.at[1], c_recv.at[1])
    cotangent_out[...] = branch[...].astype(bf16)
    back_out[:rows, :] = (vector(LAYERS - 1, 13) * branch[...]).astype(bf16)
    out_copies = [send_rows(back_out, at) for at in range(SPLIT)]
    for layer in range(LAYERS):
        first = layer == 0
        heads, mixed = heads_all.at[layer], mixed_all.at[layer]
        save("unit", 0, unit, unit_one_out.at[layer])
        save("inverse", 1, inverse, inv_one_out.at[layer])
        if first:
            ensure(0)
            stage(0, 0)
        ready(0)

        def triple(start, size):
            def step(at, carry):
                part_at = lax.rem(at, 3)
                mine = lax.div(at, 3)
                owner = jnp.where(mine == 1, col, 1 - col)
                column = aligned(part_at * half + owner * width)
                value = nn(normed[start : start + size, :], wq[:, pl.ds(column, width)])
                bias_at = aligned(
                    jnp.where(part_at == 2, 3 * D, 2 * D) + row * half + owner * width
                )
                bias = vecs[layer : layer + 1, pl.ds(bias_at, width)]
                bias = bias * jnp.where(part_at == 1, 0.0, 1.0)
                inside = valid[start % rows : start % rows + size]
                value = jnp.where(inside, value + bias, 0.0).astype(bf16)
                lanes = pl.ds(aligned(part_at * width), width)

                @pl.when(mine == 0)
                def _():
                    head_tx[start : start + size, lanes] = value

                @pl.when(mine == 1)
                def _():
                    heads[pl.ds(aligned(col * group + start, 16), size), lanes] = value

                return carry

            lax.fori_loop(0, 6, step, 0)
            return c_copy(
                head_tx.at[pl.ds(start, size), :],
                heads.at[pl.ds(aligned(col * group + start, 16), size), :],
            )

        core_copies = [triple(0, rows)]
        if first:
            ensure(1)
            gather.far_start(0)
            for copy in copies:
                copy.wait()
            core_copies.append(triple(rows, rows))
            pump(33)
        else:
            ensure(5)
            gather.far_start(1)
            stage(1, 1)
            pump(106)
            copies[0].wait()
            core_copies.append(triple(rows, chunk))
            pump(111)
            copies[1].wait()
            core_copies.append(triple(rows + chunk, chunk))
            pump(119)
        save("normed", 2, normed, normed_out.at[layer])
        for copy in core_copies:
            copy.wait()
        save("heads", 3, heads, heads_out.at[layer])
        settle("lse", "head_mix")

        attend_at = [35.0 if first else 121.0]

        def attend(owner, side):
            begin_time = attend_at[0]
            attend_at[0] += 3.4
            tile = rows // 2
            begin = owner * group + side * rows

            def step(at, carry):
                place_rows = pl.ds(aligned(begin + at * tile, 16), tile)
                for pair in range(width // 128):
                    lanes = slice(pair * 128, pair * 128 + 128)
                    query = heads[place_rows, lanes] * jnp.asarray(HEAD_DIM**-0.5, bf16)
                    zero = jnp.zeros_like(query)
                    both = jnp.concatenate(
                        [jnp.where(lane, query, zero), jnp.where(lane, zero, query)], 0
                    )
                    key = heads[:, width + pair * 128 : width + pair * 128 + 128]
                    value = heads[:, 2 * width + pair * 128 : 2 * width + pair * 128 + 128]
                    scores = nt(both, key) + mask
                    peak = jnp.max(scores, 1, keepdims=True)
                    weights = jnp.exp(scores - peak)
                    total = jnp.sum(weights, 1, keepdims=True)
                    result = nn(weights.astype(bf16), value) / total
                    logsum = peak + jnp.log(total)
                    head_mix[place_rows, lanes] = jnp.where(
                        lane, result[:tile], result[tile:]
                    ).astype(bf16)
                    lse[place_rows, lanes] = jnp.where(lane, logsum[:tile], logsum[tile:])
                pump_step(at, rows // tile, begin_time, 1.7)
                return carry

            lax.fori_loop(0, rows // tile, step, 0)
            plan_at[0] = max(plan_at[0], sum(1 for item in plan if item[0] <= attend_at[0] + LEAD))

        my_lanes = pl.ds(aligned(col * width), width)

        def send_mixed(side):
            return c_copy(
                head_mix.at[pl.ds(aligned((1 - col) * group + side * rows, 16), rows), :],
                mixed.at[pl.ds(side * rows, rows), my_lanes],
            )

        def keep_mixed(side):
            mixed[side * rows : side * rows + rows, my_lanes] = head_mix[
                pl.ds(aligned(col * group + side * rows, 16), rows), :
            ]

        attend(1 - col, 1)
        copy = send_mixed(1)
        attend(col, 1)
        keep_mixed(1)
        copy.wait()
        settle("normed_two")
        far_copy = y_copy(mixed.at[pl.ds(rows, rows), :], mixed_far)
        if first:
            stage(1, 0)
        attend(1 - col, 0)
        copy = send_mixed(0)
        gather.far_in(layer)
        attend(col, 0)
        keep_mixed(0)
        copy.wait()
        save("lse", 4, lse, lse_out.at[layer])
        save("head_mix", 14, head_mix, head_mix_out.at[layer])
        save("mixed", 5, mixed, mixed_out.at[layer])
        stage_far(layer)
        ready(1)
        settle("branch", "unit_two", "inverse_two")

        def project(start):
            def step(at, carry):
                lanes = pl.ds(aligned(at * half), half)
                value = nn(mixed[start : start + chunk, :], wm[:, lanes])
                value = value + nn(mixed_far[start : start + chunk, :], wf[:, lanes])
                bias_at = aligned(4 * D + at * half)
                value = value + vecs[layer : layer + 1, pl.ds(bias_at, half)]
                scale = vecs[layer : layer + 1, pl.ds(aligned(5 * D + at * half), half)]
                branch[start : start + chunk, lanes] = value
                state[start : start + chunk, lanes] += scale * value
                return carry

            lax.fori_loop(0, 2, step, 0)

        far_copy.wait()
        ready(KINDS)
        copies = []
        for at in range(SPLIT):
            project(at * chunk)
            norm_rows(
                state,
                vector(layer, 6),
                vector(layer, 7),
                unit_two,
                inverse_two,
                normed_two,
                at * chunk,
                chunk,
            )
            copies.append(send_rows(normed_two, at))
            pump((50 if first else 137) + at * 1.5)
        ensure(2 if first else 6)
        stage(2, layer)
        save("branch", 6, branch, branch_out.at[layer])
        save("unit_two", 7, unit_two, unit_two_out.at[layer])
        save("inverse_two", 8, inverse_two, inv_two_out.at[layer])
        ready(2)
        settle("active", "slope", "normed")

        def expand(start, size, begin_time):
            def step(at, carry):
                lanes = pl.ds(aligned(at * half), half)
                bias_at = aligned(8 * D + row * (FF // 2) + at * half)
                value = nn(normed_two[start : start + size, :], wu[:, lanes])
                value = value + vecs[layer : layer + 1, pl.ds(bias_at, half)]
                act, grad = gelu_both(value)
                active[start : start + size, lanes] = act.astype(bf16)
                slope[start : start + size, lanes] = grad.astype(bf16)
                pump_step(at, FF // 2 // half, begin_time, 0.8)
                return carry

            lax.fori_loop(0, FF // 2 // half, step, 0)
            end = begin_time + FF // 2 // half * 0.8 + LEAD
            plan_at[0] = max(plan_at[0], sum(1 for item in plan if item[0] <= end))

        def shrink(start, size, target, target_at):
            def step(at, carry):
                lanes = pl.ds(aligned(at * half), half)
                value = nn(active[start : start + size, :], wd[:, lanes])
                target[pl.ds(target_at, size), lanes] = value.astype(target.dtype)
                return carry

            lax.fori_loop(0, 2, step, 0)

        def shrink_send(at):
            shrink(rows + at * chunk, chunk, tx, at * chunk)
            view = pl.ds(at * chunk, chunk)
            return y_copy(tx.at[view, :], rx.at[view, :])

        back_copies = []
        if first:
            expand(0, rows, 56.0)
            copies[0].wait()
            expand(rows, chunk, 63.0)
            copies[1].wait()
            expand(rows + chunk, chunk, 71.0)
            ensure(3)
            stage(3, 0)
            ready(3)
            back_copies.append(shrink_send(0))
            back_copies.append(shrink_send(1))
        else:
            expand(0, rows, 139.0)
            for at in range(SPLIT):
                copies[at].wait()
                expand(rows + at * chunk, chunk, 146.0 + 8.0 * at)
        if first:
            shrink(0, rows, part, 0)
        save("normed_two", 9, normed_two, normed_two_out.at[layer])
        save("active", 10, active, active_out.at[layer])
        save("slope", 12, slope, slope_out.at[layer])
        if first:
            pump(87)
        else:
            for copy in out_copies:
                copy.wait()
            save("back_out", 15, back_out, back_out_out)
            save("state", 16, state, middle_out)
            break
        settle("unit", "inverse")
        next_copies = []
        for at in range(SPLIT):
            back_copies[at].wait()
            here = slice(at * chunk, at * chunk + chunk)
            output[here, :] = part[here, :] + rx[here, :].astype(f32) + vector(layer, 12)
            state[here, :] = state[here, :] + vector(layer, 13) * output[here, :]
            next_copies.append(norm_one(1, at))
            if at == 0:
                pump(94)
        save("output", 13, output, output_out)
        ensure(4)
        stage(0, 1)
        copies = next_copies
    ensure(GROUPS - 1)
    gather.arrive(GROUPS - 1)
    gather.finish()
    settle(*list(pending))


def padded_rows(tokens):
    return -(-tokens // (2 * TILE)) * TILE


def forward_call(mesh_count, images, cotangent, spot, masters):
    tokens = images.shape[0]
    rows = padded_rows(tokens)
    group = 2 * rows
    half = D // 2
    width = half // 2
    line = mesh_count // 2

    def shape(*dims, kind=f32):
        return jax.ShapeDtypeStruct(dims, kind)

    outs = [
        shape(LAYERS, D, 3 * half, kind=bf16),
        shape(LAYERS, half, D, kind=bf16),
        shape(LAYERS, D, FF // 2, kind=bf16),
        shape(LAYERS, FF // 2, D, kind=bf16),
        shape(LAYERS, half, D, kind=bf16),
        shape(LAYERS, 10 * D + FF),
        shape(LAYERS, rows, D),
        shape(LAYERS, rows, 128),
        shape(LAYERS, group, D, kind=bf16),
        shape(LAYERS, 2 * group, 3 * width, kind=bf16),
        shape(LAYERS, 2 * group, width),
        shape(LAYERS, group, half, kind=bf16),
        shape(LAYERS, rows, D),
        shape(LAYERS, rows, D),
        shape(LAYERS, rows, 128),
        shape(LAYERS, group, D, kind=bf16),
        shape(LAYERS, group, FF // 2, kind=bf16),
        shape(LAYERS, group, FF // 2, kind=bf16),
        shape(rows, D),
        shape(LAYERS, 2 * group, width, kind=bf16),
        shape(group, D, kind=bf16),
        shape(rows, D, kind=bf16),
        shape(rows, D),
    ]
    dma = pltpu.SemaphoreType.DMA
    scratch = [
        pltpu.VMEM((LAYERS, D // (2 * mesh_count), 3 * half), bf16),
        pltpu.VMEM((LAYERS, half // mesh_count, half), bf16),
        pltpu.VMEM((LAYERS, D // (2 * mesh_count), FF // 2), bf16),
        pltpu.VMEM((LAYERS, FF // 2 // mesh_count, half), bf16),
        pltpu.VMEM((rows, D), f32),
        pltpu.VMEM((group, half), bf16),
        pltpu.VMEM((rows, half), bf16),
        pltpu.VMEM(spot.shape, f32),
        pltpu.VMEM((3, line) + spot.shape, f32),
        pltpu.VMEM((line,) + spot.shape, f32),
        pltpu.VMEM((LAYERS, 10 * D + FF), f32),
        pltpu.VMEM((D, 3 * half), bf16),
        pltpu.VMEM((half, D), bf16),
        pltpu.VMEM((D, FF // 2), bf16),
        pltpu.VMEM((FF // 2, D), bf16),
        pltpu.VMEM((half, D), bf16),
        pltpu.VMEM((rows, D), f32),
        pltpu.VMEM((rows, 128), f32),
        pltpu.VMEM((rows, D), f32),
        pltpu.VMEM((rows, 128), f32),
        pltpu.VMEM((group, D), bf16),
        pltpu.VMEM((group, D), bf16),
        pltpu.VMEM((LAYERS, 2 * group, 3 * width), bf16),
        pltpu.VMEM((group, 3 * width), bf16),
        pltpu.VMEM((2 * group, width), bf16),
        pltpu.VMEM((2 * group, width), f32),
        pltpu.VMEM((LAYERS, group, half), bf16),
        pltpu.VMEM((rows, half), bf16),
        pltpu.VMEM((group, D), bf16),
        pltpu.VMEM((rows, D), f32),
        pltpu.VMEM((rows, D), f32),
        pltpu.VMEM((group, FF // 2), bf16),
        pltpu.VMEM((group, FF // 2), bf16),
        pltpu.VMEM((rows, D), bf16),
        pltpu.VMEM((rows, D), bf16),
        pltpu.VMEM((rows, D), f32),
        dma((GROUPS, 4 * line - 1)),
        dma((GROUPS, 4 * line - 1)),
        dma((GROUPS,)),
        dma((LAYERS, 2)),
        dma((LAYERS, 2)),
        dma((line + 2,)),
        dma((line + 2,)),
        dma((16,)),
        dma((16,)),
        dma((16,)),
        dma((16,)),
        dma((KINDS + 1,)),
        dma((17,)),
    ]
    return pl.pallas_call(
        functools.partial(forward_kernel, mesh_count),
        out_shape=outs,
        in_specs=[WHOLE] * 7,
        out_specs=[ANY] * 21 + [WHOLE] + [ANY],
        scratch_shapes=scratch,
        compiler_params=pltpu.CompilerParams(
            collective_id=0, has_side_effects=True, vmem_limit_bytes=60 << 20
        ),
        name="forward",
    )(images, cotangent, spot, *masters)


def fold(values):
    return jnp.sum(values.reshape(-1, 8, values.shape[-1]), 0)


def total(values):
    return jnp.sum(values, 0, keepdims=True)


def flip(picks, values):
    high = values.astype(bf16)
    rest = values - high.astype(f32)
    middle = rest.astype(bf16)
    low = (rest - middle.astype(f32)).astype(bf16)
    return nt(picks, high) + nt(picks, middle) + nt(picks, low)


class Scatter:
    def __init__(self, place, sums, pair_rx, line_rx, outs, refs):
        self.place, self.sums, self.pair_rx, self.line_rx = place, sums, pair_rx, line_rx
        self.outs, self.result = outs, refs["result"]
        self.x_send, self.x_recv = refs["x_send"], refs["x_recv"]
        self.z_send, self.z_recv = refs["z_send"], refs["z_recv"]
        self.x_free, self.z_free, self.out_sem = refs["x_free"], refs["z_free"], refs["out_sem"]
        self.writing = {}

    def size(self, kind):
        return self.sums[kind].shape[0] // self.place.count

    def block(self, kind, dp):
        size = self.size(kind)
        return pl.ds(aligned(dp * size, 16), size)

    def x_copy(self, layer, kind, outer):
        place = self.place
        size = self.size(kind)
        at = layer * KINDS + kind
        return remote(
            self.sums[kind].at[self.block(kind, 2 * outer + 1 - place.pair), :],
            self.pair_rx[kind].at[pl.ds(outer * size, size), :],
            self.x_send.at[at, outer],
            self.x_recv.at[at, outer],
            place.x_peer,
        )

    def z_copy(self, layer, kind, outer):
        place = self.place
        size = self.size(kind)
        at = layer * KINDS + kind
        step = lax.rem(outer - place.outer + place.line, place.line)
        return remote(
            self.pair_rx[kind].at[pl.ds(aligned(outer * size, 16), size), :],
            self.line_rx[kind].at[step - 1],
            self.z_send.at[at, step - 1],
            self.z_recv.at[at, step - 1],
            (2 * outer + place.pair, place.row, place.col),
        )

    def x_start(self, layer, kind):
        if layer < LAYERS - 1:
            pl.semaphore_wait(self.x_free.at[kind], 1)
        for outer in range(self.place.line):
            self.x_copy(layer, kind, outer).start()

    def x_finish(self, layer, kind):
        place = self.place
        size = self.size(kind)
        rows = min(size, 64)
        if layer < LAYERS - 1:
            pl.semaphore_wait(self.z_free.at[kind], place.line - 1)
        for outer in range(place.line):
            self.x_copy(layer, kind, outer).wait()

            def step(at, carry, outer=outer):
                here = pl.ds(aligned(outer * size + at * rows, 16), rows)
                own = pl.ds(aligned((2 * outer + place.pair) * size + at * rows, 16), rows)
                pair_rx = self.pair_rx[kind]
                value = pair_rx[here, :].astype(f32) + self.sums[kind][own, :].astype(f32)
                pair_rx[here, :] = value.astype(bf16)
                return carry

            lax.fori_loop(0, size // rows, step, 0)

            @pl.when(place.outer != outer)
            def _(outer=outer):
                self.z_copy(layer, kind, outer).start()

    def z_finish(self, layer, kind):
        place = self.place
        size = self.size(kind)
        for step_at in range(1, place.line):
            self.z_copy(layer, kind, lax.rem(place.outer + step_at, place.line)).wait()
        if kind in self.writing:
            self.writing.pop(kind).wait()
        rows = min(size, 64)

        def step(at, carry):
            here = pl.ds(aligned(at * rows, 16), rows)
            own = pl.ds(aligned(place.outer * size + at * rows, 16), rows)
            value = self.pair_rx[kind][own, :].astype(f32)
            for step_at in range(place.line - 1):
                value = value + self.line_rx[kind][step_at, here, :].astype(f32)
            if kind == 0:
                third = value.shape[1] // 3
                for part_at in range(3):
                    self.result[kind][part_at, here, :] = value[:, part_at * third : (part_at + 1) * third]
            else:
                self.result[kind][here, :] = value
            return carry

        lax.fori_loop(0, size // rows, step, 0)
        copy = pltpu.make_async_copy(
            self.result[kind], self.outs[kind].at[layer], self.out_sem.at[kind]
        )
        copy.start()
        self.writing[kind] = copy
        if layer == LAYERS - 1:
            pl.semaphore_signal(
                self.x_free.at[kind], inc=1, device_id=place.x_peer, device_id_type=MESH
            )
            for step_at in range(1, place.line):
                pl.semaphore_signal(
                    self.z_free.at[kind],
                    inc=1,
                    device_id=place.z_peer(step_at),
                    device_id_type=MESH,
                )

    def finish(self):
        for copy in self.writing.values():
            copy.wait()


def scatter_vectors(place, grads, packed, spare, spot, target, send, recv):
    size = spot.shape[1]
    for outer in range(place.line):
        packed[outer] = grads[:, outer * size : (outer + 1) * size]
    copies = []
    for step in range(1, place.line):
        outer = lax.rem(place.outer + step, place.line)
        copy = remote(
            packed.at[outer], spare.at[2 + step], send.at[2 + step], recv.at[2 + step], place.z_peer(step)
        )
        copy.start()
        copies.append(copy)
    for copy in copies:
        copy.wait()
    value = packed[place.outer]
    for step in range(1, place.line):
        value = value + spare[2 + step]
    spot[...] = value
    for at, peer in enumerate((place.x_peer, place.y_peer, place.c_peer)):
        copy = remote(spot, spare.at[at], send.at[at], recv.at[at], peer)
        copy.start()
        copy.wait()
        spot[...] = spot[...] + spare[at]
    target[...] = spot[...]


def backward_kernel(count, *refs):
    (
        grad_in,
        vecs,
        w_a,
        w_b,
        w_c,
        w_d,
        unit_one_in,
        inv_one_in,
        normed_in,
        heads_in,
        lse_in,
        mixed_in,
        branch_in,
        unit_two_in,
        inv_two_in,
        normed_two_in,
        active_in,
        slope_in,
        output_in,
        head_mix_in,
        back_out_in,
        middle_in,
        grad_a,
        grad_b,
        grad_c,
        grad_d,
        grad_out,
        vec_out,
        block_out,
        wq,
        wm,
        wu,
        wd,
        active,
        slope,
        feed,
        heads,
        lse,
        head_mix,
        mixed,
        aside,
        unit,
        inverse,
        grad,
        back_out,
        back_branch,
        part,
        tx,
        rx,
        rx_out,
        arrived,
        head_back,
        head_tx,
        head_grad,
        key_sum,
        value_sum,
        half_tx,
        sum_a,
        sum_b,
        sum_c,
        sum_d,
        pair_a,
        pair_b,
        pair_c,
        pair_d,
        line_a,
        line_b,
        line_c,
        line_d,
        result_a,
        result_b,
        result_c,
        result_d,
        vec_grads,
        packed,
        spare,
        spot,
        y_send,
        y_recv,
        c_send,
        c_recv,
        x_send,
        x_recv,
        z_send,
        z_recv,
        x_free,
        z_free,
        out_sem,
        v_send,
        v_recv,
        load_sem,
    ) = refs
    tokens = grad_out.shape[0]
    rows = grad_in.shape[0]
    group = 2 * rows
    half = D // 2
    width = half // 2
    pairs = width // 128
    place = Place(count)
    row, col = place.row, place.col
    sums = (sum_a, sum_b, sum_c, sum_d)
    place.greet()
    scatter = Scatter(
        place,
        sums,
        (pair_a, pair_b, pair_c, pair_d),
        (line_a, line_b, line_c, line_d),
        (grad_a, grad_b, grad_c, grad_d),
        {
            "result": (result_a, result_b, result_c, result_d),
            "x_send": x_send,
            "x_recv": x_recv,
            "z_send": z_send,
            "z_recv": z_recv,
            "x_free": x_free,
            "z_free": z_free,
            "out_sem": out_sem,
        },
    )
    triple_back = active

    sources = {
        "wd": (w_d, wd),
        "wu": (w_c, wu),
        "wm": (w_b, wm),
        "wq": (w_a, wq),
        "slope": (slope_in, slope),
        "active": (active_in, active),
        "normed_two": (normed_two_in, feed),
        "normed": (normed_in, feed),
        "output": (output_in, aside),
        "branch": (branch_in, aside),
        "unit_two": (unit_two_in, unit),
        "unit_one": (unit_one_in, unit),
        "inv_two": (inv_two_in, inverse),
        "inv_one": (inv_one_in, inverse),
        "heads": (heads_in, heads),
        "lse": (lse_in, lse),
        "head_mix": (head_mix_in, head_mix),
        "mixed": (mixed_in, mixed),
        "back_out": (back_out_in, back_out),
        "middle": (middle_in, part),
    }
    names = list(sources)
    loading = {}

    def load(layer, *wanted):
        for name in wanted:
            source, buffer = sources[name]
            if name not in ("back_out", "output", "middle"):
                source = source.at[layer]
            copy = pltpu.make_async_copy(source, buffer, load_sem.at[names.index(name)])
            copy.start()
            loading[name] = copy

    def loaded(*wanted):
        for name in wanted:
            loading.pop(name).wait()

    y_at = [0]

    def y_copy(source, target):
        at = y_at[0]
        y_at[0] += 1
        copy = remote(source, target, y_send.at[at], y_recv.at[at], place.y_peer)
        copy.start()
        return copy

    c_at = [0]

    def c_copy(source, target):
        at = c_at[0]
        c_at[0] += 1
        return remote(source, target, c_send.at[at], c_recv.at[at], place.c_peer)

    chunk = rows // SPLIT

    def send_rows(buffer, at):
        return y_copy(
            buffer.at[pl.ds(at * chunk, chunk), :],
            buffer.at[pl.ds(rows + at * chunk, chunk), :],
        )

    def send_part(at):
        view = pl.ds(at * chunk, chunk)
        return y_copy(tx.at[view, :], rx.at[view, :])

    load(1, "back_out", "wd", "slope", "wu", "branch", "active", "normed_two", "unit_two", "inv_two")
    load(1, "wm", "mixed", "heads", "lse", "head_mix", "wq")
    grad[...] = grad_in[...].astype(f32)
    vec_grads[...] = jnp.zeros_like(vec_grads)
    lane = lax.broadcasted_iota(jnp.int32, (1, 128), 1) < HEAD_DIM
    pick_row = lax.broadcasted_iota(jnp.int32, (8, 128), 0)
    pick_lane = lax.broadcasted_iota(jnp.int32, (8, 128), 1)
    halves = (
        ((pick_row == 0) & (pick_lane < HEAD_DIM)) | ((pick_row == 1) & (pick_lane >= HEAD_DIM))
    ).astype(bf16)
    firsts = (pick_lane == pick_row * HEAD_DIM).astype(bf16)
    size = 16

    def vector(layer, at):
        return vecs[layer : layer + 1, at * D : (at + 1) * D]

    def note(layer, at, value):
        vec_grads[layer : layer + 1, at * D : (at + 1) * D] += value

    def by_rows(start, count_rows, body, terms):
        def step(at, carry):
            adds = body(pl.ds(aligned(start + at * size, size), size))
            return tuple(old + fold(new) for old, new in zip(carry, adds, strict=True))

        zeros = tuple(jnp.zeros((8, D), f32) for _ in range(terms))
        sums_ = lax.fori_loop(0, count_rows // size, step, zeros)
        return [total(value) for value in sums_]

    def half_tiles(kind):
        return {0: 3, 1: 1, 2: FF // 2 // half, 3: FF // 2 // half}[kind]

    def weight_grad(kind, owner, at):
        owned = pl.ds(aligned(owner * half), half)
        tile = pl.ds(aligned(at * half), half)
        if kind == 0:
            return tn(feed[:, owned], triple_back[:, tile])
        if kind == 1:
            return tn(mixed[...], back_branch[:, owned])
        if kind == 2:
            return tn(feed[:, owned], slope[:, tile])
        return tn(active[:, tile], back_out[:, owned])

    def spot_of(kind, at):
        tile = pl.ds(aligned(at * half), half)
        return (tile, slice(None)) if kind == 3 else (slice(None), tile)

    half_copies = {}

    def produce_other(layer, kind):
        target = sums[kind]
        buffer = {
            0: half_tx[0].at[:, pl.ds(0, 3 * half)],
            1: half_tx[0].at[:, pl.ds(3 * half, half)],
            2: half_tx[0],
            3: half_tx[1],
        }[kind]

        def step(at, carry):
            buffer[spot_of(kind, at)] = weight_grad(kind, 1 - col, at).astype(bf16)
            return carry

        lax.fori_loop(0, half_tiles(kind), step, 0)
        copy = c_copy(buffer, target)
        copy.start()
        half_copies[kind] = copy

    def produce_own(layer, kind):
        target = sums[kind]
        half_copies.pop(kind).wait()

        def step(at, carry):
            here = spot_of(kind, at)
            value = weight_grad(kind, col, at) + target[here].astype(f32)
            target[here] = value.astype(bf16)
            return carry

        lax.fori_loop(0, half_tiles(kind), step, 0)
        scatter.x_start(layer, kind)

    def out_rows(layer, start, count_rows):
        def body(here):
            value = grad[here, :]
            back = (vector(layer, 13) * value).astype(bf16)
            back_out[here, :] = back
            return (value * aside[here, :], back.astype(f32))

        for at, value in zip((13, 12), by_rows(start, count_rows, body, 2), strict=True):
            note(layer, at, value)

    def last_rows(layer, start, count_rows):
        def body(here):
            value = aside[here, :] + rx_out[here, :].astype(f32) + vector(layer, 12)
            result = part[here, :] + vector(layer, 13) * value
            back_out[here, :] = result.astype(bf16)
            gradient = grad_in[here, :].astype(f32)
            back = (vector(layer, 13) * gradient).astype(bf16)
            return (gradient * value, back.astype(f32))

        for at, value in zip((13, 12), by_rows(start, count_rows, body, 2), strict=True):
            note(layer, at, value)

    def shrink(start, count_rows, target, target_at):
        def step(at, carry):
            lanes = pl.ds(aligned(at * half), half)
            value = nn(active[start : start + count_rows, :], wd[:, lanes])
            target[pl.ds(target_at, count_rows), lanes] = value.astype(target.dtype)
            return carry

        lax.fori_loop(0, 2, step, 0)

    for layer in reversed(range(LAYERS)):
        last = layer == LAYERS - 1
        if last:
            loaded("back_out")
        else:
            load(0, "branch")
            scatter.z_finish(1, 3)
            scatter.z_finish(1, 2)
        loaded("slope", "wd")

        def inner_rows(start, count_rows):
            def step(at, carry):
                lanes = pl.ds(aligned(at * half), half)
                value = nt(back_out[start : start + count_rows, :], wd[lanes, :])
                back = (value * slope[start : start + count_rows, lanes].astype(f32)).astype(bf16)
                slope[start : start + count_rows, lanes] = back
                there = pl.ds(aligned(8 * D + row * (FF // 2) + at * half), half)
                old = vec_grads[layer : layer + 1, there]
                vec_grads[layer : layer + 1, there] = old + total(back.astype(f32))
                return carry

            lax.fori_loop(0, FF // 2 // half, step, 0)

        def two_rows(start, count_rows, target, target_at):
            def step(at, carry):
                lanes = pl.ds(aligned(at * half), half)
                value = nt(slope[start : start + count_rows, :], wu[lanes, :])
                target[pl.ds(target_at, count_rows), lanes] = value.astype(target.dtype)
                return carry

            lax.fori_loop(0, 2, step, 0)

        def back_chunk(at):
            start = rows + at * chunk
            inner_rows(start, chunk)
            two_rows(start, chunk, tx, at * chunk)
            return send_part(at)

        if last:
            loaded("wu")
            back_copies = [back_chunk(at) for at in range(SPLIT)]
            inner_rows(0, rows)
        else:
            inner_rows(0, rows)
            loaded("wu")
            scatter.x_finish(1, 1)
            back_copies = []
            for at in range(SPLIT):
                out_copies[at].wait()
                back_copies.append(back_chunk(at))
        two_rows(0, rows, part, 0)
        if not last:
            scatter.x_finish(1, 0)
        loaded("active", "normed_two")
        produce_other(layer, 3)
        produce_other(layer, 2)
        produce_own(layer, 3)
        produce_own(layer, 2)
        load(layer, "normed")
        loaded("unit_two", "inv_two", "branch")

        def middle_rows(here):
            back = part[here, :] + rx[here, :].astype(f32)
            norm = unit[here, :]
            scaled = back * vector(layer, 6)
            first = jnp.sum(scaled, 1, keepdims=True) * (1.0 / D)
            second = jnp.sum(scaled * norm, 1, keepdims=True) * (1.0 / D)
            scale = inverse[here, 0:1]
            value = grad[here, :] + scale * (scaled - first - norm * second)
            grad[here, :] = value
            branch_back = (vector(layer, 5) * value).astype(bf16)
            back_branch[here, :] = branch_back
            return (back * norm, back, value * aside[here, :], branch_back.astype(f32))

        copies = []
        for at in range(SPLIT):
            back_copies[at].wait()
            terms = by_rows(at * chunk, chunk, middle_rows, 4)
            copies.append(send_rows(back_branch, at))
            for spot_at, value in zip((6, 7, 5, 4), terms, strict=True):
                note(layer, spot_at, value)
        load(layer, "unit_one", "inv_one")
        loaded("wm")

        def mixed_rows(start, count_rows):
            for owner in range(2):
                lanes = slice(owner * width, owner * width + width)
                value = nt(back_branch[start : start + count_rows, :], wm[lanes, :]).astype(bf16)

                @pl.when(owner == col)
                def _():
                    head_back[pl.ds(aligned(col * group + start, 16), count_rows), :] = value

                @pl.when(owner != col)
                def _():
                    head_tx[start : start + count_rows, :] = value

        core_copies = []

        def send_back(start, count_rows):
            core_copies.append(
                c_copy(
                    head_tx.at[pl.ds(start, count_rows), :],
                    head_back.at[pl.ds(aligned(col * group + start, 16), count_rows), :],
                )
            )
            core_copies[-1].start()

        mixed_rows(0, rows)
        send_back(0, rows)
        if last:
            shrink(rows, rows, tx, 0)
            shrink(0, rows, aside, 0)
            load(0, "wd")
            load(1, "middle")
        for at in range(SPLIT):
            copies[at].wait()
            mixed_rows(rows + at * chunk, chunk)
            send_back(rows + at * chunk, chunk)
        if last:
            last_copies = [
                y_copy(tx.at[view, :], rx_out.at[view, :])
                for view in (pl.ds(at * chunk, chunk) for at in range(SPLIT))
            ]
        loaded("heads", "lse", "head_mix", "mixed")
        if last:
            load(0, "wm")
        else:
            scatter.z_finish(1, 1)
            scatter.z_finish(1, 0)
        for copy in core_copies:
            copy.wait()

        piece = 2 * group // 2
        head_copies = []
        for pair in range(pairs):
            lanes = slice(pair * 128, pair * 128 + 128)
            key_lanes = slice(width + pair * 128, width + pair * 128 + 128)
            value_lanes = slice(2 * width + pair * 128, 2 * width + pair * 128 + 128)
            key_sum[...] = jnp.zeros_like(key_sum)
            value_sum[...] = jnp.zeros_like(value_sum)

            def step(at, carry, lanes=lanes, key_lanes=key_lanes, value_lanes=value_lanes):
                here = pl.ds(aligned(at * 128), 128)
                query = heads[here, lanes] * jnp.asarray(HEAD_DIM**-0.5, bf16)
                back = head_back[here, lanes]
                zero = jnp.zeros_like(query)
                queries = jnp.concatenate(
                    [jnp.where(lane, query, zero), jnp.where(lane, zero, query)], 0
                )
                backs = jnp.concatenate(
                    [jnp.where(lane, back, zero), jnp.where(lane, zero, back)], 0
                )
                logs = flip(firsts, lse[here, lanes])
                logs = jnp.concatenate([logs[0:1], logs[1:2]], 1)
                inner = flip(halves, back.astype(f32) * head_mix[here, lanes].astype(f32))
                inner = jnp.concatenate([inner[0:1], inner[1:2]], 1)
                query_grad = jnp.zeros((256, 128), f32)
                for block in range(2):
                    keys = slice(block * piece, block * piece + piece)
                    key = heads[keys, key_lanes]
                    scores = nt(key, queries)
                    probs = jnp.exp(jnp.minimum(scores - logs, 0.0))
                    back_probs = nt(heads[keys, value_lanes], backs)
                    back_scores = (probs * (back_probs - inner)).astype(bf16)
                    value_sum[keys, :] += nn(probs.astype(bf16), backs)
                    key_sum[keys, :] += nn(back_scores, queries)
                    query_grad = query_grad + tn(back_scores, key)
                query_grad = query_grad * HEAD_DIM**-0.5
                head_grad[here, lanes] = jnp.where(
                    lane, query_grad[:128], query_grad[128:]
                ).astype(bf16)
                return carry

            lax.fori_loop(0, 2 * group // 128, step, 0)
            for owner in range(2):
                edge = owner * rows
                valid = lax.broadcasted_iota(jnp.int32, (rows, 1), 0) < tokens - edge
                for part_at in range(2):
                    here = slice(owner * group + part_at * rows, owner * group + part_at * rows + rows)
                    head_grad[here, key_lanes] = jnp.where(valid, key_sum[here, :], 0.0).astype(bf16)
                    head_grad[here, value_lanes] = jnp.where(valid, value_sum[here, :], 0.0).astype(bf16)
            if pair == pairs - 1:
                if last:
                    scatter.x_finish(1, 2)
            else:
                scatter.x_finish(layer, 3)
            there = pl.ds(aligned((1 - col) * group, 16), group)
            mine = pl.ds(aligned(col * group, 16), group)
            for part_at, source in enumerate((lanes, key_lanes, value_lanes)):
                target = pl.ds(aligned(part_at * half + col * width + pair * 128), 128)
                copy = c_copy(head_grad.at[there, source], triple_back.at[:, target])
                copy.start()
                head_copies.append(copy)
                triple_back[:, target] = head_grad[mine, source]
                if part_at != 1:
                    bias_at = pl.ds(
                        aligned((3 * D if part_at else 2 * D) + row * half + col * width + pair * 128), 128
                    )
                    vec_grads[layer : layer + 1, bias_at] = total(head_grad[:, source].astype(f32))
        if not last:
            scatter.x_finish(0, 2)
        for copy in head_copies:
            copy.wait()
        loaded("wq", "normed")
        if last:
            for copy in last_copies:
                copy.wait()
        if not last:
            produce_other(layer, 0)

        def one_rows(start, count_rows, target, target_at):
            def step(at, carry):
                lanes = pl.ds(aligned(at * half), half)
                value = nt(triple_back[start : start + count_rows, : 3 * half], wq[lanes, :])
                target[pl.ds(target_at, count_rows), lanes] = value.astype(target.dtype)
                return carry

            lax.fori_loop(0, 2, step, 0)

        back_copies = []
        for at in range(SPLIT):
            one_rows(rows + at * chunk, chunk, tx, at * chunk)
            back_copies.append(send_part(at))
        if last:
            produce_other(layer, 1)
            produce_other(layer, 0)
            produce_own(layer, 1)
            produce_own(layer, 0)
            loaded("middle")
            last_rows(layer, 0, rows)
            to_features(
                place, back_out.at[pl.ds(0, rows), :], arrived, block_out, c_send.at[27], c_recv.at[27]
            )
        else:
            produce_own(layer, 0)
            produce_other(layer, 1)
            produce_own(layer, 1)
        one_rows(0, rows, part, 0)
        if last:
            load(0, "slope", "wu", "wq", "output", "normed_two", "active")
            load(0, "mixed", "heads", "lse", "head_mix")
        loaded("unit_one", "inv_one")

        def input_rows(here):
            back = part[here, :] + rx[here, :].astype(f32)
            norm = unit[here, :]
            scaled = back * vector(layer, 0)
            first = jnp.sum(scaled, 1, keepdims=True) * (1.0 / D)
            second = jnp.sum(scaled * norm, 1, keepdims=True) * (1.0 / D)
            scale = inverse[here, 0:1]
            grad[here, :] = grad[here, :] + scale * (scaled - first - norm * second)
            return (back * norm, back)

        if last:
            loaded("output")
        out_copies = []
        for at in range(SPLIT):
            back_copies[at].wait()
            terms = by_rows(at * chunk, chunk, input_rows, 2)
            if last:
                out_rows(0, at * chunk, chunk)
                out_copies.append(send_rows(back_out, at))
            for spot_at, value in zip((0, 1), terms, strict=True):
                note(layer, spot_at, value)
        if last:
            load(0, "unit_two", "inv_two")
    scatter.z_finish(0, 3)
    scatter.z_finish(0, 2)
    to_features(place, grad, aside.at[:, pl.ds(0, half)], grad_out, c_send.at[26], c_recv.at[26])
    scatter.x_finish(0, 0)
    scatter.x_finish(0, 1)
    scatter_vectors(place, vec_grads, packed, spare, spot, vec_out, v_send, v_recv)
    scatter.z_finish(0, 0)
    scatter.z_finish(0, 1)
    scatter.finish()


def backward_call(mesh_count, tokens, grad, vecs, weights, saved, spot_shape):
    rows = padded_rows(tokens)
    group = 2 * rows
    half = D // 2
    width = half // 2
    line = mesh_count // 2
    wide = FF // 2

    def shape(*dims, kind=f32):
        return jax.ShapeDtypeStruct(dims, kind)

    halves = [(half, 3 * half), (half, half), (half, wide), (wide, half)]
    shards = [(dims[0] // mesh_count, dims[1]) for dims in halves]
    results = [(3, shards[0][0], half)] + shards[1:]
    outs = [shape(LAYERS, *dims) for dims in results]
    outs += [shape(tokens, half), shape(*spot_shape), shape(tokens, half, kind=bf16)]
    dma = pltpu.SemaphoreType.DMA
    scratch = [
        pltpu.VMEM((D, 3 * half), bf16),
        pltpu.VMEM((half, D), bf16),
        pltpu.VMEM((D, wide), bf16),
        pltpu.VMEM((wide, D), bf16),
        pltpu.VMEM((group, wide), bf16),
        pltpu.VMEM((group, wide), bf16),
        pltpu.VMEM((group, D), bf16),
        pltpu.VMEM((2 * group, 3 * width), bf16),
        pltpu.VMEM((2 * group, width), f32),
        pltpu.VMEM((2 * group, width), bf16),
        pltpu.VMEM((group, half), bf16),
        pltpu.VMEM((rows, D), f32),
        pltpu.VMEM((rows, D), f32),
        pltpu.VMEM((rows, 128), f32),
        pltpu.VMEM((rows, D), f32),
        pltpu.VMEM((group, D), bf16),
        pltpu.VMEM((group, D), bf16),
        pltpu.VMEM((rows, D), f32),
        pltpu.VMEM((rows, D), bf16),
        pltpu.VMEM((rows, D), bf16),
        pltpu.VMEM((rows, D), bf16),
        pltpu.VMEM((rows, half), bf16),
        pltpu.VMEM((2 * group, width), bf16),
        pltpu.VMEM((group, width), bf16),
        pltpu.VMEM((2 * group, 3 * width), bf16),
        pltpu.VMEM((2 * group, 128), f32),
        pltpu.VMEM((2 * group, 128), f32),
        [pltpu.VMEM(dims, bf16) for dims in halves[2:]],
    ]
    scratch += [pltpu.VMEM(dims, bf16) for dims in halves]
    scratch += [pltpu.VMEM((dims[0] // 2, dims[1]), bf16) for dims in halves]
    scratch += [pltpu.VMEM((line - 1,) + dims, bf16) for dims in shards]
    scratch += [pltpu.VMEM(dims, f32) for dims in results]
    scratch += [
        pltpu.VMEM((LAYERS, 10 * D + FF), f32),
        pltpu.VMEM((line,) + spot_shape, f32),
        pltpu.VMEM((line + 2,) + spot_shape, f32),
        pltpu.VMEM(spot_shape, f32),
        dma((LAYERS * 4 * SPLIT,)),
        dma((LAYERS * 4 * SPLIT,)),
        dma((LAYERS * 13 + 2,)),
        dma((LAYERS * 13 + 2,)),
        dma((GROUPS, line)),
        dma((GROUPS, line)),
        dma((GROUPS, line - 1)),
        dma((GROUPS, line - 1)),
        pltpu.SemaphoreType.REGULAR((KINDS,)),
        pltpu.SemaphoreType.REGULAR((KINDS,)),
        dma((KINDS,)),
        dma((line + 2,)),
        dma((line + 2,)),
        dma((20,)),
    ]
    return pl.pallas_call(
        functools.partial(backward_kernel, mesh_count),
        out_shape=outs,
        in_specs=[WHOLE] * 2 + [ANY] * 20,
        out_specs=[ANY] * 4 + [WHOLE] * 3,
        scratch_shapes=scratch,
        compiler_params=pltpu.CompilerParams(
            collective_id=1, has_side_effects=True, vmem_limit_bytes=63 << 20
        ),
        name="backward",
    )(grad, vecs, *weights, *saved)


def local(
    images,
    cotangent,
    triplet_master,
    triplet_first,
    triplet_second,
    project_master,
    project_first,
    project_second,
    expand_master,
    expand_first,
    expand_second,
    shrink_master,
    shrink_first,
    shrink_second,
    vectors_master,
    vectors_first,
    vectors_second,
):
    count = lax.axis_size("dp")
    row_at = lax.axis_index("row")
    col_at = lax.axis_index("col")
    masters = (triplet_master.transpose(0, 2, 1, 3), project_master, expand_master, shrink_master)
    piece = vectors_master.shape[1]
    line_at = (lax.axis_index("dp") % 2 * 2 + row_at) * 2 + col_at
    spot = jnp.where(
        jnp.arange(8 * piece) // piece == line_at, jnp.tile(vectors_master, (1, 8)), 0.0
    )
    (w_a, w_b, w_c, w_d, _, vectors, *saved, grad_rows, middle) = forward_call(
        count, images, cotangent, spot, masters
    )
    *grads, grad_out, vector_sums, block_out = backward_call(
        count,
        images.shape[0],
        grad_rows,
        vectors,
        (w_a, w_b, w_c, w_d),
        (*saved, middle),
        spot.shape,
    )
    vector_reduced = lax.dynamic_slice_in_dim(vector_sums, line_at * piece, piece, 1)

    outs = []
    states = (
        (triplet_master, triplet_first, triplet_second),
        (project_master, project_first, project_second),
        (expand_master, expand_first, expand_second),
        (shrink_master, shrink_first, shrink_second),
    )
    grads[0] = grads[0].transpose(0, 2, 1, 3)
    for kind, (master, first, second) in enumerate(states):
        outs += adam_step(master, first, second, grads[kind], learn_rate, decay_rate)
    outs += adam_step(
        vectors_master, vectors_first, vectors_second, vector_reduced, vector_rate, 0.0
    )
    return (block_out, grad_out, *outs)


def solution(mesh):
    tokens = P(("dp", "row"), "col")
    triplet = P(None, ("col", "dp"), None, "row")
    narrow = P(None, ("row", "dp"), "col")
    wide = P(None, ("col", "dp"), "row")
    vector = P(None, ("dp", "row", "col"))
    states = (triplet,) * 3 + (narrow,) * 3 + (wide,) * 3 + (narrow,) * 3 + (vector,) * 3
    return jax.shard_map(
        local,
        mesh=mesh,
        in_specs=(tokens, tokens) + states,
        out_specs=(tokens, tokens) + states,
        check_vma=False,
    )
```

```python
import functools

import jax
import jax.numpy as jnp
from jax import lax
from jax.experimental import pallas as pl
from jax.experimental.pallas import tpu as pltpu
from jax.sharding import PartitionSpec as P

D = 1024
HEAD_DIM = 64
FF = 4096
LAYERS = 2
STEP = 10
TILE = 16

norm_epsilon = 1e-06
beta_first = 0.9
beta_second = 0.999
adam_epsilon = 1e-08
learn_rate = 0.02
vector_rate = 0.1
decay_rate = 0.05
bf16 = jnp.bfloat16
f32 = jnp.float32


def contract(left, right, left_dims, right_dims):
    return lax.dot_general(
        left, right, ((left_dims, right_dims), ((), ())), preferred_element_type=f32
    )


def adam_step(master, first, second, grad, rate, decay):
    first_new = beta_first * first + (1.0 - beta_first) * grad
    second_new = beta_second * second + (1.0 - beta_second) * grad * grad
    ratio = (
        first_new
        / (1.0 - beta_first**STEP)
        / (jnp.sqrt(second_new / (1.0 - beta_second**STEP)) + adam_epsilon)
    )
    return (first_new, second_new, master - rate * (ratio + decay * master))


MESH = pl.DeviceIdType.MESH
KINDS = 4
GROUPS = LAYERS * KINDS
WINDOW = 3
TRIGGER = 1.0
LEAD = 25.0
EARLY = 4
SPLIT = 2
ANY = pl.BlockSpec(memory_space=pl.ANY)
WHOLE = pl.BlockSpec(memory_space=pltpu.VMEM)


def nt(left, right):
    return contract(left, right, (1,), (1,))


def nn(left, right):
    return contract(left, right, (1,), (0,))


def tn(left, right):
    return contract(left, right, (0,), (0,))


class Place:
    def __init__(self, count):
        self.count = count
        self.line = count // 2
        self.dp = lax.axis_index("dp")
        self.row = lax.axis_index("row")
        self.col = lax.axis_index("col")
        self.pair = lax.rem(self.dp, 2)
        self.outer = lax.div(self.dp, 2)
        self.x_dp = self.dp + 1 - 2 * self.pair
        self.x_peer = (self.x_dp, self.row, self.col)
        self.y_peer = (self.dp, 1 - self.row, self.col)
        self.c_peer = (self.dp, self.row, 1 - self.col)

    def nearest(self, at):
        inside = (at + 1) // 2 if at % 2 else self.line - at // 2
        return jnp.where(
            self.outer == 0, self.line - at, jnp.where(self.outer == self.line - 1, at, inside)
        )

    def ahead(self, step):
        return lax.rem(self.dp + 2 * step, self.count)

    def behind(self, step):
        return lax.rem(self.dp + self.count - 2 * step, self.count)

    def z_peer(self, step):
        return (self.ahead(step), self.row, self.col)

    def greet(self):
        barrier = pltpu.get_barrier_semaphore()
        peers = [self.z_peer(step) for step in range(1, self.line)]
        peers += [self.x_peer, self.y_peer, self.c_peer]
        for peer in peers:
            pl.semaphore_signal(barrier, inc=1, device_id=peer, device_id_type=MESH)
        pl.semaphore_wait(barrier, len(peers))


def remote(source, target, send, recv, peer):
    return pltpu.make_async_remote_copy(
        source, target, send, recv, device_id=peer, device_id_type=MESH
    )


def aligned(value, by=128):
    return pl.multiple_of(value, by)


def weight_view(kind, ref, layer, place, dp, col):
    if kind in (0, 2):
        size = ref.shape[1] // (2 * place.count)
        return ref.at[layer, pl.ds(aligned((col * place.count + dp) * size, 16), size), :]
    size = ref.shape[1] // place.count
    return ref.at[
        layer,
        pl.ds(aligned(dp * size, 16), size),
        pl.ds(aligned(col * (D // 2)), D // 2),
    ]


def column_view(kind, ref, layer, col):
    if kind in (0, 2):
        return ref.at[layer, pl.ds(aligned(col * (D // 2), 16), D // 2), :]
    return ref.at[layer, :, pl.ds(aligned(col * (D // 2)), D // 2)]


class Gather:
    def __init__(self, place, shards, wholes, far, refs):
        self.place, self.shards, self.wholes, self.far = place, shards, wholes, far
        self.send, self.recv, self.own = refs["send"], refs["recv"], refs["own"]
        self.far_send, self.far_recv = refs["far_send"], refs["far_recv"]

    def view(self, group, dp):
        layer, kind = divmod(group, KINDS)
        return weight_view(kind, self.wholes[kind], layer, self.place, dp, self.place.col)

    def copy(self, group, at, source, target, peer):
        return remote(source, target, self.send.at[group, at], self.recv.at[group, at], peer)

    def shard(self, group):
        layer, kind = divmod(group, KINDS)
        return self.shards[kind].at[layer]

    def line_copy(self, group, step):
        place = self.place
        target = self.view(group, place.dp)
        return self.copy(group, step - 1, self.shard(group), target, place.z_peer(step))

    def pair_copy(self, group, step):
        place = self.place
        view = self.view(group, place.behind(step))
        source = self.shard(group) if isinstance(step, int) else view
        return self.copy(group, place.line - 1 + step, source, view, place.x_peer)

    def core_copy(self, group, step, pair):
        place = self.place
        dp = lax.rem(place.x_dp + place.count - 2 * step, place.count) if pair else place.behind(step)
        view = self.view(group, dp)
        source = view if pair or not isinstance(step, int) else self.shard(group)
        at = 2 * place.line - 1 + pair * place.line + step
        return self.copy(group, at, source, view, place.c_peer)

    def own_copy(self, group):
        return pltpu.make_async_copy(
            self.shard(group), self.view(group, self.place.dp), self.own.at[group]
        )

    def line_out(self, group):
        for at in range(1, self.place.line):
            self.line_copy(group, at).start()

    def own_out(self, group):
        self.pair_copy(group, 0).start()
        self.core_copy(group, 0, 0).start()
        self.own_copy(group).start()

    def line_in(self, group, at):
        step = self.place.nearest(at)
        self.line_copy(group, step).wait_recv()
        self.pair_copy(group, step).start()
        self.core_copy(group, step, 0).start()

    def pair_in(self, group, at):
        step = self.place.nearest(at) if at else 0
        self.pair_copy(group, step).wait_recv()
        self.core_copy(group, step, 1).start()

    def arrive(self, group):
        self.own_copy(group).wait()
        for pair in range(2):
            for step in range(self.place.line):
                self.core_copy(group, step, pair).wait_recv()

    def far_copy(self, layer):
        place = self.place
        return remote(
            column_view(1, self.wholes[1], layer, place.col),
            column_view(1, self.far, layer, place.col),
            self.far_send.at[layer, 0],
            self.far_recv.at[layer, 0],
            place.y_peer,
        )

    def far_core_copy(self, layer):
        view = column_view(1, self.far, layer, self.place.col)
        return remote(
            view, view, self.far_send.at[layer, 1], self.far_recv.at[layer, 1], self.place.c_peer
        )

    def far_start(self, layer):
        self.own_copy(layer * KINDS + 1).wait()
        self.far_copy(layer).start()

    def far_in(self, layer):
        self.far_copy(layer).wait_recv()
        self.far_core_copy(layer).start()

    def far_arrive(self, layer):
        self.far_core_copy(layer).wait_recv()

    def finish(self):
        for group in range(GROUPS):
            for step in range(self.place.line):
                if step:
                    self.line_copy(group, step).wait_send()
                self.pair_copy(group, step).wait_send()
                self.core_copy(group, step, 0).wait_send()
                self.core_copy(group, step, 1).wait_send()
        for layer in range(LAYERS):
            self.far_copy(layer).wait_send()
            self.far_core_copy(layer).wait_send()


class Vectors:
    def __init__(self, place, spot, raw, spare, send, recv):
        self.place, self.spot, self.raw, self.spare = place, spot, raw, spare
        self.send, self.recv = send, recv

    def line_copy(self, step):
        place = self.place
        return remote(
            self.spot,
            self.raw.at[place.outer],
            self.send.at[2 + step],
            self.recv.at[2 + step],
            place.z_peer(step),
        )

    def start(self):
        for step in range(1, self.place.line):
            self.line_copy(step).start()
        self.raw[self.place.outer] = self.spot[...]

    def line_in(self):
        for step in range(1, self.place.line):
            self.line_copy(step).wait()

    def add(self, at, peer):
        copy = remote(self.raw, self.spare.at[at], self.send.at[at], self.recv.at[at], peer)
        copy.start()
        copy.wait()
        self.raw[...] = self.raw[...] + self.spare[at]

    def spread(self, vecs):
        size = self.spot.shape[1]
        for outer in range(self.place.line):
            vecs[:, outer * size : (outer + 1) * size] = self.raw[outer]


def to_tokens(place, values, padded, arrived, target, send, recv):
    rows = arrived.shape[0]
    tokens, half = values.shape
    padded[rows:, :] = jnp.zeros_like(padded[rows:, :])
    padded[:tokens, :] = values[...]
    copy = remote(
        padded.at[pl.ds(aligned((1 - place.col) * rows, 16), rows), :],
        arrived,
        send,
        recv,
        place.c_peer,
    )
    copy.start()
    own = padded[pl.ds(aligned(place.col * rows, 16), rows), :]
    target[:, pl.ds(aligned(place.col * half), half)] = own.astype(target.dtype)
    copy.wait()
    other = pl.ds(aligned((1 - place.col) * half), half)
    target[:, other] = arrived[...].astype(target.dtype)


def to_features(place, values, arrived, target, send, recv):
    rows = values.shape[0]
    tokens, half = target.shape
    copy = remote(
        values.at[:, pl.ds(aligned((1 - place.col) * half), half)], arrived, send, recv, place.c_peer
    )
    copy.start()
    own = values[:, pl.ds(aligned(place.col * half), half)]
    copy.wait()
    other = arrived[...]

    @pl.when(place.col == 0)
    def _():
        target[:rows, :] = own
        target[rows:, :] = other[: tokens - rows]

    @pl.when(place.col == 1)
    def _():
        target[:rows, :] = other
        target[rows:, :] = own[: tokens - rows]


def norm_rows(source, gain, shift, unit, inverse, target, start, rows):
    size = 16

    def step(at, carry):
        place = pl.ds(aligned(start + at * size, size), size)
        values = source[place, :].astype(f32)
        centre = jnp.sum(values, 1, keepdims=True) * (1.0 / D)
        spread = jnp.sum(values * values, 1, keepdims=True) * (1.0 / D) - centre * centre
        scale = lax.rsqrt(spread + norm_epsilon)
        norm = (values - centre) * scale
        unit[place, :] = norm
        inverse[place, :] = jnp.broadcast_to(scale, (size, 128))
        target[place, :] = (norm * gain + shift).astype(bf16)
        return carry

    lax.fori_loop(0, rows // size, step, 0)


def gelu_both(values):
    normal = 0.5 + 0.5 * lax.erf(values * (0.5**0.5))
    density = jnp.exp(-0.5 * values * values) * 0.3989422804014327
    return values * normal, normal + values * density


def forward_kernel(count, *refs):
    (
        images,
        cotangent,
        spot_in,
        master_a,
        master_b,
        master_c,
        master_d,
        w_a,
        w_b,
        w_c,
        w_d,
        w_far,
        vecs_out,
        unit_one_out,
        inv_one_out,
        normed_out,
        heads_out,
        lse_out,
        mixed_out,
        branch_out,
        unit_two_out,
        inv_two_out,
        normed_two_out,
        active_out,
        slope_out,
        output_out,
        head_mix_out,
        back_out_out,
        cotangent_out,
        middle_out,
        shard_a,
        shard_b,
        shard_c,
        shard_d,
        state,
        padded,
        arrived,
        spot,
        spare,
        raw,
        vecs,
        wq,
        wm,
        wu,
        wd,
        wf,
        unit,
        inverse,
        unit_two,
        inverse_two,
        normed,
        normed_two,
        heads_all,
        head_tx,
        head_mix,
        lse,
        mixed_all,
        mixed_far,
        back_out,
        branch,
        output,
        active,
        slope,
        tx,
        rx,
        part,
        g_send,
        g_recv,
        g_own,
        far_send,
        far_recv,
        v_send,
        v_recv,
        y_send,
        y_recv,
        c_send,
        c_recv,
        stage_sem,
        save_sem,
    ) = refs
    tokens = images.shape[0]
    rows = state.shape[0]
    group = 2 * rows
    half = D // 2
    width = half // 2
    place = Place(count)
    row, col = place.row, place.col
    wholes = (w_a, w_b, w_c, w_d)
    gather = Gather(
        place,
        (shard_a, shard_b, shard_c, shard_d),
        wholes,
        w_far,
        {
            "send": g_send,
            "recv": g_recv,
            "own": g_own,
            "far_send": far_send,
            "far_recv": far_recv,
        },
    )
    place.greet()
    spot[...] = spot_in[...]
    vectors = Vectors(place, spot, raw, spare, v_send, v_recv)
    vectors.start()
    cast_done = set()

    def cast(at):
        if at in cast_done or at >= GROUPS:
            return
        cast_done.add(at)
        layer, kind = divmod(at, KINDS)
        if kind == 0:
            for part_at in range(3):
                shard_a[layer, :, part_at * half : (part_at + 1) * half] = master_a[
                    layer, part_at
                ].astype(bf16)
        else:
            source = (master_a, master_b, master_c, master_d)[kind]
            (shard_a, shard_b, shard_c, shard_d)[kind][layer] = source[layer].astype(bf16)

    for at in range(WINDOW):
        cast(at)
        gather.line_out(at)

    plan = []
    due = [4.0]
    for at in range(GROUPS):
        dims = wholes[at % KINDS].shape
        due.append(due[-1] + 1.1 * (dims[1] * dims[2] / 92e3))
    for at in range(GROUPS):
        begin, span = due[at], due[at + 1] - due[at]
        for step in range(1, place.line):
            line_due = begin + span * (0.3 + 0.7 * step / (place.line - 1))
            plan.append((line_due, 1, gather.line_in, (at, step)))
            if at >= EARLY and step == 1:
                plan.append((begin - 5.0, 0.5, gather.own_out, (at,)))
            if at + WINDOW < GROUPS and step == max(1, round(TRIGGER * (place.line - 1))):
                plan.append((line_due, 1.5, gather.line_out, (at + WINDOW,)))
        for step in range(place.line):
            pair_due = begin + span * (0.6 + 0.7 * step / (place.line - 1)) + 2.0
            plan.append((pair_due, 2, gather.pair_in, (at, step)))
    plan.sort(key=lambda item: item[:2])
    last_of = [
        max(
            spot
            for spot, item in enumerate(plan)
            if item[2] == gather.pair_in and item[3] == (at, place.line - 1)
        )
        for at in range(GROUPS)
    ]
    plan_at = [0]

    def advance(until):
        for item in plan[plan_at[0] : until]:
            item[2](*item[3])
        plan_at[0] = max(until, plan_at[0])

    def pump(time):
        advance(sum(1 for item in plan if item[0] <= time + LEAD))

    def ensure(at):
        advance(last_of[at] + 1)

    def pump_step(at, count_steps, begin, step_time):
        for step in range(count_steps):
            until = sum(1 for item in plan if item[0] <= begin + (step + 1) * step_time + LEAD)
            if until > plan_at[0]:
                pl.when(at == step)(functools.partial(advance, until))

    pending = {}

    def settle(*names):
        for name in names:
            if name in pending:
                pending.pop(name).wait()

    def save(name, at, source, target):
        settle(name)
        copy = pltpu.make_async_copy(source, target, save_sem.at[at])
        copy.start()
        pending[name] = copy

    staged = {}
    buffers = (wq, wm, wu, wd)

    def stage(kind, layer):
        at = layer * KINDS + kind
        if kind == 1:
            for pair in range(2):
                for step in range(place.line):
                    gather.core_copy(at, step, pair).wait_recv()
        else:
            gather.arrive(at)
        copy = pltpu.make_async_copy(wholes[kind].at[layer], buffers[kind], stage_sem.at[kind])
        copy.start()
        staged[kind] = copy

    def stage_far(layer):
        gather.far_arrive(layer)
        copy = pltpu.make_async_copy(w_far.at[layer], wf, stage_sem.at[KINDS])
        copy.start()
        staged[KINDS] = copy

    def ready(kind):
        staged.pop(kind).wait()

    y_at = [0]

    def y_copy(source, target):
        at = y_at[0]
        y_at[0] += 1
        copy = remote(source, target, y_send.at[at], y_recv.at[at], place.y_peer)
        copy.start()
        return copy

    c_at = [0]

    def c_copy(source, target):
        at = c_at[0]
        c_at[0] += 1
        copy = remote(source, target, c_send.at[at], c_recv.at[at], place.c_peer)
        copy.start()
        return copy

    chunk = rows // SPLIT

    def send_rows(buffer, at):
        return y_copy(
            buffer.at[pl.ds(at * chunk, chunk), :],
            buffer.at[pl.ds(rows + at * chunk, chunk), :],
        )

    to_tokens(place, images, padded, arrived, state, c_send.at[0], c_recv.at[0])
    c_at[0] = 2
    vectors.line_in()
    vectors.add(0, place.x_peer)
    for at in range(GROUPS):
        cast(at)
    for at in range(EARLY):
        gather.own_out(at)
    vectors.add(1, place.y_peer)
    vectors.add(2, place.c_peer)
    vectors.spread(vecs)
    save("vecs", 11, vecs, vecs_out)

    lane = lax.broadcasted_iota(jnp.int32, (1, 128), 1) < HEAD_DIM
    key_at = lax.broadcasted_iota(jnp.int32, (1, 2 * group), 1)
    late = key_at >= group
    spare_row = tokens - rows
    padding = late & (
        (key_at >= group + spare_row) & (key_at < group + rows) | (key_at >= group + rows + spare_row)
    )
    mask = jnp.where(padding, -1e30, 0.0)
    valid = lax.broadcasted_iota(jnp.int32, (rows, 1), 0) < tokens - col * rows

    def vector(layer, at):
        return vecs[layer : layer + 1, at * D : (at + 1) * D]

    def norm_one(layer, at):
        norm_rows(
            state, vector(layer, 0), vector(layer, 1), unit, inverse, normed, at * chunk, chunk
        )
        return send_rows(normed, at)

    copies = [norm_one(0, at) for at in range(SPLIT)]
    to_tokens(place, cotangent, padded, arrived, branch, c_send.at[1], c_recv.at[1])
    cotangent_out[...] = branch[...].astype(bf16)
    back_out[:rows, :] = (vector(LAYERS - 1, 13) * branch[...]).astype(bf16)
    out_copies = [send_rows(back_out, at) for at in range(SPLIT)]
    for layer in range(LAYERS):
        first = layer == 0
        heads, mixed = heads_all.at[layer], mixed_all.at[layer]
        save("unit", 0, unit, unit_one_out.at[layer])
        save("inverse", 1, inverse, inv_one_out.at[layer])
        if first:
            ensure(0)
            stage(0, 0)
        ready(0)

        def triple(start, size):
            def step(at, carry):
                part_at = lax.rem(at, 3)
                mine = lax.div(at, 3)
                owner = jnp.where(mine == 1, col, 1 - col)
                column = aligned(part_at * half + owner * width)
                value = nn(normed[start : start + size, :], wq[:, pl.ds(column, width)])
                bias_at = aligned(
                    jnp.where(part_at == 2, 3 * D, 2 * D) + row * half + owner * width
                )
                bias = vecs[layer : layer + 1, pl.ds(bias_at, width)]
                bias = bias * jnp.where(part_at == 1, 0.0, 1.0)
                inside = valid[start % rows : start % rows + size]
                value = jnp.where(inside, value + bias, 0.0).astype(bf16)
                lanes = pl.ds(aligned(part_at * width), width)

                @pl.when(mine == 0)
                def _():
                    head_tx[start : start + size, lanes] = value

                @pl.when(mine == 1)
                def _():
                    heads[pl.ds(aligned(col * group + start, 16), size), lanes] = value

                return carry

            lax.fori_loop(0, 6, step, 0)
            return c_copy(
                head_tx.at[pl.ds(start, size), :],
                heads.at[pl.ds(aligned(col * group + start, 16), size), :],
            )

        core_copies = [triple(0, rows)]
        if first:
            ensure(1)
            gather.far_start(0)
            for copy in copies:
                copy.wait()
            core_copies.append(triple(rows, rows))
            pump(33)
        else:
            ensure(5)
            gather.far_start(1)
            stage(1, 1)
            pump(106)
            copies[0].wait()
            core_copies.append(triple(rows, chunk))
            pump(111)
            copies[1].wait()
            core_copies.append(triple(rows + chunk, chunk))
            pump(119)
        save("normed", 2, normed, normed_out.at[layer])
        for copy in core_copies:
            copy.wait()
        save("heads", 3, heads, heads_out.at[layer])
        settle("lse", "head_mix")

        attend_at = [35.0 if first else 121.0]

        def attend(owner, side):
            begin_time = attend_at[0]
            attend_at[0] += 3.4
            tile = rows // 2
            begin = owner * group + side * rows

            def step(at, carry):
                place_rows = pl.ds(aligned(begin + at * tile, 16), tile)
                for pair in range(width // 128):
                    lanes = slice(pair * 128, pair * 128 + 128)
                    query = heads[place_rows, lanes] * jnp.asarray(HEAD_DIM**-0.5, bf16)
                    zero = jnp.zeros_like(query)
                    both = jnp.concatenate(
                        [jnp.where(lane, query, zero), jnp.where(lane, zero, query)], 0
                    )
                    key = heads[:, width + pair * 128 : width + pair * 128 + 128]
                    value = heads[:, 2 * width + pair * 128 : 2 * width + pair * 128 + 128]
                    scores = nt(both, key) + mask
                    peak = jnp.max(scores, 1, keepdims=True)
                    weights = jnp.exp(scores - peak)
                    total = jnp.sum(weights, 1, keepdims=True)
                    result = nn(weights.astype(bf16), value) / total
                    logsum = peak + jnp.log(total)
                    head_mix[place_rows, lanes] = jnp.where(
                        lane, result[:tile], result[tile:]
                    ).astype(bf16)
                    lse[place_rows, lanes] = jnp.where(lane, logsum[:tile], logsum[tile:])
                pump_step(at, rows // tile, begin_time, 1.7)
                return carry

            lax.fori_loop(0, rows // tile, step, 0)
            plan_at[0] = max(plan_at[0], sum(1 for item in plan if item[0] <= attend_at[0] + LEAD))

        my_lanes = pl.ds(aligned(col * width), width)

        def send_mixed(side):
            return c_copy(
                head_mix.at[pl.ds(aligned((1 - col) * group + side * rows, 16), rows), :],
                mixed.at[pl.ds(side * rows, rows), my_lanes],
            )

        def keep_mixed(side):
            mixed[side * rows : side * rows + rows, my_lanes] = head_mix[
                pl.ds(aligned(col * group + side * rows, 16), rows), :
            ]

        attend(1 - col, 1)
        copy = send_mixed(1)
        attend(col, 1)
        keep_mixed(1)
        copy.wait()
        settle("normed_two")
        far_copy = y_copy(mixed.at[pl.ds(rows, rows), :], mixed_far)
        if first:
            stage(1, 0)
        attend(1 - col, 0)
        copy = send_mixed(0)
        gather.far_in(layer)
        attend(col, 0)
        keep_mixed(0)
        copy.wait()
        save("lse", 4, lse, lse_out.at[layer])
        save("head_mix", 14, head_mix, head_mix_out.at[layer])
        save("mixed", 5, mixed, mixed_out.at[layer])
        stage_far(layer)
        ready(1)
        settle("branch", "unit_two", "inverse_two")

        def project(start):
            def step(at, carry):
                lanes = pl.ds(aligned(at * half), half)
                value = nn(mixed[start : start + chunk, :], wm[:, lanes])
                value = value + nn(mixed_far[start : start + chunk, :], wf[:, lanes])
                bias_at = aligned(4 * D + at * half)
                value = value + vecs[layer : layer + 1, pl.ds(bias_at, half)]
                scale = vecs[layer : layer + 1, pl.ds(aligned(5 * D + at * half), half)]
                branch[start : start + chunk, lanes] = value
                state[start : start + chunk, lanes] += scale * value
                return carry

            lax.fori_loop(0, 2, step, 0)

        far_copy.wait()
        ready(KINDS)
        copies = []
        for at in range(SPLIT):
            project(at * chunk)
            norm_rows(
                state,
                vector(layer, 6),
                vector(layer, 7),
                unit_two,
                inverse_two,
                normed_two,
                at * chunk,
                chunk,
            )
            copies.append(send_rows(normed_two, at))
            pump((50 if first else 137) + at * 1.5)
        ensure(2 if first else 6)
        stage(2, layer)
        save("branch", 6, branch, branch_out.at[layer])
        save("unit_two", 7, unit_two, unit_two_out.at[layer])
        save("inverse_two", 8, inverse_two, inv_two_out.at[layer])
        ready(2)
        settle("active", "slope", "normed")

        def expand(start, size, begin_time):
            def step(at, carry):
                lanes = pl.ds(aligned(at * half), half)
                bias_at = aligned(8 * D + row * (FF // 2) + at * half)
                value = nn(normed_two[start : start + size, :], wu[:, lanes])
                value = value + vecs[layer : layer + 1, pl.ds(bias_at, half)]
                act, grad = gelu_both(value)
                active[start : start + size, lanes] = act.astype(bf16)
                slope[start : start + size, lanes] = grad.astype(bf16)
                pump_step(at, FF // 2 // half, begin_time, 0.8)
                return carry

            lax.fori_loop(0, FF // 2 // half, step, 0)
            end = begin_time + FF // 2 // half * 0.8 + LEAD
            plan_at[0] = max(plan_at[0], sum(1 for item in plan if item[0] <= end))

        def shrink(start, size, target, target_at):
            def step(at, carry):
                lanes = pl.ds(aligned(at * half), half)
                value = nn(active[start : start + size, :], wd[:, lanes])
                target[pl.ds(target_at, size), lanes] = value.astype(target.dtype)
                return carry

            lax.fori_loop(0, 2, step, 0)

        def shrink_send(at):
            shrink(rows + at * chunk, chunk, tx, at * chunk)
            view = pl.ds(at * chunk, chunk)
            return y_copy(tx.at[view, :], rx.at[view, :])

        back_copies = []
        if first:
            expand(0, rows, 56.0)
            copies[0].wait()
            expand(rows, chunk, 63.0)
            copies[1].wait()
            expand(rows + chunk, chunk, 71.0)
            ensure(3)
            stage(3, 0)
            ready(3)
            back_copies.append(shrink_send(0))
            back_copies.append(shrink_send(1))
        else:
            expand(0, rows, 139.0)
            for at in range(SPLIT):
                copies[at].wait()
                expand(rows + at * chunk, chunk, 146.0 + 8.0 * at)
        if first:
            shrink(0, rows, part, 0)
        save("normed_two", 9, normed_two, normed_two_out.at[layer])
        save("active", 10, active, active_out.at[layer])
        save("slope", 12, slope, slope_out.at[layer])
        if first:
            pump(87)
        else:
            for copy in out_copies:
                copy.wait()
            save("back_out", 15, back_out, back_out_out)
            save("state", 16, state, middle_out)
            break
        settle("unit", "inverse")
        next_copies = []
        for at in range(SPLIT):
            back_copies[at].wait()
            here = slice(at * chunk, at * chunk + chunk)
            output[here, :] = part[here, :] + rx[here, :].astype(f32) + vector(layer, 12)
            state[here, :] = state[here, :] + vector(layer, 13) * output[here, :]
            next_copies.append(norm_one(1, at))
            if at == 0:
                pump(94)
        save("output", 13, output, output_out)
        ensure(4)
        stage(0, 1)
        copies = next_copies
    ensure(GROUPS - 1)
    gather.arrive(GROUPS - 1)
    gather.finish()
    settle(*list(pending))


def padded_rows(tokens):
    return -(-tokens // (2 * TILE)) * TILE


def forward_call(mesh_count, images, cotangent, spot, masters):
    tokens = images.shape[0]
    rows = padded_rows(tokens)
    group = 2 * rows
    half = D // 2
    width = half // 2
    line = mesh_count // 2

    def shape(*dims, kind=f32):
        return jax.ShapeDtypeStruct(dims, kind)

    outs = [
        shape(LAYERS, D, 3 * half, kind=bf16),
        shape(LAYERS, half, D, kind=bf16),
        shape(LAYERS, D, FF // 2, kind=bf16),
        shape(LAYERS, FF // 2, D, kind=bf16),
        shape(LAYERS, half, D, kind=bf16),
        shape(LAYERS, 10 * D + FF),
        shape(LAYERS, rows, D),
        shape(LAYERS, rows, 128),
        shape(LAYERS, group, D, kind=bf16),
        shape(LAYERS, 2 * group, 3 * width, kind=bf16),
        shape(LAYERS, 2 * group, width),
        shape(LAYERS, group, half, kind=bf16),
        shape(LAYERS, rows, D),
        shape(LAYERS, rows, D),
        shape(LAYERS, rows, 128),
        shape(LAYERS, group, D, kind=bf16),
        shape(LAYERS, group, FF // 2, kind=bf16),
        shape(LAYERS, group, FF // 2, kind=bf16),
        shape(rows, D),
        shape(LAYERS, 2 * group, width, kind=bf16),
        shape(group, D, kind=bf16),
        shape(rows, D, kind=bf16),
        shape(rows, D),
    ]
    dma = pltpu.SemaphoreType.DMA
    scratch = [
        pltpu.VMEM((LAYERS, D // (2 * mesh_count), 3 * half), bf16),
        pltpu.VMEM((LAYERS, half // mesh_count, half), bf16),
        pltpu.VMEM((LAYERS, D // (2 * mesh_count), FF // 2), bf16),
        pltpu.VMEM((LAYERS, FF // 2 // mesh_count, half), bf16),
        pltpu.VMEM((rows, D), f32),
        pltpu.VMEM((group, half), bf16),
        pltpu.VMEM((rows, half), bf16),
        pltpu.VMEM(spot.shape, f32),
        pltpu.VMEM((3, line) + spot.shape, f32),
        pltpu.VMEM((line,) + spot.shape, f32),
        pltpu.VMEM((LAYERS, 10 * D + FF), f32),
        pltpu.VMEM((D, 3 * half), bf16),
        pltpu.VMEM((half, D), bf16),
        pltpu.VMEM((D, FF // 2), bf16),
        pltpu.VMEM((FF // 2, D), bf16),
        pltpu.VMEM((half, D), bf16),
        pltpu.VMEM((rows, D), f32),
        pltpu.VMEM((rows, 128), f32),
        pltpu.VMEM((rows, D), f32),
        pltpu.VMEM((rows, 128), f32),
        pltpu.VMEM((group, D), bf16),
        pltpu.VMEM((group, D), bf16),
        pltpu.VMEM((LAYERS, 2 * group, 3 * width), bf16),
        pltpu.VMEM((group, 3 * width), bf16),
        pltpu.VMEM((2 * group, width), bf16),
        pltpu.VMEM((2 * group, width), f32),
        pltpu.VMEM((LAYERS, group, half), bf16),
        pltpu.VMEM((rows, half), bf16),
        pltpu.VMEM((group, D), bf16),
        pltpu.VMEM((rows, D), f32),
        pltpu.VMEM((rows, D), f32),
        pltpu.VMEM((group, FF // 2), bf16),
        pltpu.VMEM((group, FF // 2), bf16),
        pltpu.VMEM((rows, D), bf16),
        pltpu.VMEM((rows, D), bf16),
        pltpu.VMEM((rows, D), f32),
        dma((GROUPS, 4 * line - 1)),
        dma((GROUPS, 4 * line - 1)),
        dma((GROUPS,)),
        dma((LAYERS, 2)),
        dma((LAYERS, 2)),
        dma((line + 2,)),
        dma((line + 2,)),
        dma((16,)),
        dma((16,)),
        dma((16,)),
        dma((16,)),
        dma((KINDS + 1,)),
        dma((17,)),
    ]
    return pl.pallas_call(
        functools.partial(forward_kernel, mesh_count),
        out_shape=outs,
        in_specs=[WHOLE] * 7,
        out_specs=[ANY] * 21 + [WHOLE] + [ANY],
        scratch_shapes=scratch,
        compiler_params=pltpu.CompilerParams(
            collective_id=0, has_side_effects=True, vmem_limit_bytes=60 << 20
        ),
        name="forward",
    )(images, cotangent, spot, *masters)


def fold(values):
    return jnp.sum(values.reshape(-1, 8, values.shape[-1]), 0)


def total(values):
    return jnp.sum(values, 0, keepdims=True)


def flip(picks, values):
    high = values.astype(bf16)
    rest = values - high.astype(f32)
    middle = rest.astype(bf16)
    low = (rest - middle.astype(f32)).astype(bf16)
    return nt(picks, high) + nt(picks, middle) + nt(picks, low)


class Scatter:
    def __init__(self, place, sums, pair_rx, line_rx, outs, refs):
        self.place, self.sums, self.pair_rx, self.line_rx = place, sums, pair_rx, line_rx
        self.outs, self.result = outs, refs["result"]
        self.x_send, self.x_recv = refs["x_send"], refs["x_recv"]
        self.z_send, self.z_recv = refs["z_send"], refs["z_recv"]
        self.x_free, self.z_free, self.out_sem = refs["x_free"], refs["z_free"], refs["out_sem"]
        self.writing = {}

    def size(self, kind):
        return self.sums[kind].shape[0] // self.place.count

    def block(self, kind, dp):
        size = self.size(kind)
        return pl.ds(aligned(dp * size, 16), size)

    def x_copy(self, layer, kind, outer):
        place = self.place
        size = self.size(kind)
        at = layer * KINDS + kind
        return remote(
            self.sums[kind].at[self.block(kind, 2 * outer + 1 - place.pair), :],
            self.pair_rx[kind].at[pl.ds(outer * size, size), :],
            self.x_send.at[at, outer],
            self.x_recv.at[at, outer],
            place.x_peer,
        )

    def z_copy(self, layer, kind, outer):
        place = self.place
        size = self.size(kind)
        at = layer * KINDS + kind
        step = lax.rem(outer - place.outer + place.line, place.line)
        return remote(
            self.pair_rx[kind].at[pl.ds(aligned(outer * size, 16), size), :],
            self.line_rx[kind].at[step - 1],
            self.z_send.at[at, step - 1],
            self.z_recv.at[at, step - 1],
            (2 * outer + place.pair, place.row, place.col),
        )

    def x_start(self, layer, kind):
        if layer < LAYERS - 1:
            pl.semaphore_wait(self.x_free.at[kind], 1)
        for outer in range(self.place.line):
            self.x_copy(layer, kind, outer).start()

    def x_finish(self, layer, kind):
        place = self.place
        size = self.size(kind)
        rows = min(size, 64)
        if layer < LAYERS - 1:
            pl.semaphore_wait(self.z_free.at[kind], place.line - 1)
        for outer in range(place.line):
            self.x_copy(layer, kind, outer).wait()

            def step(at, carry, outer=outer):
                here = pl.ds(aligned(outer * size + at * rows, 16), rows)
                own = pl.ds(aligned((2 * outer + place.pair) * size + at * rows, 16), rows)
                pair_rx = self.pair_rx[kind]
                value = pair_rx[here, :].astype(f32) + self.sums[kind][own, :].astype(f32)
                pair_rx[here, :] = value.astype(bf16)
                return carry

            lax.fori_loop(0, size // rows, step, 0)

            @pl.when(place.outer != outer)
            def _(outer=outer):
                self.z_copy(layer, kind, outer).start()

    def z_finish(self, layer, kind):
        place = self.place
        size = self.size(kind)
        for step_at in range(1, place.line):
            self.z_copy(layer, kind, lax.rem(place.outer + step_at, place.line)).wait()
        if kind in self.writing:
            self.writing.pop(kind).wait()
        rows = min(size, 64)

        def step(at, carry):
            here = pl.ds(aligned(at * rows, 16), rows)
            own = pl.ds(aligned(place.outer * size + at * rows, 16), rows)
            value = self.pair_rx[kind][own, :].astype(f32)
            for step_at in range(place.line - 1):
                value = value + self.line_rx[kind][step_at, here, :].astype(f32)
            if kind == 0:
                third = value.shape[1] // 3
                for part_at in range(3):
                    self.result[kind][part_at, here, :] = value[:, part_at * third : (part_at + 1) * third]
            else:
                self.result[kind][here, :] = value
            return carry

        lax.fori_loop(0, size // rows, step, 0)
        copy = pltpu.make_async_copy(
            self.result[kind], self.outs[kind].at[layer], self.out_sem.at[kind]
        )
        copy.start()
        self.writing[kind] = copy
        if layer == LAYERS - 1:
            pl.semaphore_signal(
                self.x_free.at[kind], inc=1, device_id=place.x_peer, device_id_type=MESH
            )
            for step_at in range(1, place.line):
                pl.semaphore_signal(
                    self.z_free.at[kind],
                    inc=1,
                    device_id=place.z_peer(step_at),
                    device_id_type=MESH,
                )

    def finish(self):
        for copy in self.writing.values():
            copy.wait()


def scatter_vectors(place, grads, packed, spare, spot, target, send, recv):
    size = spot.shape[1]
    for outer in range(place.line):
        packed[outer] = grads[:, outer * size : (outer + 1) * size]
    copies = []
    for step in range(1, place.line):
        outer = lax.rem(place.outer + step, place.line)
        copy = remote(
            packed.at[outer], spare.at[2 + step], send.at[2 + step], recv.at[2 + step], place.z_peer(step)
        )
        copy.start()
        copies.append(copy)
    for copy in copies:
        copy.wait()
    value = packed[place.outer]
    for step in range(1, place.line):
        value = value + spare[2 + step]
    spot[...] = value
    for at, peer in enumerate((place.x_peer, place.y_peer, place.c_peer)):
        copy = remote(spot, spare.at[at], send.at[at], recv.at[at], peer)
        copy.start()
        copy.wait()
        spot[...] = spot[...] + spare[at]
    target[...] = spot[...]


def backward_kernel(count, *refs):
    (
        grad_in,
        vecs,
        w_a,
        w_b,
        w_c,
        w_d,
        w_far,
        unit_one_in,
        inv_one_in,
        normed_in,
        heads_in,
        lse_in,
        mixed_in,
        branch_in,
        unit_two_in,
        inv_two_in,
        normed_two_in,
        active_in,
        slope_in,
        output_in,
        head_mix_in,
        back_out_in,
        middle_in,
        grad_a,
        grad_b,
        grad_c,
        grad_d,
        grad_out,
        vec_out,
        block_out,
        wq,
        wm,
        wu,
        wd,
        wf,
        far_tx,
        far_rx,
        active,
        slope,
        feed,
        heads,
        lse,
        head_mix,
        mixed,
        aside,
        unit,
        inverse,
        grad,
        back_out,
        back_branch,
        part,
        tx,
        rx,
        rx_out,
        arrived,
        head_back,
        head_tx,
        head_grad,
        key_sum,
        value_sum,
        half_tx,
        sum_a,
        sum_b,
        sum_c,
        sum_d,
        pair_a,
        pair_b,
        pair_c,
        pair_d,
        line_a,
        line_b,
        line_c,
        line_d,
        result_a,
        result_b,
        result_c,
        result_d,
        vec_grads,
        packed,
        spare,
        spot,
        y_send,
        y_recv,
        c_send,
        c_recv,
        x_send,
        x_recv,
        z_send,
        z_recv,
        x_free,
        z_free,
        out_sem,
        v_send,
        v_recv,
        load_sem,
    ) = refs
    tokens = grad_out.shape[0]
    rows = grad_in.shape[0]
    group = 2 * rows
    half = D // 2
    width = half // 2
    pairs = width // 128
    place = Place(count)
    row, col = place.row, place.col
    sums = (sum_a, sum_b, sum_c, sum_d)
    place.greet()
    scatter = Scatter(
        place,
        sums,
        (pair_a, pair_b, pair_c, pair_d),
        (line_a, line_b, line_c, line_d),
        (grad_a, grad_b, grad_c, grad_d),
        {
            "result": (result_a, result_b, result_c, result_d),
            "x_send": x_send,
            "x_recv": x_recv,
            "z_send": z_send,
            "z_recv": z_recv,
            "x_free": x_free,
            "z_free": z_free,
            "out_sem": out_sem,
        },
    )
    triple_back = active

    sources = {
        "wd": (w_d, wd),
        "wu": (w_c, wu),
        "wm": (w_b, wm),
        "wf": (w_far, wf),
        "wq": (w_a, wq),
        "slope": (slope_in, slope),
        "active": (active_in, active),
        "normed_two": (normed_two_in, feed),
        "normed": (normed_in, feed),
        "output": (output_in, aside),
        "branch": (branch_in, aside),
        "unit_two": (unit_two_in, unit),
        "unit_one": (unit_one_in, unit),
        "inv_two": (inv_two_in, inverse),
        "inv_one": (inv_one_in, inverse),
        "heads": (heads_in, heads),
        "lse": (lse_in, lse),
        "head_mix": (head_mix_in, head_mix),
        "mixed": (mixed_in, mixed),
        "back_out": (back_out_in, back_out),
        "middle": (middle_in, part),
    }
    names = list(sources)
    loading = {}

    def load(layer, *wanted):
        for name in wanted:
            source, buffer = sources[name]
            if name not in ("back_out", "output", "middle"):
                source = source.at[layer]
            copy = pltpu.make_async_copy(source, buffer, load_sem.at[names.index(name)])
            copy.start()
            loading[name] = copy

    def loaded(*wanted):
        for name in wanted:
            loading.pop(name).wait()

    y_at = [0]

    def y_copy(source, target):
        at = y_at[0]
        y_at[0] += 1
        copy = remote(source, target, y_send.at[at], y_recv.at[at], place.y_peer)
        copy.start()
        return copy

    c_at = [0]

    def c_copy(source, target):
        at = c_at[0]
        c_at[0] += 1
        return remote(source, target, c_send.at[at], c_recv.at[at], place.c_peer)

    chunk = rows // SPLIT

    def send_rows(buffer, at):
        return y_copy(
            buffer.at[pl.ds(at * chunk, chunk), :],
            buffer.at[pl.ds(rows + at * chunk, chunk), :],
        )

    def send_part(at):
        view = pl.ds(at * chunk, chunk)
        return y_copy(tx.at[view, :], rx.at[view, :])

    load(1, "back_out", "wd", "slope", "wu", "branch", "active", "normed_two", "unit_two", "inv_two")
    load(1, "wf", "wm", "mixed", "heads", "lse", "head_mix", "wq")
    grad[...] = grad_in[...].astype(f32)
    vec_grads[...] = jnp.zeros_like(vec_grads)
    lane = lax.broadcasted_iota(jnp.int32, (1, 128), 1) < HEAD_DIM
    pick_row = lax.broadcasted_iota(jnp.int32, (8, 128), 0)
    pick_lane = lax.broadcasted_iota(jnp.int32, (8, 128), 1)
    halves = (
        ((pick_row == 0) & (pick_lane < HEAD_DIM)) | ((pick_row == 1) & (pick_lane >= HEAD_DIM))
    ).astype(bf16)
    firsts = (pick_lane == pick_row * HEAD_DIM).astype(bf16)
    size = 16

    def vector(layer, at):
        return vecs[layer : layer + 1, at * D : (at + 1) * D]

    def note(layer, at, value):
        vec_grads[layer : layer + 1, at * D : (at + 1) * D] += value

    def by_rows(start, count_rows, body, terms):
        def step(at, carry):
            adds = body(pl.ds(aligned(start + at * size, size), size))
            return tuple(old + fold(new) for old, new in zip(carry, adds, strict=True))

        zeros = tuple(jnp.zeros((8, D), f32) for _ in range(terms))
        sums_ = lax.fori_loop(0, count_rows // size, step, zeros)
        return [total(value) for value in sums_]

    def half_tiles(kind):
        return {0: 3, 1: 1, 2: FF // 2 // half, 3: FF // 2 // half}[kind]

    def weight_grad(kind, owner, at):
        owned = pl.ds(aligned(owner * half), half)
        tile = pl.ds(aligned(at * half), half)
        if kind == 0:
            return tn(feed[:, owned], triple_back[:, tile])
        if kind == 1:
            return tn(mixed[...], back_branch[:, owned])
        if kind == 2:
            return tn(feed[:, owned], slope[:, tile])
        return tn(active[:, tile], back_out[:, owned])

    def spot_of(kind, at):
        tile = pl.ds(aligned(at * half), half)
        return (tile, slice(None)) if kind == 3 else (slice(None), tile)

    half_copies = {}

    def produce_other(layer, kind):
        target = sums[kind]
        buffer = {
            0: half_tx[0].at[:, pl.ds(0, 3 * half)],
            1: half_tx[0].at[:, pl.ds(3 * half, half)],
            2: half_tx[0],
            3: half_tx[1],
        }[kind]

        def step(at, carry):
            buffer[spot_of(kind, at)] = weight_grad(kind, 1 - col, at).astype(bf16)
            return carry

        lax.fori_loop(0, half_tiles(kind), step, 0)
        copy = c_copy(buffer, target)
        copy.start()
        half_copies[kind] = copy

    def produce_own(layer, kind):
        target = sums[kind]
        half_copies.pop(kind).wait()

        def step(at, carry):
            here = spot_of(kind, at)
            value = weight_grad(kind, col, at) + target[here].astype(f32)
            target[here] = value.astype(bf16)
            return carry

        lax.fori_loop(0, half_tiles(kind), step, 0)
        scatter.x_start(layer, kind)

    def out_rows(layer, start, count_rows):
        def body(here):
            value = grad[here, :]
            back = (vector(layer, 13) * value).astype(bf16)
            back_out[here, :] = back
            return (value * aside[here, :], back.astype(f32))

        for at, value in zip((13, 12), by_rows(start, count_rows, body, 2), strict=True):
            note(layer, at, value)

    def last_rows(layer, start, count_rows):
        def body(here):
            value = aside[here, :] + rx_out[here, :].astype(f32) + vector(layer, 12)
            result = part[here, :] + vector(layer, 13) * value
            back_out[here, :] = result.astype(bf16)
            gradient = grad_in[here, :].astype(f32)
            back = (vector(layer, 13) * gradient).astype(bf16)
            return (gradient * value, back.astype(f32))

        for at, value in zip((13, 12), by_rows(start, count_rows, body, 2), strict=True):
            note(layer, at, value)

    def shrink(start, count_rows, target, target_at):
        def step(at, carry):
            lanes = pl.ds(aligned(at * half), half)
            value = nn(active[start : start + count_rows, :], wd[:, lanes])
            target[pl.ds(target_at, count_rows), lanes] = value.astype(target.dtype)
            return carry

        lax.fori_loop(0, 2, step, 0)

    for layer in reversed(range(LAYERS)):
        last = layer == LAYERS - 1
        if last:
            loaded("back_out")
        else:
            load(0, "branch")
            scatter.z_finish(1, 3)
            scatter.z_finish(1, 2)
        loaded("slope", "wd")

        def inner_rows(start, count_rows):
            def step(at, carry):
                lanes = pl.ds(aligned(at * half), half)
                value = nt(back_out[start : start + count_rows, :], wd[lanes, :])
                back = (value * slope[start : start + count_rows, lanes].astype(f32)).astype(bf16)
                slope[start : start + count_rows, lanes] = back
                there = pl.ds(aligned(8 * D + row * (FF // 2) + at * half), half)
                old = vec_grads[layer : layer + 1, there]
                vec_grads[layer : layer + 1, there] = old + total(back.astype(f32))
                return carry

            lax.fori_loop(0, FF // 2 // half, step, 0)

        def two_rows(start, count_rows, target, target_at):
            def step(at, carry):
                lanes = pl.ds(aligned(at * half), half)
                value = nt(slope[start : start + count_rows, :], wu[lanes, :])
                target[pl.ds(target_at, count_rows), lanes] = value.astype(target.dtype)
                return carry

            lax.fori_loop(0, 2, step, 0)

        def back_chunk(at):
            start = rows + at * chunk
            inner_rows(start, chunk)
            two_rows(start, chunk, tx, at * chunk)
            return send_part(at)

        if last:
            loaded("wu")
            back_copies = [back_chunk(at) for at in range(SPLIT)]
            inner_rows(0, rows)
        else:
            inner_rows(0, rows)
            loaded("wu")
            scatter.x_finish(1, 1)
            back_copies = []
            for at in range(SPLIT):
                out_copies[at].wait()
                back_copies.append(back_chunk(at))
        two_rows(0, rows, part, 0)
        if not last:
            scatter.x_finish(1, 0)
        loaded("active", "normed_two")
        produce_other(layer, 3)
        produce_other(layer, 2)
        produce_own(layer, 3)
        loaded("unit_two", "inv_two", "branch", "wf")

        def far_rows(at):
            here = slice(at * chunk, at * chunk + chunk)
            far_tx[here, :] = nt(back_branch[here, :], wf[...]).astype(bf16)
            return y_copy(
                far_tx.at[pl.ds(at * chunk, chunk), :], far_rx.at[pl.ds(at * chunk, chunk), :]
            )


        def middle_rows(here):
            back = part[here, :] + rx[here, :].astype(f32)
            norm = unit[here, :]
            scaled = back * vector(layer, 6)
            first = jnp.sum(scaled, 1, keepdims=True) * (1.0 / D)
            second = jnp.sum(scaled * norm, 1, keepdims=True) * (1.0 / D)
            scale = inverse[here, 0:1]
            value = grad[here, :] + scale * (scaled - first - norm * second)
            grad[here, :] = value
            branch_back = (vector(layer, 5) * value).astype(bf16)
            back_branch[here, :] = branch_back
            return (back * norm, back, value * aside[here, :], branch_back.astype(f32))

        copies = []
        for at in range(SPLIT):
            back_copies[at].wait()
            terms = by_rows(at * chunk, chunk, middle_rows, 4)
            copies.append(far_rows(at))
            for spot_at, value in zip((6, 7, 5, 4), terms, strict=True):
                note(layer, spot_at, value)
        branch_copies = [send_rows(back_branch, at) for at in range(SPLIT)]
        load(layer, "unit_one", "inv_one")
        if last:
            load(0, "wf")
        loaded("wm")

        def keep_back(owner, start, count_rows, value):
            @pl.when(owner == col)
            def _():
                head_back[pl.ds(aligned(col * group + start, 16), count_rows), :] = value

            @pl.when(owner != col)
            def _():
                head_tx[start : start + count_rows, :] = value

        core_copies = []

        def send_back(start, count_rows):
            core_copies.append(
                c_copy(
                    head_tx.at[pl.ds(start, count_rows), :],
                    head_back.at[pl.ds(aligned(col * group + start, 16), count_rows), :],
                )
            )
            core_copies[-1].start()

        for owner in range(2):
            lanes = slice(owner * width, owner * width + width)
            keep_back(owner, 0, rows, nt(back_branch[:rows, :], wm[lanes, :]).astype(bf16))
        send_back(0, rows)
        produce_own(layer, 2)
        load(layer, "normed")
        if last:
            shrink(rows, rows, tx, 0)
            shrink(0, rows, aside, 0)
            load(0, "wd")
            load(1, "middle")
        for at in range(SPLIT):
            copies[at].wait()
            here = slice(at * chunk, at * chunk + chunk)
            for owner in range(2):
                lanes = slice(owner * width, owner * width + width)
                keep_back(owner, rows + at * chunk, chunk, far_rx[here, lanes])
            send_back(rows + at * chunk, chunk)
        if last:
            last_copies = [
                y_copy(tx.at[view, :], rx_out.at[view, :])
                for view in (pl.ds(at * chunk, chunk) for at in range(SPLIT))
            ]
        loaded("heads", "lse", "head_mix", "mixed")
        if last:
            load(0, "wm")
        else:
            scatter.z_finish(1, 1)
            scatter.z_finish(1, 0)
        for copy in core_copies:
            copy.wait()

        piece = 2 * group // 2
        head_copies = []
        for pair in range(pairs):
            lanes = slice(pair * 128, pair * 128 + 128)
            key_lanes = slice(width + pair * 128, width + pair * 128 + 128)
            value_lanes = slice(2 * width + pair * 128, 2 * width + pair * 128 + 128)
            key_sum[...] = jnp.zeros_like(key_sum)
            value_sum[...] = jnp.zeros_like(value_sum)

            def step(at, carry, lanes=lanes, key_lanes=key_lanes, value_lanes=value_lanes):
                here = pl.ds(aligned(at * 128), 128)
                query = heads[here, lanes] * jnp.asarray(HEAD_DIM**-0.5, bf16)
                back = head_back[here, lanes]
                zero = jnp.zeros_like(query)
                queries = jnp.concatenate(
                    [jnp.where(lane, query, zero), jnp.where(lane, zero, query)], 0
                )
                backs = jnp.concatenate(
                    [jnp.where(lane, back, zero), jnp.where(lane, zero, back)], 0
                )
                logs = flip(firsts, lse[here, lanes])
                logs = jnp.concatenate([logs[0:1], logs[1:2]], 1)
                inner = flip(halves, back.astype(f32) * head_mix[here, lanes].astype(f32))
                inner = jnp.concatenate([inner[0:1], inner[1:2]], 1)
                query_grad = jnp.zeros((256, 128), f32)
                for block in range(2):
                    keys = slice(block * piece, block * piece + piece)
                    key = heads[keys, key_lanes]
                    scores = nt(key, queries)
                    probs = jnp.exp(jnp.minimum(scores - logs, 0.0))
                    back_probs = nt(heads[keys, value_lanes], backs)
                    back_scores = (probs * (back_probs - inner)).astype(bf16)
                    value_sum[keys, :] += nn(probs.astype(bf16), backs)
                    key_sum[keys, :] += nn(back_scores, queries)
                    query_grad = query_grad + tn(back_scores, key)
                query_grad = query_grad * HEAD_DIM**-0.5
                head_grad[here, lanes] = jnp.where(
                    lane, query_grad[:128], query_grad[128:]
                ).astype(bf16)
                return carry

            lax.fori_loop(0, 2 * group // 128, step, 0)
            for owner in range(2):
                edge = owner * rows
                valid = lax.broadcasted_iota(jnp.int32, (rows, 1), 0) < tokens - edge
                for part_at in range(2):
                    here = slice(owner * group + part_at * rows, owner * group + part_at * rows + rows)
                    head_grad[here, key_lanes] = jnp.where(valid, key_sum[here, :], 0.0).astype(bf16)
                    head_grad[here, value_lanes] = jnp.where(valid, value_sum[here, :], 0.0).astype(bf16)
            if pair == pairs - 1:
                if last:
                    scatter.x_finish(1, 2)
            else:
                scatter.x_finish(layer, 3)
                for copy in branch_copies:
                    copy.wait()
                produce_other(layer, 1)
                produce_own(layer, 1)
            there = pl.ds(aligned((1 - col) * group, 16), group)
            mine = pl.ds(aligned(col * group, 16), group)
            for part_at, source in enumerate((lanes, key_lanes, value_lanes)):
                target = pl.ds(aligned(part_at * half + col * width + pair * 128), 128)
                copy = c_copy(head_grad.at[there, source], triple_back.at[:, target])
                copy.start()
                head_copies.append(copy)
                triple_back[:, target] = head_grad[mine, source]
                if part_at != 1:
                    bias_at = pl.ds(
                        aligned((3 * D if part_at else 2 * D) + row * half + col * width + pair * 128), 128
                    )
                    vec_grads[layer : layer + 1, bias_at] = total(head_grad[:, source].astype(f32))
        if not last:
            scatter.x_finish(0, 2)
        for copy in head_copies:
            copy.wait()
        loaded("wq", "normed")
        if last:
            for copy in last_copies:
                copy.wait()
        if not last:
            produce_other(layer, 0)

        def one_rows(start, count_rows, target, target_at):
            def step(at, carry):
                lanes = pl.ds(aligned(at * half), half)
                value = nt(triple_back[start : start + count_rows, : 3 * half], wq[lanes, :])
                target[pl.ds(target_at, count_rows), lanes] = value.astype(target.dtype)
                return carry

            lax.fori_loop(0, 2, step, 0)

        back_copies = []
        for at in range(SPLIT):
            one_rows(rows + at * chunk, chunk, tx, at * chunk)
            back_copies.append(send_part(at))
        if last:
            produce_other(layer, 0)
            produce_own(layer, 0)
            loaded("middle")
            last_rows(layer, 0, rows)
            to_features(
                place, back_out.at[pl.ds(0, rows), :], arrived, block_out, c_send.at[27], c_recv.at[27]
            )
        else:
            produce_own(layer, 0)
        one_rows(0, rows, part, 0)
        if last:
            load(0, "slope", "wu", "wq", "output", "normed_two", "active")
            load(0, "mixed", "heads", "lse", "head_mix")
        loaded("unit_one", "inv_one")

        def input_rows(here):
            back = part[here, :] + rx[here, :].astype(f32)
            norm = unit[here, :]
            scaled = back * vector(layer, 0)
            first = jnp.sum(scaled, 1, keepdims=True) * (1.0 / D)
            second = jnp.sum(scaled * norm, 1, keepdims=True) * (1.0 / D)
            scale = inverse[here, 0:1]
            grad[here, :] = grad[here, :] + scale * (scaled - first - norm * second)
            return (back * norm, back)

        if last:
            loaded("output")
        out_copies = []
        for at in range(SPLIT):
            back_copies[at].wait()
            terms = by_rows(at * chunk, chunk, input_rows, 2)
            if last:
                out_rows(0, at * chunk, chunk)
                out_copies.append(send_rows(back_out, at))
            for spot_at, value in zip((0, 1), terms, strict=True):
                note(layer, spot_at, value)
        if last:
            load(0, "unit_two", "inv_two")
    scatter.z_finish(0, 3)
    scatter.z_finish(0, 2)
    to_features(place, grad, aside.at[:, pl.ds(0, half)], grad_out, c_send.at[26], c_recv.at[26])
    scatter.x_finish(0, 1)
    scatter.x_finish(0, 0)
    scatter_vectors(place, vec_grads, packed, spare, spot, vec_out, v_send, v_recv)
    scatter.z_finish(0, 1)
    scatter.z_finish(0, 0)
    scatter.finish()


def backward_call(mesh_count, tokens, grad, vecs, weights, saved, spot_shape):
    rows = padded_rows(tokens)
    group = 2 * rows
    half = D // 2
    width = half // 2
    line = mesh_count // 2
    wide = FF // 2

    def shape(*dims, kind=f32):
        return jax.ShapeDtypeStruct(dims, kind)

    halves = [(half, 3 * half), (half, half), (half, wide), (wide, half)]
    shards = [(dims[0] // mesh_count, dims[1]) for dims in halves]
    results = [(3, shards[0][0], half)] + shards[1:]
    outs = [shape(LAYERS, *dims) for dims in results]
    outs += [shape(tokens, half), shape(*spot_shape), shape(tokens, half, kind=bf16)]
    dma = pltpu.SemaphoreType.DMA
    scratch = [
        pltpu.VMEM((D, 3 * half), bf16),
        pltpu.VMEM((half, D), bf16),
        pltpu.VMEM((D, wide), bf16),
        pltpu.VMEM((wide, D), bf16),
        pltpu.VMEM((half, D), bf16),
        pltpu.VMEM((rows, half), bf16),
        pltpu.VMEM((rows, half), bf16),
        pltpu.VMEM((group, wide), bf16),
        pltpu.VMEM((group, wide), bf16),
        pltpu.VMEM((group, D), bf16),
        pltpu.VMEM((2 * group, 3 * width), bf16),
        pltpu.VMEM((2 * group, width), f32),
        pltpu.VMEM((2 * group, width), bf16),
        pltpu.VMEM((group, half), bf16),
        pltpu.VMEM((rows, D), f32),
        pltpu.VMEM((rows, D), f32),
        pltpu.VMEM((rows, 128), f32),
        pltpu.VMEM((rows, D), f32),
        pltpu.VMEM((group, D), bf16),
        pltpu.VMEM((group, D), bf16),
        pltpu.VMEM((rows, D), f32),
        pltpu.VMEM((rows, D), bf16),
        pltpu.VMEM((rows, D), bf16),
        pltpu.VMEM((rows, D), bf16),
        pltpu.VMEM((rows, half), bf16),
        pltpu.VMEM((2 * group, width), bf16),
        pltpu.VMEM((group, width), bf16),
        pltpu.VMEM((2 * group, 3 * width), bf16),
        pltpu.VMEM((2 * group, 128), f32),
        pltpu.VMEM((2 * group, 128), f32),
        [pltpu.VMEM(dims, bf16) for dims in halves[2:]],
    ]
    scratch += [pltpu.VMEM(dims, bf16) for dims in halves]
    scratch += [pltpu.VMEM((dims[0] // 2, dims[1]), bf16) for dims in halves]
    scratch += [pltpu.VMEM((line - 1,) + dims, bf16) for dims in shards]
    scratch += [pltpu.VMEM(dims, f32) for dims in results]
    scratch += [
        pltpu.VMEM((LAYERS, 10 * D + FF), f32),
        pltpu.VMEM((line,) + spot_shape, f32),
        pltpu.VMEM((line + 2,) + spot_shape, f32),
        pltpu.VMEM(spot_shape, f32),
        dma((24,)),
        dma((24,)),
        dma((LAYERS * 13 + 2,)),
        dma((LAYERS * 13 + 2,)),
        dma((GROUPS, line)),
        dma((GROUPS, line)),
        dma((GROUPS, line - 1)),
        dma((GROUPS, line - 1)),
        pltpu.SemaphoreType.REGULAR((KINDS,)),
        pltpu.SemaphoreType.REGULAR((KINDS,)),
        dma((KINDS,)),
        dma((line + 2,)),
        dma((line + 2,)),
        dma((21,)),
    ]
    return pl.pallas_call(
        functools.partial(backward_kernel, mesh_count),
        out_shape=outs,
        in_specs=[WHOLE] * 2 + [ANY] * 21,
        out_specs=[ANY] * 4 + [WHOLE] * 3,
        scratch_shapes=scratch,
        compiler_params=pltpu.CompilerParams(
            collective_id=1, has_side_effects=True, vmem_limit_bytes=63 << 20
        ),
        name="backward",
    )(grad, vecs, *weights, *saved)


def local(
    images,
    cotangent,
    triplet_master,
    triplet_first,
    triplet_second,
    project_master,
    project_first,
    project_second,
    expand_master,
    expand_first,
    expand_second,
    shrink_master,
    shrink_first,
    shrink_second,
    vectors_master,
    vectors_first,
    vectors_second,
):
    count = lax.axis_size("dp")
    row_at = lax.axis_index("row")
    col_at = lax.axis_index("col")
    masters = (triplet_master.transpose(0, 2, 1, 3), project_master, expand_master, shrink_master)
    piece = vectors_master.shape[1]
    line_at = (lax.axis_index("dp") % 2 * 2 + row_at) * 2 + col_at
    spot = jnp.where(
        jnp.arange(8 * piece) // piece == line_at, jnp.tile(vectors_master, (1, 8)), 0.0
    )
    (w_a, w_b, w_c, w_d, w_far, vectors, *saved, grad_rows, middle) = forward_call(
        count, images, cotangent, spot, masters
    )
    *grads, grad_out, vector_sums, block_out = backward_call(
        count,
        images.shape[0],
        grad_rows,
        vectors,
        (w_a, w_b, w_c, w_d, w_far),
        (*saved, middle),
        spot.shape,
    )
    vector_reduced = lax.dynamic_slice_in_dim(vector_sums, line_at * piece, piece, 1)

    outs = []
    states = (
        (triplet_master, triplet_first, triplet_second),
        (project_master, project_first, project_second),
        (expand_master, expand_first, expand_second),
        (shrink_master, shrink_first, shrink_second),
    )
    grads[0] = grads[0].transpose(0, 2, 1, 3)
    for kind, (master, first, second) in enumerate(states):
        outs += adam_step(master, first, second, grads[kind], learn_rate, decay_rate)
    outs += adam_step(
        vectors_master, vectors_first, vectors_second, vector_reduced, vector_rate, 0.0
    )
    return (block_out, grad_out, *outs)


def solution(mesh):
    tokens = P(("dp", "row"), "col")
    triplet = P(None, ("col", "dp"), None, "row")
    narrow = P(None, ("row", "dp"), "col")
    wide = P(None, ("col", "dp"), "row")
    vector = P(None, ("dp", "row", "col"))
    states = (triplet,) * 3 + (narrow,) * 3 + (wide,) * 3 + (narrow,) * 3 + (vector,) * 3
    return jax.shard_map(
        local,
        mesh=mesh,
        in_specs=(tokens, tokens) + states,
        out_specs=(tokens, tokens) + states,
        check_vma=False,
    )
```

```python
import functools

import jax
import jax.numpy as jnp
from jax import lax
from jax.experimental import pallas as pl
from jax.experimental.pallas import tpu as pltpu
from jax.sharding import PartitionSpec as P

D = 1024
HEAD_DIM = 64
FF = 4096
LAYERS = 2
STEP = 10
TILE = 16

norm_epsilon = 1e-06
beta_first = 0.9
beta_second = 0.999
adam_epsilon = 1e-08
learn_rate = 0.02
vector_rate = 0.1
decay_rate = 0.05
bf16 = jnp.bfloat16
f32 = jnp.float32


def contract(left, right, left_dims, right_dims):
    return lax.dot_general(
        left, right, ((left_dims, right_dims), ((), ())), preferred_element_type=f32
    )


def adam_step(master, first, second, grad, rate, decay):
    first_new = beta_first * first + (1.0 - beta_first) * grad
    second_new = beta_second * second + (1.0 - beta_second) * grad * grad
    ratio = (
        first_new
        / (1.0 - beta_first**STEP)
        / (jnp.sqrt(second_new / (1.0 - beta_second**STEP)) + adam_epsilon)
    )
    return (first_new, second_new, master - rate * (ratio + decay * master))


MESH = pl.DeviceIdType.MESH
KINDS = 4
GROUPS = LAYERS * KINDS
WINDOW = 3
TRIGGER = 1.0
LEAD = 25.0
EARLY = 4
SPLIT = 2
ANY = pl.BlockSpec(memory_space=pl.ANY)
WHOLE = pl.BlockSpec(memory_space=pltpu.VMEM)


def nt(left, right):
    return contract(left, right, (1,), (1,))


def nn(left, right):
    return contract(left, right, (1,), (0,))


def tn(left, right):
    return contract(left, right, (0,), (0,))


class Place:
    def __init__(self, count):
        self.count = count
        self.line = count // 2
        self.dp = lax.axis_index("dp")
        self.row = lax.axis_index("row")
        self.col = lax.axis_index("col")
        self.pair = lax.rem(self.dp, 2)
        self.outer = lax.div(self.dp, 2)
        self.x_dp = self.dp + 1 - 2 * self.pair
        self.x_peer = (self.x_dp, self.row, self.col)
        self.y_peer = (self.dp, 1 - self.row, self.col)
        self.c_peer = (self.dp, self.row, 1 - self.col)

    def nearest(self, at):
        inside = (at + 1) // 2 if at % 2 else self.line - at // 2
        return jnp.where(
            self.outer == 0, self.line - at, jnp.where(self.outer == self.line - 1, at, inside)
        )

    def ahead(self, step):
        return lax.rem(self.dp + 2 * step, self.count)

    def behind(self, step):
        return lax.rem(self.dp + self.count - 2 * step, self.count)

    def z_peer(self, step):
        return (self.ahead(step), self.row, self.col)

    def greet(self):
        barrier = pltpu.get_barrier_semaphore()
        peers = [self.z_peer(step) for step in range(1, self.line)]
        peers += [self.x_peer, self.y_peer, self.c_peer]
        for peer in peers:
            pl.semaphore_signal(barrier, inc=1, device_id=peer, device_id_type=MESH)
        pl.semaphore_wait(barrier, len(peers))


def remote(source, target, send, recv, peer):
    return pltpu.make_async_remote_copy(
        source, target, send, recv, device_id=peer, device_id_type=MESH
    )


def aligned(value, by=128):
    return pl.multiple_of(value, by)


def weight_view(kind, ref, layer, place, dp, col):
    if kind in (0, 2):
        size = ref.shape[1] // (2 * place.count)
        return ref.at[layer, pl.ds(aligned((col * place.count + dp) * size, 16), size), :]
    size = ref.shape[1] // place.count
    return ref.at[
        layer,
        pl.ds(aligned(dp * size, 16), size),
        pl.ds(aligned(col * (D // 2)), D // 2),
    ]


def column_view(kind, ref, layer, col):
    if kind in (0, 2):
        return ref.at[layer, pl.ds(aligned(col * (D // 2), 16), D // 2), :]
    return ref.at[layer, :, pl.ds(aligned(col * (D // 2)), D // 2)]


class Gather:
    def __init__(self, place, shards, wholes, far, refs):
        self.place, self.shards, self.wholes, self.far = place, shards, wholes, far
        self.send, self.recv, self.own = refs["send"], refs["recv"], refs["own"]
        self.far_send, self.far_recv = refs["far_send"], refs["far_recv"]

    def view(self, group, dp):
        layer, kind = divmod(group, KINDS)
        return weight_view(kind, self.wholes[kind], layer, self.place, dp, self.place.col)

    def copy(self, group, at, source, target, peer):
        return remote(source, target, self.send.at[group, at], self.recv.at[group, at], peer)

    def shard(self, group):
        layer, kind = divmod(group, KINDS)
        return self.shards[kind].at[layer]

    def line_copy(self, group, step):
        place = self.place
        target = self.view(group, place.dp)
        return self.copy(group, step - 1, self.shard(group), target, place.z_peer(step))

    def pair_copy(self, group, step):
        place = self.place
        view = self.view(group, place.behind(step))
        source = self.shard(group) if isinstance(step, int) else view
        return self.copy(group, place.line - 1 + step, source, view, place.x_peer)

    def core_copy(self, group, step, pair):
        place = self.place
        dp = lax.rem(place.x_dp + place.count - 2 * step, place.count) if pair else place.behind(step)
        view = self.view(group, dp)
        source = view if pair or not isinstance(step, int) else self.shard(group)
        at = 2 * place.line - 1 + pair * place.line + step
        return self.copy(group, at, source, view, place.c_peer)

    def own_copy(self, group):
        return pltpu.make_async_copy(
            self.shard(group), self.view(group, self.place.dp), self.own.at[group]
        )

    def line_out(self, group):
        for at in range(1, self.place.line):
            self.line_copy(group, at).start()

    def own_out(self, group):
        self.pair_copy(group, 0).start()
        self.core_copy(group, 0, 0).start()
        self.own_copy(group).start()

    def line_in(self, group, at):
        step = self.place.nearest(at)
        self.line_copy(group, step).wait_recv()
        self.pair_copy(group, step).start()
        self.core_copy(group, step, 0).start()

    def pair_in(self, group, at):
        step = self.place.nearest(at) if at else 0
        self.pair_copy(group, step).wait_recv()
        self.core_copy(group, step, 1).start()

    def arrive(self, group):
        self.own_copy(group).wait()
        for pair in range(2):
            for step in range(self.place.line):
                self.core_copy(group, step, pair).wait_recv()

    def far_copy(self, layer):
        place = self.place
        return remote(
            column_view(1, self.wholes[1], layer, place.col),
            column_view(1, self.far, layer, place.col),
            self.far_send.at[layer, 0],
            self.far_recv.at[layer, 0],
            place.y_peer,
        )

    def far_core_copy(self, layer):
        view = column_view(1, self.far, layer, self.place.col)
        return remote(
            view, view, self.far_send.at[layer, 1], self.far_recv.at[layer, 1], self.place.c_peer
        )

    def far_start(self, layer):
        self.own_copy(layer * KINDS + 1).wait()
        self.far_copy(layer).start()

    def far_in(self, layer):
        self.far_copy(layer).wait_recv()
        self.far_core_copy(layer).start()

    def far_arrive(self, layer):
        self.far_core_copy(layer).wait_recv()

    def finish(self):
        for group in range(GROUPS):
            for step in range(self.place.line):
                if step:
                    self.line_copy(group, step).wait_send()
                self.pair_copy(group, step).wait_send()
                self.core_copy(group, step, 0).wait_send()
                self.core_copy(group, step, 1).wait_send()
        for layer in range(LAYERS):
            self.far_copy(layer).wait_send()
            self.far_core_copy(layer).wait_send()


class Vectors:
    def __init__(self, place, spot, raw, spare, send, recv):
        self.place, self.spot, self.raw, self.spare = place, spot, raw, spare
        self.send, self.recv = send, recv

    def line_copy(self, step):
        place = self.place
        return remote(
            self.spot,
            self.raw.at[place.outer],
            self.send.at[2 + step],
            self.recv.at[2 + step],
            place.z_peer(step),
        )

    def start(self):
        for step in range(1, self.place.line):
            self.line_copy(step).start()
        self.raw[self.place.outer] = self.spot[...]

    def line_in(self):
        for step in range(1, self.place.line):
            self.line_copy(step).wait()

    def add(self, at, peer):
        copy = remote(self.raw, self.spare.at[at], self.send.at[at], self.recv.at[at], peer)
        copy.start()
        copy.wait()
        self.raw[...] = self.raw[...] + self.spare[at]

    def spread(self, vecs):
        size = self.spot.shape[1]
        for outer in range(self.place.line):
            vecs[:, outer * size : (outer + 1) * size] = self.raw[outer]


def to_tokens(place, values, padded, arrived, target, send, recv):
    rows = arrived.shape[0]
    tokens, half = values.shape
    padded[rows:, :] = jnp.zeros_like(padded[rows:, :])
    padded[:tokens, :] = values[...]
    copy = remote(
        padded.at[pl.ds(aligned((1 - place.col) * rows, 16), rows), :],
        arrived,
        send,
        recv,
        place.c_peer,
    )
    copy.start()
    own = padded[pl.ds(aligned(place.col * rows, 16), rows), :]
    target[:, pl.ds(aligned(place.col * half), half)] = own.astype(target.dtype)
    copy.wait()
    other = pl.ds(aligned((1 - place.col) * half), half)
    target[:, other] = arrived[...].astype(target.dtype)


def to_features(place, values, arrived, target, send, recv):
    rows = values.shape[0]
    tokens, half = target.shape
    copy = remote(
        values.at[:, pl.ds(aligned((1 - place.col) * half), half)], arrived, send, recv, place.c_peer
    )
    copy.start()
    own = values[:, pl.ds(aligned(place.col * half), half)]
    copy.wait()
    other = arrived[...]

    @pl.when(place.col == 0)
    def _():
        target[:rows, :] = own
        target[rows:, :] = other[: tokens - rows]

    @pl.when(place.col == 1)
    def _():
        target[:rows, :] = other
        target[rows:, :] = own[: tokens - rows]


def norm_rows(source, gain, shift, unit, inverse, target, start, rows):
    size = 16

    def step(at, carry):
        place = pl.ds(aligned(start + at * size, size), size)
        values = source[place, :].astype(f32)
        centre = jnp.sum(values, 1, keepdims=True) * (1.0 / D)
        spread = jnp.sum(values * values, 1, keepdims=True) * (1.0 / D) - centre * centre
        scale = lax.rsqrt(spread + norm_epsilon)
        norm = (values - centre) * scale
        unit[place, :] = norm
        inverse[place, :] = jnp.broadcast_to(scale, (size, 128))
        target[place, :] = (norm * gain + shift).astype(bf16)
        return carry

    lax.fori_loop(0, rows // size, step, 0)


def gelu_both(values):
    normal = 0.5 + 0.5 * lax.erf(values * (0.5**0.5))
    density = jnp.exp(-0.5 * values * values) * 0.3989422804014327
    return values * normal, normal + values * density


def forward_kernel(count, *refs):
    (
        images,
        cotangent,
        spot_in,
        master_a,
        master_b,
        master_c,
        master_d,
        w_a,
        w_b,
        w_c,
        w_d,
        w_far,
        vecs_out,
        unit_one_out,
        inv_one_out,
        normed_out,
        heads_out,
        lse_out,
        mixed_out,
        branch_out,
        unit_two_out,
        inv_two_out,
        normed_two_out,
        active_out,
        slope_out,
        output_out,
        head_mix_out,
        back_out_out,
        cotangent_out,
        middle_out,
        shard_a,
        shard_b,
        shard_c,
        shard_d,
        state,
        padded,
        arrived,
        spot,
        spare,
        raw,
        vecs,
        wq,
        wm,
        wu,
        wd,
        wf,
        unit,
        inverse,
        unit_two,
        inverse_two,
        normed,
        normed_two,
        heads_all,
        head_tx,
        head_mix,
        lse,
        mixed_all,
        mixed_far,
        back_out,
        branch,
        output,
        active,
        slope,
        tx,
        rx,
        part,
        g_send,
        g_recv,
        g_own,
        far_send,
        far_recv,
        v_send,
        v_recv,
        y_send,
        y_recv,
        c_send,
        c_recv,
        stage_sem,
        save_sem,
    ) = refs
    tokens = images.shape[0]
    rows = state.shape[0]
    group = 2 * rows
    half = D // 2
    width = half // 2
    place = Place(count)
    row, col = place.row, place.col
    wholes = (w_a, w_b, w_c, w_d)
    gather = Gather(
        place,
        (shard_a, shard_b, shard_c, shard_d),
        wholes,
        w_far,
        {
            "send": g_send,
            "recv": g_recv,
            "own": g_own,
            "far_send": far_send,
            "far_recv": far_recv,
        },
    )
    place.greet()
    spot[...] = spot_in[...]
    vectors = Vectors(place, spot, raw, spare, v_send, v_recv)
    vectors.start()
    cast_done = set()

    def cast(at):
        if at in cast_done or at >= GROUPS:
            return
        cast_done.add(at)
        layer, kind = divmod(at, KINDS)
        if kind == 0:
            for part_at in range(3):
                shard_a[layer, :, part_at * half : (part_at + 1) * half] = master_a[
                    layer, part_at
                ].astype(bf16)
        else:
            source = (master_a, master_b, master_c, master_d)[kind]
            (shard_a, shard_b, shard_c, shard_d)[kind][layer] = source[layer].astype(bf16)

    for at in range(WINDOW):
        cast(at)
        gather.line_out(at)

    plan = []
    due = [4.0]
    for at in range(GROUPS):
        dims = wholes[at % KINDS].shape
        due.append(due[-1] + 1.1 * (dims[1] * dims[2] / 92e3))
    for at in range(GROUPS):
        begin, span = due[at], due[at + 1] - due[at]
        for step in range(1, place.line):
            line_due = begin + span * (0.3 + 0.7 * step / (place.line - 1))
            plan.append((line_due, 1, gather.line_in, (at, step)))
            if at >= EARLY and step == 1:
                plan.append((begin - 5.0, 0.5, gather.own_out, (at,)))
            if at + WINDOW < GROUPS and step == max(1, round(TRIGGER * (place.line - 1))):
                plan.append((line_due, 1.5, gather.line_out, (at + WINDOW,)))
        for step in range(place.line):
            pair_due = begin + span * (0.6 + 0.7 * step / (place.line - 1)) + 2.0
            plan.append((pair_due, 2, gather.pair_in, (at, step)))
    plan.sort(key=lambda item: item[:2])
    last_of = [
        max(
            spot
            for spot, item in enumerate(plan)
            if item[2] == gather.pair_in and item[3] == (at, place.line - 1)
        )
        for at in range(GROUPS)
    ]
    plan_at = [0]

    def advance(until):
        for item in plan[plan_at[0] : until]:
            item[2](*item[3])
        plan_at[0] = max(until, plan_at[0])

    def pump(time):
        advance(sum(1 for item in plan if item[0] <= time + LEAD))

    def ensure(at):
        advance(last_of[at] + 1)

    def pump_step(at, count_steps, begin, step_time):
        for step in range(count_steps):
            until = sum(1 for item in plan if item[0] <= begin + (step + 1) * step_time + LEAD)
            if until > plan_at[0]:
                pl.when(at == step)(functools.partial(advance, until))

    pending = {}

    def settle(*names):
        for name in names:
            if name in pending:
                pending.pop(name).wait()

    def save(name, at, source, target):
        settle(name)
        copy = pltpu.make_async_copy(source, target, save_sem.at[at])
        copy.start()
        pending[name] = copy

    staged = {}
    buffers = (wq, wm, wu, wd)

    def stage(kind, layer):
        at = layer * KINDS + kind
        if kind == 1:
            for pair in range(2):
                for step in range(place.line):
                    gather.core_copy(at, step, pair).wait_recv()
        else:
            gather.arrive(at)
        copy = pltpu.make_async_copy(wholes[kind].at[layer], buffers[kind], stage_sem.at[kind])
        copy.start()
        staged[kind] = copy

    def stage_far(layer):
        gather.far_arrive(layer)
        copy = pltpu.make_async_copy(w_far.at[layer], wf, stage_sem.at[KINDS])
        copy.start()
        staged[KINDS] = copy

    def ready(kind):
        staged.pop(kind).wait()

    y_at = [0]

    def y_copy(source, target):
        at = y_at[0]
        y_at[0] += 1
        copy = remote(source, target, y_send.at[at], y_recv.at[at], place.y_peer)
        copy.start()
        return copy

    c_at = [0]

    def c_copy(source, target):
        at = c_at[0]
        c_at[0] += 1
        copy = remote(source, target, c_send.at[at], c_recv.at[at], place.c_peer)
        copy.start()
        return copy

    chunk = rows // SPLIT

    def send_rows(buffer, at):
        return y_copy(
            buffer.at[pl.ds(at * chunk, chunk), :],
            buffer.at[pl.ds(rows + at * chunk, chunk), :],
        )

    to_tokens(place, images, padded, arrived, state, c_send.at[0], c_recv.at[0])
    c_at[0] = 2
    vectors.line_in()
    vectors.add(0, place.x_peer)
    for at in range(GROUPS):
        cast(at)
    for at in range(EARLY):
        gather.own_out(at)
    vectors.add(1, place.y_peer)
    vectors.add(2, place.c_peer)
    vectors.spread(vecs)
    save("vecs", 11, vecs, vecs_out)

    lane = lax.broadcasted_iota(jnp.int32, (1, 128), 1) < HEAD_DIM
    key_at = lax.broadcasted_iota(jnp.int32, (1, 2 * group), 1)
    late = key_at >= group
    spare_row = tokens - rows
    padding = late & (
        (key_at >= group + spare_row) & (key_at < group + rows) | (key_at >= group + rows + spare_row)
    )
    mask = jnp.where(padding, -1e30, 0.0)
    valid = lax.broadcasted_iota(jnp.int32, (rows, 1), 0) < tokens - col * rows

    def vector(layer, at):
        return vecs[layer : layer + 1, at * D : (at + 1) * D]

    def norm_one(layer, at):
        norm_rows(
            state, vector(layer, 0), vector(layer, 1), unit, inverse, normed, at * chunk, chunk
        )
        return send_rows(normed, at)

    copies = [norm_one(0, at) for at in range(SPLIT)]
    to_tokens(place, cotangent, padded, arrived, branch, c_send.at[1], c_recv.at[1])
    cotangent_out[...] = branch[...].astype(bf16)
    back_out[:rows, :] = (vector(LAYERS - 1, 13) * branch[...]).astype(bf16)
    out_copies = [send_rows(back_out, at) for at in range(SPLIT)]
    for layer in range(LAYERS):
        first = layer == 0
        heads, mixed = heads_all.at[layer], mixed_all.at[layer]
        save("unit", 0, unit, unit_one_out.at[layer])
        save("inverse", 1, inverse, inv_one_out.at[layer])
        if first:
            ensure(0)
            stage(0, 0)
        ready(0)

        def triple(start, size):
            def step(at, carry):
                part_at = lax.rem(at, 3)
                mine = lax.div(at, 3)
                owner = jnp.where(mine == 1, col, 1 - col)
                column = aligned(part_at * half + owner * width)
                value = nn(normed[start : start + size, :], wq[:, pl.ds(column, width)])
                bias_at = aligned(
                    jnp.where(part_at == 2, 3 * D, 2 * D) + row * half + owner * width
                )
                bias = vecs[layer : layer + 1, pl.ds(bias_at, width)]
                bias = bias * jnp.where(part_at == 1, 0.0, 1.0)
                inside = valid[start % rows : start % rows + size]
                value = jnp.where(inside, value + bias, 0.0).astype(bf16)
                lanes = pl.ds(aligned(part_at * width), width)

                @pl.when(mine == 0)
                def _():
                    head_tx[start : start + size, lanes] = value

                @pl.when(mine == 1)
                def _():
                    heads[pl.ds(aligned(col * group + start, 16), size), lanes] = value

                return carry

            lax.fori_loop(0, 6, step, 0)
            return c_copy(
                head_tx.at[pl.ds(start, size), :],
                heads.at[pl.ds(aligned(col * group + start, 16), size), :],
            )

        core_copies = [triple(0, rows)]
        if first:
            ensure(1)
            gather.far_start(0)
            for copy in copies:
                copy.wait()
            core_copies.append(triple(rows, rows))
            pump(33)
        else:
            ensure(5)
            gather.far_start(1)
            stage(1, 1)
            pump(106)
            copies[0].wait()
            core_copies.append(triple(rows, chunk))
            pump(111)
            copies[1].wait()
            core_copies.append(triple(rows + chunk, chunk))
            pump(119)
        save("normed", 2, normed, normed_out.at[layer])
        for copy in core_copies:
            copy.wait()
        save("heads", 3, heads, heads_out.at[layer])
        settle("lse", "head_mix")

        attend_at = [35.0 if first else 121.0]

        def attend(owner, side):
            begin_time = attend_at[0]
            attend_at[0] += 3.4
            tile = rows // 2
            begin = owner * group + side * rows

            def step(at, carry):
                place_rows = pl.ds(aligned(begin + at * tile, 16), tile)
                for pair in range(width // 128):
                    lanes = slice(pair * 128, pair * 128 + 128)
                    query = heads[place_rows, lanes] * jnp.asarray(HEAD_DIM**-0.5, bf16)
                    zero = jnp.zeros_like(query)
                    both = jnp.concatenate(
                        [jnp.where(lane, query, zero), jnp.where(lane, zero, query)], 0
                    )
                    key = heads[:, width + pair * 128 : width + pair * 128 + 128]
                    value = heads[:, 2 * width + pair * 128 : 2 * width + pair * 128 + 128]
                    scores = nt(both, key) + mask
                    peak = jnp.max(scores, 1, keepdims=True)
                    weights = jnp.exp(scores - peak)
                    total = jnp.sum(weights, 1, keepdims=True)
                    result = nn(weights.astype(bf16), value) / total
                    logsum = peak + jnp.log(total)
                    head_mix[place_rows, lanes] = jnp.where(
                        lane, result[:tile], result[tile:]
                    ).astype(bf16)
                    lse[place_rows, lanes] = jnp.where(lane, logsum[:tile], logsum[tile:])
                pump_step(at, rows // tile, begin_time, 1.7)
                return carry

            lax.fori_loop(0, rows // tile, step, 0)
            plan_at[0] = max(plan_at[0], sum(1 for item in plan if item[0] <= attend_at[0] + LEAD))

        my_lanes = pl.ds(aligned(col * width), width)

        def send_mixed(side):
            return c_copy(
                head_mix.at[pl.ds(aligned((1 - col) * group + side * rows, 16), rows), :],
                mixed.at[pl.ds(side * rows, rows), my_lanes],
            )

        def keep_mixed(side):
            mixed[side * rows : side * rows + rows, my_lanes] = head_mix[
                pl.ds(aligned(col * group + side * rows, 16), rows), :
            ]

        attend(1 - col, 1)
        copy = send_mixed(1)
        attend(col, 1)
        keep_mixed(1)
        copy.wait()
        settle("normed_two")
        far_copy = y_copy(mixed.at[pl.ds(rows, rows), :], mixed_far)
        if first:
            stage(1, 0)
        attend(1 - col, 0)
        copy = send_mixed(0)
        gather.far_in(layer)
        attend(col, 0)
        keep_mixed(0)
        copy.wait()
        save("lse", 4, lse, lse_out.at[layer])
        save("head_mix", 14, head_mix, head_mix_out.at[layer])
        save("mixed", 5, mixed, mixed_out.at[layer])
        stage_far(layer)
        ready(1)
        settle("branch", "unit_two", "inverse_two")

        def project(start):
            def step(at, carry):
                lanes = pl.ds(aligned(at * half), half)
                value = nn(mixed[start : start + chunk, :], wm[:, lanes])
                value = value + nn(mixed_far[start : start + chunk, :], wf[:, lanes])
                bias_at = aligned(4 * D + at * half)
                value = value + vecs[layer : layer + 1, pl.ds(bias_at, half)]
                scale = vecs[layer : layer + 1, pl.ds(aligned(5 * D + at * half), half)]
                branch[start : start + chunk, lanes] = value
                state[start : start + chunk, lanes] += scale * value
                return carry

            lax.fori_loop(0, 2, step, 0)

        far_copy.wait()
        ready(KINDS)
        copies = []
        for at in range(SPLIT):
            project(at * chunk)
            norm_rows(
                state,
                vector(layer, 6),
                vector(layer, 7),
                unit_two,
                inverse_two,
                normed_two,
                at * chunk,
                chunk,
            )
            copies.append(send_rows(normed_two, at))
            pump((50 if first else 137) + at * 1.5)
        ensure(2 if first else 6)
        stage(2, layer)
        save("branch", 6, branch, branch_out.at[layer])
        save("unit_two", 7, unit_two, unit_two_out.at[layer])
        save("inverse_two", 8, inverse_two, inv_two_out.at[layer])
        ready(2)
        settle("active", "slope", "normed")

        def expand(start, size, begin_time):
            def step(at, carry):
                lanes = pl.ds(aligned(at * half), half)
                bias_at = aligned(8 * D + row * (FF // 2) + at * half)
                value = nn(normed_two[start : start + size, :], wu[:, lanes])
                value = value + vecs[layer : layer + 1, pl.ds(bias_at, half)]
                act, grad = gelu_both(value)
                active[start : start + size, lanes] = act.astype(bf16)
                slope[start : start + size, lanes] = grad.astype(bf16)
                pump_step(at, FF // 2 // half, begin_time, 0.8)
                return carry

            lax.fori_loop(0, FF // 2 // half, step, 0)
            end = begin_time + FF // 2 // half * 0.8 + LEAD
            plan_at[0] = max(plan_at[0], sum(1 for item in plan if item[0] <= end))

        def shrink(start, size, target, target_at):
            def step(at, carry):
                lanes = pl.ds(aligned(at * half), half)
                value = nn(active[start : start + size, :], wd[:, lanes])
                target[pl.ds(target_at, size), lanes] = value.astype(target.dtype)
                return carry

            lax.fori_loop(0, 2, step, 0)

        def shrink_send(at):
            shrink(rows + at * chunk, chunk, tx, at * chunk)
            view = pl.ds(at * chunk, chunk)
            return y_copy(tx.at[view, :], rx.at[view, :])

        back_copies = []
        if first:
            expand(0, rows, 56.0)
            copies[0].wait()
            expand(rows, chunk, 63.0)
            copies[1].wait()
            expand(rows + chunk, chunk, 71.0)
            ensure(3)
            stage(3, 0)
            ready(3)
            back_copies.append(shrink_send(0))
            back_copies.append(shrink_send(1))
        else:
            expand(0, rows, 139.0)
            for at in range(SPLIT):
                copies[at].wait()
                expand(rows + at * chunk, chunk, 146.0 + 8.0 * at)
        if first:
            shrink(0, rows, part, 0)
        save("normed_two", 9, normed_two, normed_two_out.at[layer])
        save("active", 10, active, active_out.at[layer])
        save("slope", 12, slope, slope_out.at[layer])
        if first:
            pump(87)
        else:
            for copy in out_copies:
                copy.wait()
            save("back_out", 15, back_out, back_out_out)
            save("state", 16, state, middle_out)
            break
        settle("unit", "inverse")
        next_copies = []
        for at in range(SPLIT):
            back_copies[at].wait()
            here = slice(at * chunk, at * chunk + chunk)
            output[here, :] = part[here, :] + rx[here, :].astype(f32) + vector(layer, 12)
            state[here, :] = state[here, :] + vector(layer, 13) * output[here, :]
            next_copies.append(norm_one(1, at))
            if at == 0:
                pump(94)
        save("output", 13, output, output_out)
        ensure(4)
        stage(0, 1)
        copies = next_copies
    ensure(GROUPS - 1)
    gather.arrive(GROUPS - 1)
    gather.finish()
    settle(*list(pending))


def padded_rows(tokens):
    return -(-tokens // (2 * TILE)) * TILE


def forward_call(mesh_count, images, cotangent, spot, masters):
    tokens = images.shape[0]
    rows = padded_rows(tokens)
    group = 2 * rows
    half = D // 2
    width = half // 2
    line = mesh_count // 2

    def shape(*dims, kind=f32):
        return jax.ShapeDtypeStruct(dims, kind)

    outs = [
        shape(LAYERS, D, 3 * half, kind=bf16),
        shape(LAYERS, half, D, kind=bf16),
        shape(LAYERS, D, FF // 2, kind=bf16),
        shape(LAYERS, FF // 2, D, kind=bf16),
        shape(LAYERS, half, D, kind=bf16),
        shape(LAYERS, 10 * D + FF),
        shape(LAYERS, rows, D),
        shape(LAYERS, rows, 128),
        shape(LAYERS, group, D, kind=bf16),
        shape(LAYERS, 2 * group, 3 * width, kind=bf16),
        shape(LAYERS, 2 * group, width),
        shape(LAYERS, group, half, kind=bf16),
        shape(LAYERS, rows, D),
        shape(LAYERS, rows, D),
        shape(LAYERS, rows, 128),
        shape(LAYERS, group, D, kind=bf16),
        shape(LAYERS, group, FF // 2, kind=bf16),
        shape(LAYERS, group, FF // 2, kind=bf16),
        shape(rows, D),
        shape(LAYERS, 2 * group, width, kind=bf16),
        shape(group, D, kind=bf16),
        shape(rows, D, kind=bf16),
        shape(rows, D),
    ]
    dma = pltpu.SemaphoreType.DMA
    scratch = [
        pltpu.VMEM((LAYERS, D // (2 * mesh_count), 3 * half), bf16),
        pltpu.VMEM((LAYERS, half // mesh_count, half), bf16),
        pltpu.VMEM((LAYERS, D // (2 * mesh_count), FF // 2), bf16),
        pltpu.VMEM((LAYERS, FF // 2 // mesh_count, half), bf16),
        pltpu.VMEM((rows, D), f32),
        pltpu.VMEM((group, half), bf16),
        pltpu.VMEM((rows, half), bf16),
        pltpu.VMEM(spot.shape, f32),
        pltpu.VMEM((3, line) + spot.shape, f32),
        pltpu.VMEM((line,) + spot.shape, f32),
        pltpu.VMEM((LAYERS, 10 * D + FF), f32),
        pltpu.VMEM((D, 3 * half), bf16),
        pltpu.VMEM((half, D), bf16),
        pltpu.VMEM((D, FF // 2), bf16),
        pltpu.VMEM((FF // 2, D), bf16),
        pltpu.VMEM((half, D), bf16),
        pltpu.VMEM((rows, D), f32),
        pltpu.VMEM((rows, 128), f32),
        pltpu.VMEM((rows, D), f32),
        pltpu.VMEM((rows, 128), f32),
        pltpu.VMEM((group, D), bf16),
        pltpu.VMEM((group, D), bf16),
        pltpu.VMEM((LAYERS, 2 * group, 3 * width), bf16),
        pltpu.VMEM((group, 3 * width), bf16),
        pltpu.VMEM((2 * group, width), bf16),
        pltpu.VMEM((2 * group, width), f32),
        pltpu.VMEM((LAYERS, group, half), bf16),
        pltpu.VMEM((rows, half), bf16),
        pltpu.VMEM((group, D), bf16),
        pltpu.VMEM((rows, D), f32),
        pltpu.VMEM((rows, D), f32),
        pltpu.VMEM((group, FF // 2), bf16),
        pltpu.VMEM((group, FF // 2), bf16),
        pltpu.VMEM((rows, D), bf16),
        pltpu.VMEM((rows, D), bf16),
        pltpu.VMEM((rows, D), f32),
        dma((GROUPS, 4 * line - 1)),
        dma((GROUPS, 4 * line - 1)),
        dma((GROUPS,)),
        dma((LAYERS, 2)),
        dma((LAYERS, 2)),
        dma((line + 2,)),
        dma((line + 2,)),
        dma((16,)),
        dma((16,)),
        dma((16,)),
        dma((16,)),
        dma((KINDS + 1,)),
        dma((17,)),
    ]
    return pl.pallas_call(
        functools.partial(forward_kernel, mesh_count),
        out_shape=outs,
        in_specs=[WHOLE] * 7,
        out_specs=[ANY] * 21 + [WHOLE] + [ANY],
        scratch_shapes=scratch,
        compiler_params=pltpu.CompilerParams(
            collective_id=0, has_side_effects=True, vmem_limit_bytes=60 << 20
        ),
        name="forward",
    )(images, cotangent, spot, *masters)


def fold(values):
    return jnp.sum(values.reshape(-1, 8, values.shape[-1]), 0)


def total(values):
    return jnp.sum(values, 0, keepdims=True)


def flip(picks, values):
    high = values.astype(bf16)
    rest = values - high.astype(f32)
    middle = rest.astype(bf16)
    low = (rest - middle.astype(f32)).astype(bf16)
    return nt(picks, high) + nt(picks, middle) + nt(picks, low)


class Scatter:
    def __init__(self, place, sums, pair_rx, line_rx, outs, refs):
        self.place, self.sums, self.pair_rx, self.line_rx = place, sums, pair_rx, line_rx
        self.outs, self.result = outs, refs["result"]
        self.x_send, self.x_recv = refs["x_send"], refs["x_recv"]
        self.z_send, self.z_recv = refs["z_send"], refs["z_recv"]
        self.x_free, self.z_free, self.out_sem = refs["x_free"], refs["z_free"], refs["out_sem"]
        self.writing = {}

    def size(self, kind):
        return self.sums[kind].shape[0] // self.place.count

    def block(self, kind, dp):
        size = self.size(kind)
        return pl.ds(aligned(dp * size, 16), size)

    def x_copy(self, layer, kind, outer):
        place = self.place
        size = self.size(kind)
        at = layer * KINDS + kind
        return remote(
            self.sums[kind].at[self.block(kind, 2 * outer + 1 - place.pair), :],
            self.pair_rx[kind].at[pl.ds(outer * size, size), :],
            self.x_send.at[at, outer],
            self.x_recv.at[at, outer],
            place.x_peer,
        )

    def z_copy(self, layer, kind, outer):
        place = self.place
        size = self.size(kind)
        at = layer * KINDS + kind
        step = lax.rem(outer - place.outer + place.line, place.line)
        return remote(
            self.pair_rx[kind].at[pl.ds(aligned(outer * size, 16), size), :],
            self.line_rx[kind].at[step - 1],
            self.z_send.at[at, step - 1],
            self.z_recv.at[at, step - 1],
            (2 * outer + place.pair, place.row, place.col),
        )

    def x_start(self, layer, kind):
        if layer < LAYERS - 1:
            pl.semaphore_wait(self.x_free.at[kind], 1)
        for outer in range(self.place.line):
            self.x_copy(layer, kind, outer).start()

    def x_finish(self, layer, kind):
        place = self.place
        size = self.size(kind)
        rows = min(size, 64)
        if layer < LAYERS - 1:
            pl.semaphore_wait(self.z_free.at[kind], place.line - 1)
        for outer in range(place.line):
            self.x_copy(layer, kind, outer).wait()

            def step(at, carry, outer=outer):
                here = pl.ds(aligned(outer * size + at * rows, 16), rows)
                own = pl.ds(aligned((2 * outer + place.pair) * size + at * rows, 16), rows)
                pair_rx = self.pair_rx[kind]
                value = pair_rx[here, :].astype(f32) + self.sums[kind][own, :].astype(f32)
                pair_rx[here, :] = value.astype(bf16)
                return carry

            lax.fori_loop(0, size // rows, step, 0)

            @pl.when(place.outer != outer)
            def _(outer=outer):
                self.z_copy(layer, kind, outer).start()

    def z_finish(self, layer, kind):
        place = self.place
        size = self.size(kind)
        for step_at in range(1, place.line):
            self.z_copy(layer, kind, lax.rem(place.outer + step_at, place.line)).wait()
        if kind in self.writing:
            self.writing.pop(kind).wait()
        rows = min(size, 64)

        def step(at, carry):
            here = pl.ds(aligned(at * rows, 16), rows)
            own = pl.ds(aligned(place.outer * size + at * rows, 16), rows)
            value = self.pair_rx[kind][own, :].astype(f32)
            for step_at in range(place.line - 1):
                value = value + self.line_rx[kind][step_at, here, :].astype(f32)
            if kind == 0:
                third = value.shape[1] // 3
                for part_at in range(3):
                    self.result[kind][part_at, here, :] = value[:, part_at * third : (part_at + 1) * third]
            else:
                self.result[kind][here, :] = value
            return carry

        lax.fori_loop(0, size // rows, step, 0)
        copy = pltpu.make_async_copy(
            self.result[kind], self.outs[kind].at[layer], self.out_sem.at[kind]
        )
        copy.start()
        self.writing[kind] = copy
        if layer == LAYERS - 1:
            pl.semaphore_signal(
                self.x_free.at[kind], inc=1, device_id=place.x_peer, device_id_type=MESH
            )
            for step_at in range(1, place.line):
                pl.semaphore_signal(
                    self.z_free.at[kind],
                    inc=1,
                    device_id=place.z_peer(step_at),
                    device_id_type=MESH,
                )

    def finish(self):
        for copy in self.writing.values():
            copy.wait()


class VectorSums:
    def __init__(self, place, grads, packed, spare, spot, send, recv):
        self.place, self.grads, self.packed = place, grads, packed
        self.spare, self.spot, self.send, self.recv = spare, spot, send, recv
        self.peers = (place.x_peer, place.y_peer, place.c_peer)

    def line_copy(self, step):
        place = self.place
        return remote(
            self.packed.at[lax.rem(place.outer + step, place.line)],
            self.spare.at[2 + step],
            self.send.at[2 + step],
            self.recv.at[2 + step],
            place.z_peer(step),
        )

    def line_start(self):
        size = self.spot.shape[1]
        for outer in range(self.place.line):
            self.packed[outer] = self.grads[:, outer * size : (outer + 1) * size]
        for step in range(1, self.place.line):
            self.line_copy(step).start()

    def line_finish(self):
        value = self.packed[self.place.outer]
        for step in range(1, self.place.line):
            self.line_copy(step).wait()
            value = value + self.spare[2 + step]
        self.spot[...] = value

    def copy(self, at):
        return remote(
            self.spot, self.spare.at[at], self.send.at[at], self.recv.at[at], self.peers[at]
        )

    def start(self, at):
        self.copy(at).start()

    def finish(self, at):
        self.copy(at).wait()
        self.spot[...] = self.spot[...] + self.spare[at]


def backward_kernel(count, *refs):
    (
        grad_in,
        vecs,
        w_a,
        w_b,
        w_c,
        w_d,
        w_far,
        unit_one_in,
        inv_one_in,
        normed_in,
        heads_in,
        lse_in,
        mixed_in,
        branch_in,
        unit_two_in,
        inv_two_in,
        normed_two_in,
        active_in,
        slope_in,
        output_in,
        head_mix_in,
        back_out_in,
        middle_in,
        grad_a,
        grad_b,
        grad_c,
        grad_d,
        grad_out,
        vec_out,
        block_out,
        wq,
        wm,
        wu,
        wd,
        wf,
        far_tx,
        far_rx,
        active,
        slope,
        feed,
        heads,
        lse,
        head_mix,
        mixed,
        aside,
        unit,
        inverse,
        grad,
        back_out,
        back_branch,
        part,
        tx,
        rx,
        rx_out,
        arrived,
        head_back,
        head_tx,
        head_grad,
        key_sum,
        value_sum,
        half_tx,
        sum_a,
        sum_b,
        sum_c,
        sum_d,
        pair_a,
        pair_b,
        pair_c,
        pair_d,
        line_a,
        line_b,
        line_c,
        line_d,
        result_a,
        result_b,
        result_c,
        result_d,
        vec_grads,
        packed,
        spare,
        spot,
        y_send,
        y_recv,
        c_send,
        c_recv,
        x_send,
        x_recv,
        z_send,
        z_recv,
        x_free,
        z_free,
        out_sem,
        v_send,
        v_recv,
        load_sem,
    ) = refs
    tokens = grad_out.shape[0]
    rows = grad_in.shape[0]
    group = 2 * rows
    half = D // 2
    width = half // 2
    pairs = width // 128
    place = Place(count)
    row, col = place.row, place.col
    sums = (sum_a, sum_b, sum_c, sum_d)
    place.greet()
    scatter = Scatter(
        place,
        sums,
        (pair_a, pair_b, pair_c, pair_d),
        (line_a, line_b, line_c, line_d),
        (grad_a, grad_b, grad_c, grad_d),
        {
            "result": (result_a, result_b, result_c, result_d),
            "x_send": x_send,
            "x_recv": x_recv,
            "z_send": z_send,
            "z_recv": z_recv,
            "x_free": x_free,
            "z_free": z_free,
            "out_sem": out_sem,
        },
    )
    triple_back = active

    sources = {
        "wd": (w_d, wd),
        "wu": (w_c, wu),
        "wm": (w_b, wm),
        "wf": (w_far, wf),
        "wq": (w_a, wq),
        "slope": (slope_in, slope),
        "active": (active_in, active),
        "normed_two": (normed_two_in, feed),
        "normed": (normed_in, feed),
        "output": (output_in, aside),
        "branch": (branch_in, aside),
        "unit_two": (unit_two_in, unit),
        "unit_one": (unit_one_in, unit),
        "inv_two": (inv_two_in, inverse),
        "inv_one": (inv_one_in, inverse),
        "heads": (heads_in, heads),
        "lse": (lse_in, lse),
        "head_mix": (head_mix_in, head_mix),
        "mixed": (mixed_in, mixed),
        "back_out": (back_out_in, back_out),
        "middle": (middle_in, part),
    }
    names = list(sources)
    loading = {}

    def load(layer, *wanted):
        for name in wanted:
            source, buffer = sources[name]
            if name not in ("back_out", "output", "middle"):
                source = source.at[layer]
            copy = pltpu.make_async_copy(source, buffer, load_sem.at[names.index(name)])
            copy.start()
            loading[name] = copy

    def loaded(*wanted):
        for name in wanted:
            loading.pop(name).wait()

    y_at = [0]

    def y_copy(source, target):
        at = y_at[0]
        y_at[0] += 1
        copy = remote(source, target, y_send.at[at], y_recv.at[at], place.y_peer)
        copy.start()
        return copy

    c_at = [0]

    def c_copy(source, target):
        at = c_at[0]
        c_at[0] += 1
        return remote(source, target, c_send.at[at], c_recv.at[at], place.c_peer)

    chunk = rows // SPLIT

    def send_rows(buffer, at):
        return y_copy(
            buffer.at[pl.ds(at * chunk, chunk), :],
            buffer.at[pl.ds(rows + at * chunk, chunk), :],
        )

    def send_part(at):
        view = pl.ds(at * chunk, chunk)
        return y_copy(tx.at[view, :], rx.at[view, :])

    load(1, "back_out", "wd", "slope", "wu", "branch", "active", "normed_two", "unit_two", "inv_two")
    load(1, "wf", "wm", "mixed", "heads", "lse", "head_mix", "wq")
    grad[...] = grad_in[...].astype(f32)
    vec_grads[...] = jnp.zeros_like(vec_grads)
    lane = lax.broadcasted_iota(jnp.int32, (1, 128), 1) < HEAD_DIM
    pick_row = lax.broadcasted_iota(jnp.int32, (8, 128), 0)
    pick_lane = lax.broadcasted_iota(jnp.int32, (8, 128), 1)
    halves = (
        ((pick_row == 0) & (pick_lane < HEAD_DIM)) | ((pick_row == 1) & (pick_lane >= HEAD_DIM))
    ).astype(bf16)
    firsts = (pick_lane == pick_row * HEAD_DIM).astype(bf16)
    size = 16

    def vector(layer, at):
        return vecs[layer : layer + 1, at * D : (at + 1) * D]

    def note(layer, at, value):
        vec_grads[layer : layer + 1, at * D : (at + 1) * D] += value

    def by_rows(start, count_rows, body, terms):
        def step(at, carry):
            adds = body(pl.ds(aligned(start + at * size, size), size))
            return tuple(old + fold(new) for old, new in zip(carry, adds, strict=True))

        zeros = tuple(jnp.zeros((8, D), f32) for _ in range(terms))
        sums_ = lax.fori_loop(0, count_rows // size, step, zeros)
        return [total(value) for value in sums_]

    def half_tiles(kind):
        return {0: 3, 1: 1, 2: FF // 2 // half, 3: FF // 2 // half}[kind]

    def weight_grad(kind, owner, at):
        owned = pl.ds(aligned(owner * half), half)
        tile = pl.ds(aligned(at * half), half)
        if kind == 0:
            return tn(feed[:, owned], triple_back[:, tile])
        if kind == 1:
            return tn(mixed[...], back_branch[:, owned])
        if kind == 2:
            return tn(feed[:, owned], slope[:, tile])
        return tn(active[:, tile], back_out[:, owned])

    def spot_of(kind, at):
        tile = pl.ds(aligned(at * half), half)
        return (tile, slice(None)) if kind == 3 else (slice(None), tile)

    half_copies = {}

    def produce_other(layer, kind):
        target = sums[kind]
        buffer = {
            0: half_tx[0].at[:, pl.ds(0, 3 * half)],
            1: half_tx[0].at[:, pl.ds(3 * half, half)],
            2: half_tx[0],
            3: half_tx[1],
        }[kind]

        def step(at, carry):
            buffer[spot_of(kind, at)] = weight_grad(kind, 1 - col, at).astype(bf16)
            return carry

        lax.fori_loop(0, half_tiles(kind), step, 0)
        copy = c_copy(buffer, target)
        copy.start()
        half_copies[kind] = copy

    def produce_own(layer, kind):
        target = sums[kind]
        half_copies.pop(kind).wait()

        def step(at, carry):
            here = spot_of(kind, at)
            value = weight_grad(kind, col, at) + target[here].astype(f32)
            target[here] = value.astype(bf16)
            return carry

        lax.fori_loop(0, half_tiles(kind), step, 0)
        scatter.x_start(layer, kind)

    def out_rows(layer, start, count_rows):
        def body(here):
            value = grad[here, :]
            back = (vector(layer, 13) * value).astype(bf16)
            back_out[here, :] = back
            return (value * aside[here, :], back.astype(f32))

        for at, value in zip((13, 12), by_rows(start, count_rows, body, 2), strict=True):
            note(layer, at, value)

    def last_rows(layer, start, count_rows):
        def body(here):
            value = aside[here, :] + rx_out[here, :].astype(f32) + vector(layer, 12)
            result = part[here, :] + vector(layer, 13) * value
            back_out[here, :] = result.astype(bf16)
            gradient = grad_in[here, :].astype(f32)
            back = (vector(layer, 13) * gradient).astype(bf16)
            return (gradient * value, back.astype(f32))

        for at, value in zip((13, 12), by_rows(start, count_rows, body, 2), strict=True):
            note(layer, at, value)

    def shrink(start, count_rows, target, target_at):
        def step(at, carry):
            lanes = pl.ds(aligned(at * half), half)
            value = nn(active[start : start + count_rows, :], wd[:, lanes])
            target[pl.ds(target_at, count_rows), lanes] = value.astype(target.dtype)
            return carry

        lax.fori_loop(0, 2, step, 0)

    for layer in reversed(range(LAYERS)):
        last = layer == LAYERS - 1
        if last:
            loaded("back_out")
        else:
            load(0, "branch")
            scatter.z_finish(1, 3)
            scatter.z_finish(1, 2)
        loaded("slope", "wd")

        def inner_rows(start, count_rows):
            def step(at, carry):
                lanes = pl.ds(aligned(at * half), half)
                value = nt(back_out[start : start + count_rows, :], wd[lanes, :])
                back = (value * slope[start : start + count_rows, lanes].astype(f32)).astype(bf16)
                slope[start : start + count_rows, lanes] = back
                there = pl.ds(aligned(8 * D + row * (FF // 2) + at * half), half)
                old = vec_grads[layer : layer + 1, there]
                vec_grads[layer : layer + 1, there] = old + total(back.astype(f32))
                return carry

            lax.fori_loop(0, FF // 2 // half, step, 0)

        def two_rows(start, count_rows, target, target_at):
            def step(at, carry):
                lanes = pl.ds(aligned(at * half), half)
                value = nt(slope[start : start + count_rows, :], wu[lanes, :])
                target[pl.ds(target_at, count_rows), lanes] = value.astype(target.dtype)
                return carry

            lax.fori_loop(0, 2, step, 0)

        def back_chunk(at):
            start = rows + at * chunk
            inner_rows(start, chunk)
            two_rows(start, chunk, tx, at * chunk)
            return send_part(at)

        if last:
            loaded("wu")
            back_copies = [back_chunk(at) for at in range(SPLIT)]
            inner_rows(0, rows)
        else:
            inner_rows(0, rows)
            loaded("wu")
            back_copies = []
            for at in range(SPLIT):
                out_copies[at].wait()
                back_copies.append(back_chunk(at))
        two_rows(0, rows, part, 0)
        if not last:
            scatter.x_finish(1, 0)
        loaded("active", "normed_two")
        produce_other(layer, 3)
        produce_other(layer, 2)
        produce_own(layer, 3)
        loaded("unit_two", "inv_two", "branch", "wf")

        def far_rows(at):
            here = slice(at * chunk, at * chunk + chunk)
            far_tx[here, :] = nt(back_branch[here, :], wf[...]).astype(bf16)
            return y_copy(
                far_tx.at[pl.ds(at * chunk, chunk), :], far_rx.at[pl.ds(at * chunk, chunk), :]
            )


        def middle_rows(here):
            back = part[here, :] + rx[here, :].astype(f32)
            norm = unit[here, :]
            scaled = back * vector(layer, 6)
            first = jnp.sum(scaled, 1, keepdims=True) * (1.0 / D)
            second = jnp.sum(scaled * norm, 1, keepdims=True) * (1.0 / D)
            scale = inverse[here, 0:1]
            value = grad[here, :] + scale * (scaled - first - norm * second)
            grad[here, :] = value
            branch_back = (vector(layer, 5) * value).astype(bf16)
            back_branch[here, :] = branch_back
            return (back * norm, back, value * aside[here, :], branch_back.astype(f32))

        copies = []
        for at in range(SPLIT):
            back_copies[at].wait()
            terms = by_rows(at * chunk, chunk, middle_rows, 4)
            copies.append(far_rows(at))
            for spot_at, value in zip((6, 7, 5, 4), terms, strict=True):
                note(layer, spot_at, value)
        branch_copies = [send_rows(back_branch, at) for at in range(SPLIT)]
        load(layer, "unit_one", "inv_one")
        if last:
            load(0, "wf")
        loaded("wm")

        def keep_back(owner, start, count_rows, value):
            @pl.when(owner == col)
            def _():
                head_back[pl.ds(aligned(col * group + start, 16), count_rows), :] = value

            @pl.when(owner != col)
            def _():
                head_tx[start : start + count_rows, :] = value

        core_copies = []

        def send_back(start, count_rows):
            core_copies.append(
                c_copy(
                    head_tx.at[pl.ds(start, count_rows), :],
                    head_back.at[pl.ds(aligned(col * group + start, 16), count_rows), :],
                )
            )
            core_copies[-1].start()

        for owner in range(2):
            lanes = slice(owner * width, owner * width + width)
            keep_back(owner, 0, rows, nt(back_branch[:rows, :], wm[lanes, :]).astype(bf16))
        send_back(0, rows)
        produce_own(layer, 2)
        load(layer, "normed")
        if last:
            shrink(rows, rows, tx, 0)
            shrink(0, rows, aside, 0)
            load(0, "wd")
            load(1, "middle")
        for at in range(SPLIT):
            copies[at].wait()
            here = slice(at * chunk, at * chunk + chunk)
            for owner in range(2):
                lanes = slice(owner * width, owner * width + width)
                keep_back(owner, rows + at * chunk, chunk, far_rx[here, lanes])
            send_back(rows + at * chunk, chunk)
        if last:
            last_copies = [
                y_copy(tx.at[view, :], rx_out.at[view, :])
                for view in (pl.ds(at * chunk, chunk) for at in range(SPLIT))
            ]
        loaded("heads", "lse", "head_mix", "mixed")
        if last:
            load(0, "wm")
        else:
            scatter.z_finish(1, 1)
            scatter.z_finish(1, 0)
        for copy in core_copies:
            copy.wait()

        piece = 2 * group // 2
        head_copies = []
        for pair in range(pairs):
            lanes = slice(pair * 128, pair * 128 + 128)
            key_lanes = slice(width + pair * 128, width + pair * 128 + 128)
            value_lanes = slice(2 * width + pair * 128, 2 * width + pair * 128 + 128)
            key_sum[...] = jnp.zeros_like(key_sum)
            value_sum[...] = jnp.zeros_like(value_sum)

            def step(at, carry, lanes=lanes, key_lanes=key_lanes, value_lanes=value_lanes):
                here = pl.ds(aligned(at * 128), 128)
                query = heads[here, lanes] * jnp.asarray(HEAD_DIM**-0.5, bf16)
                back = head_back[here, lanes]
                zero = jnp.zeros_like(query)
                queries = jnp.concatenate(
                    [jnp.where(lane, query, zero), jnp.where(lane, zero, query)], 0
                )
                backs = jnp.concatenate(
                    [jnp.where(lane, back, zero), jnp.where(lane, zero, back)], 0
                )
                logs = flip(firsts, lse[here, lanes])
                logs = jnp.concatenate([logs[0:1], logs[1:2]], 1)
                inner = flip(halves, back.astype(f32) * head_mix[here, lanes].astype(f32))
                inner = jnp.concatenate([inner[0:1], inner[1:2]], 1)
                query_grad = jnp.zeros((256, 128), f32)
                for block in range(2):
                    keys = slice(block * piece, block * piece + piece)
                    key = heads[keys, key_lanes]
                    scores = nt(key, queries)
                    probs = jnp.exp(jnp.minimum(scores - logs, 0.0))
                    back_probs = nt(heads[keys, value_lanes], backs)
                    back_scores = (probs * (back_probs - inner)).astype(bf16)
                    value_sum[keys, :] += nn(probs.astype(bf16), backs)
                    key_sum[keys, :] += nn(back_scores, queries)
                    query_grad = query_grad + tn(back_scores, key)
                query_grad = query_grad * HEAD_DIM**-0.5
                head_grad[here, lanes] = jnp.where(
                    lane, query_grad[:128], query_grad[128:]
                ).astype(bf16)
                return carry

            lax.fori_loop(0, 2 * group // 128, step, 0)
            if pair == pairs - 1:
                scatter.x_finish(layer, 2)
            for owner in range(2):
                edge = owner * rows
                valid = lax.broadcasted_iota(jnp.int32, (rows, 1), 0) < tokens - edge
                for part_at in range(2):
                    here = slice(owner * group + part_at * rows, owner * group + part_at * rows + rows)
                    head_grad[here, key_lanes] = jnp.where(valid, key_sum[here, :], 0.0).astype(bf16)
                    head_grad[here, value_lanes] = jnp.where(valid, value_sum[here, :], 0.0).astype(bf16)
            if pair < pairs - 1:
                scatter.x_finish(layer, 3)
                for copy in branch_copies:
                    copy.wait()
                produce_other(layer, 1)
                produce_own(layer, 1)
            there = pl.ds(aligned((1 - col) * group, 16), group)
            mine = pl.ds(aligned(col * group, 16), group)
            for part_at, source in enumerate((lanes, key_lanes, value_lanes)):
                target = pl.ds(aligned(part_at * half + col * width + pair * 128), 128)
                copy = c_copy(head_grad.at[there, source], triple_back.at[:, target])
                copy.start()
                head_copies.append(copy)
                triple_back[:, target] = head_grad[mine, source]
                if part_at != 1:
                    bias_at = pl.ds(
                        aligned((3 * D if part_at else 2 * D) + row * half + col * width + pair * 128), 128
                    )
                    vec_grads[layer : layer + 1, bias_at] = total(head_grad[:, source].astype(f32))
        scatter.x_finish(layer, 1)
        for copy in head_copies:
            copy.wait()
        loaded("wq", "normed")
        if last:
            for copy in last_copies:
                copy.wait()
        if not last:
            produce_other(layer, 0)

        def one_rows(start, count_rows, target, target_at):
            def step(at, carry):
                lanes = pl.ds(aligned(at * half), half)
                value = nt(triple_back[start : start + count_rows, : 3 * half], wq[lanes, :])
                target[pl.ds(target_at, count_rows), lanes] = value.astype(target.dtype)
                return carry

            lax.fori_loop(0, 2, step, 0)

        back_copies = []
        for at in range(SPLIT):
            one_rows(rows + at * chunk, chunk, tx, at * chunk)
            back_copies.append(send_part(at))
        if last:
            produce_other(layer, 0)
            produce_own(layer, 0)
            loaded("middle")
            last_rows(layer, 0, rows)
            to_features(
                place, back_out.at[pl.ds(0, rows), :], arrived, block_out, c_send.at[27], c_recv.at[27]
            )
        else:
            produce_own(layer, 0)
            scatter.z_finish(0, 3)
        one_rows(0, rows, part, 0)
        if last:
            load(0, "slope", "wu", "wq", "output", "normed_two", "active")
            load(0, "mixed", "heads", "lse", "head_mix")
        loaded("unit_one", "inv_one")

        def input_rows(here):
            back = part[here, :] + rx[here, :].astype(f32)
            norm = unit[here, :]
            scaled = back * vector(layer, 0)
            first = jnp.sum(scaled, 1, keepdims=True) * (1.0 / D)
            second = jnp.sum(scaled * norm, 1, keepdims=True) * (1.0 / D)
            scale = inverse[here, 0:1]
            grad[here, :] = grad[here, :] + scale * (scaled - first - norm * second)
            return (back * norm, back)

        if last:
            loaded("output")
        out_copies = []
        for at in range(SPLIT):
            back_copies[at].wait()
            terms = by_rows(at * chunk, chunk, input_rows, 2)
            if last:
                out_rows(0, at * chunk, chunk)
                out_copies.append(send_rows(back_out, at))
            for spot_at, value in zip((0, 1), terms, strict=True):
                note(layer, spot_at, value)
        if last:
            load(0, "unit_two", "inv_two")
    vector_sums = VectorSums(place, vec_grads, packed, spare, spot, v_send, v_recv)
    scatter.z_finish(0, 2)
    vector_sums.line_start()
    to_features(place, grad, aside.at[:, pl.ds(0, half)], grad_out, c_send.at[26], c_recv.at[26])
    vector_sums.line_finish()
    scatter.x_finish(0, 0)
    for at in range(3):
        vector_sums.start(at)
        vector_sums.finish(at)
    vec_out[...] = spot[...]
    scatter.z_finish(0, 1)
    scatter.z_finish(0, 0)
    scatter.finish()


def backward_call(mesh_count, tokens, grad, vecs, weights, saved, spot_shape):
    rows = padded_rows(tokens)
    group = 2 * rows
    half = D // 2
    width = half // 2
    line = mesh_count // 2
    wide = FF // 2

    def shape(*dims, kind=f32):
        return jax.ShapeDtypeStruct(dims, kind)

    halves = [(half, 3 * half), (half, half), (half, wide), (wide, half)]
    shards = [(dims[0] // mesh_count, dims[1]) for dims in halves]
    results = [(3, shards[0][0], half)] + shards[1:]
    outs = [shape(LAYERS, *dims) for dims in results]
    outs += [shape(tokens, half), shape(*spot_shape), shape(tokens, half, kind=bf16)]
    dma = pltpu.SemaphoreType.DMA
    scratch = [
        pltpu.VMEM((D, 3 * half), bf16),
        pltpu.VMEM((half, D), bf16),
        pltpu.VMEM((D, wide), bf16),
        pltpu.VMEM((wide, D), bf16),
        pltpu.VMEM((half, D), bf16),
        pltpu.VMEM((rows, half), bf16),
        pltpu.VMEM((rows, half), bf16),
        pltpu.VMEM((group, wide), bf16),
        pltpu.VMEM((group, wide), bf16),
        pltpu.VMEM((group, D), bf16),
        pltpu.VMEM((2 * group, 3 * width), bf16),
        pltpu.VMEM((2 * group, width), f32),
        pltpu.VMEM((2 * group, width), bf16),
        pltpu.VMEM((group, half), bf16),
        pltpu.VMEM((rows, D), f32),
        pltpu.VMEM((rows, D), f32),
        pltpu.VMEM((rows, 128), f32),
        pltpu.VMEM((rows, D), f32),
        pltpu.VMEM((group, D), bf16),
        pltpu.VMEM((group, D), bf16),
        pltpu.VMEM((rows, D), f32),
        pltpu.VMEM((rows, D), bf16),
        pltpu.VMEM((rows, D), bf16),
        pltpu.VMEM((rows, D), bf16),
        pltpu.VMEM((rows, half), bf16),
        pltpu.VMEM((2 * group, width), bf16),
        pltpu.VMEM((group, width), bf16),
        pltpu.VMEM((2 * group, 3 * width), bf16),
        pltpu.VMEM((2 * group, 128), f32),
        pltpu.VMEM((2 * group, 128), f32),
        [pltpu.VMEM(dims, bf16) for dims in halves[2:]],
    ]
    scratch += [pltpu.VMEM(dims, bf16) for dims in halves]
    scratch += [pltpu.VMEM((dims[0] // 2, dims[1]), bf16) for dims in halves]
    scratch += [pltpu.VMEM((line - 1,) + dims, bf16) for dims in shards]
    scratch += [pltpu.VMEM(dims, f32) for dims in results]
    scratch += [
        pltpu.VMEM((LAYERS, 10 * D + FF), f32),
        pltpu.VMEM((line,) + spot_shape, f32),
        pltpu.VMEM((line + 2,) + spot_shape, f32),
        pltpu.VMEM(spot_shape, f32),
        dma((24,)),
        dma((24,)),
        dma((LAYERS * 13 + 2,)),
        dma((LAYERS * 13 + 2,)),
        dma((GROUPS, line)),
        dma((GROUPS, line)),
        dma((GROUPS, line - 1)),
        dma((GROUPS, line - 1)),
        pltpu.SemaphoreType.REGULAR((KINDS,)),
        pltpu.SemaphoreType.REGULAR((KINDS,)),
        dma((KINDS,)),
        dma((line + 2,)),
        dma((line + 2,)),
        dma((21,)),
    ]
    return pl.pallas_call(
        functools.partial(backward_kernel, mesh_count),
        out_shape=outs,
        in_specs=[WHOLE] * 2 + [ANY] * 21,
        out_specs=[ANY] * 4 + [WHOLE] * 3,
        scratch_shapes=scratch,
        compiler_params=pltpu.CompilerParams(
            collective_id=1, has_side_effects=True, vmem_limit_bytes=63 << 20
        ),
        name="backward",
    )(grad, vecs, *weights, *saved)


def local(
    images,
    cotangent,
    triplet_master,
    triplet_first,
    triplet_second,
    project_master,
    project_first,
    project_second,
    expand_master,
    expand_first,
    expand_second,
    shrink_master,
    shrink_first,
    shrink_second,
    vectors_master,
    vectors_first,
    vectors_second,
):
    count = lax.axis_size("dp")
    row_at = lax.axis_index("row")
    col_at = lax.axis_index("col")
    masters = (triplet_master.transpose(0, 2, 1, 3), project_master, expand_master, shrink_master)
    piece = vectors_master.shape[1]
    line_at = (lax.axis_index("dp") % 2 * 2 + row_at) * 2 + col_at
    spot = jnp.where(
        jnp.arange(8 * piece) // piece == line_at, jnp.tile(vectors_master, (1, 8)), 0.0
    )
    (w_a, w_b, w_c, w_d, w_far, vectors, *saved, grad_rows, middle) = forward_call(
        count, images, cotangent, spot, masters
    )
    *grads, grad_out, vector_sums, block_out = backward_call(
        count,
        images.shape[0],
        grad_rows,
        vectors,
        (w_a, w_b, w_c, w_d, w_far),
        (*saved, middle),
        spot.shape,
    )
    vector_reduced = lax.dynamic_slice_in_dim(vector_sums, line_at * piece, piece, 1)

    outs = []
    states = (
        (triplet_master, triplet_first, triplet_second),
        (project_master, project_first, project_second),
        (expand_master, expand_first, expand_second),
        (shrink_master, shrink_first, shrink_second),
    )
    grads[0] = grads[0].transpose(0, 2, 1, 3)
    for kind, (master, first, second) in enumerate(states):
        outs += adam_step(master, first, second, grads[kind], learn_rate, decay_rate)
    outs += adam_step(
        vectors_master, vectors_first, vectors_second, vector_reduced, vector_rate, 0.0
    )
    return (block_out, grad_out, *outs)


def solution(mesh):
    tokens = P(("dp", "row"), "col")
    triplet = P(None, ("col", "dp"), None, "row")
    narrow = P(None, ("row", "dp"), "col")
    wide = P(None, ("col", "dp"), "row")
    vector = P(None, ("dp", "row", "col"))
    states = (triplet,) * 3 + (narrow,) * 3 + (wide,) * 3 + (narrow,) * 3 + (vector,) * 3
    return jax.shard_map(
        local,
        mesh=mesh,
        in_specs=(tokens, tokens) + states,
        out_specs=(tokens, tokens) + states,
        check_vma=False,
    )
```
